256 devices in a mesh: tgt: 8 (over z_lo, core), sup: 32 (over z_hi, x, y).
Axes of the slice: x: 4, y: 4, z: 8 (z_hi: 2, z_lo: 4; z = z_hi * 4 + z_lo), core: 2. Of those that a mesh axis runs over, the one named last changes fastest.
Arguments:
- image_pool: bfloat16 [16384, 3072], P(('tgt', 'sup')), may hold values from -1 to 2
- target_index: int32 [256], replicated, may hold values from 0 to 16383, as said below
- labels: int32 [256], P('tgt'), may hold values from 0 to 1023
- support: float32 [128, 3, 1024], P('sup'), may hold values from -1 to 2
- ridge_coef: float32 [128, 1024], P('sup'), may hold values from -1 to 1
Outputs:
- residual: float32 [256, 1024], P('tgt', 'sup')
- support_grad: float32 [128, 3, 1024], P('sup')
The draws below stay inside these ranges and needn't reach their ends.
Inputs may be any that keep to these rules, and one draw needn't show every extreme that they name: `target_index`: any row of the pool; the first of each group's 32 targets lies in the pool rows of the devices half the tgt axis away.
All inputs are finite; a program needn't handle non-finite values.
Results may differ from the reference program's by a relative error of at most 0.0003.
Values may be sent and summed in bfloat16 or wider, within the bound.
No kernel may reach another device: no remote copies, remote signals or barrier semaphores. Data moves between devices by JAX's collectives and lax.ppermute only.
A program may use at most 64 MiB of HBM per device.

```python
import math
import jax
import jax.numpy as jnp
from jax import lax

SIDE = 32
CHAN = 3
CLASSES = 1024
LAYERS = 4
TGT_DEV = 32
PIX = 1024
TARGETS = 256
SUPPORTS = 128
POOL = 16384
N_TGT = 8


def draw_target_index(key, part):
    groups = TARGETS // TGT_DEV
    span = POOL // groups
    position = jnp.arange(TARGETS, dtype=jnp.int32)
    group = position // TGT_DEV
    anywhere = jax.random.randint(jax.random.fold_in(key, 17), (TARGETS,), 0, POOL, dtype=jnp.int32)
    offset = jax.random.randint(jax.random.fold_in(key, 29), (TARGETS,), 0, span, dtype=jnp.int32)
    far_group = (group + groups // 2) % groups
    far_row = far_group * span + offset
    rows = jnp.where(position % TGT_DEV == 0, far_row, anywhere)
    rows = jnp.where(position == 1, 0, rows)
    rows = jnp.where(position == TARGETS - 1, POOL - 1, rows)
    return rows.astype(jnp.int32)


def plant(values, stream_key, low, high):
    longest = values.shape.index(max(values.shape))
    spots = []
    for shift in (0, 1):
        where = [jax.random.randint(jax.random.fold_in(stream_key, axis), (), 0, length) for axis, length in enumerate(values.shape)]
        where[longest] = (where[longest] + shift) % values.shape[longest]
        spots.append(tuple(where))
    return values.at[spots[0]].set(low).at[spots[1]].set(high)


def block_scale(key, dims, pieces, smallest, top_value):
    def one(axis_at, parts):
        steps = jax.random.uniform(jax.random.fold_in(jax.random.fold_in(key, 6), axis_at), (parts,), jnp.float32, smallest / len(pieces), top_value / len(pieces))
        return jnp.repeat(jnp.exp(steps), dims[axis_at] // parts).reshape((-1,) + (1,) * (len(dims) - axis_at - 1))

    loudness = one(*pieces[0])
    for cut in pieces[1:]:
        loudness = loudness * one(*cut)
    return loudness


def bell_draw(key, shape, width, reach, cuts=(), held_as=jnp.bfloat16):
    array = jax.random.normal(key, shape, jnp.float32) * width
    if len(cuts) > 0:
        array = block_scale(key, shape, cuts, -0.22, 0.18) * array
    return jnp.clip(array, min=-reach, max=reach).astype(held_as)


def setup_inputs(seed: int = 0) -> dict:
    arg_keys = jax.random.split(jax.random.key(seed), 6)
    image_pool = jnp.clip(-1.0 + 3.0 * jax.random.uniform(arg_keys[0], (POOL, CHAN * PIX), jnp.float32) ** block_scale(arg_keys[0], (POOL, CHAN * PIX), ((0, 256),), -0.2, 0.2), -1.0, 2.0).astype(jnp.bfloat16)
    target_index = draw_target_index(jax.random.fold_in(arg_keys[5], 71), 0)
    labels = plant(jax.random.randint(arg_keys[2], (TARGETS,), 0, CLASSES), jax.random.fold_in(arg_keys[2], 1), 0, CLASSES - 1).astype(jnp.int32)
    support = jnp.clip(-1.0 + 3.0 * jax.random.uniform(arg_keys[3], (SUPPORTS, CHAN, PIX), jnp.float32) ** block_scale(arg_keys[3], (SUPPORTS, CHAN, PIX), ((0, 32),), -0.2, 0.2), -1.0, 2.0)
    ridge_coef = bell_draw(arg_keys[4], (SUPPORTS, CLASSES), (SUPPORTS // 4) ** -0.5, 1.0, ((0, 32),), jnp.float32)
    return {"image_pool": image_pool, "target_index": target_index, "labels": labels, "support": support, "ridge_coef": ridge_coef}


WEIGHT_VAR = 2.0
BIAS_VAR = 0.1

def box_sum(values_map):
    column = jnp.arange(SIDE * SIDE) % SIDE
    zero_col = jnp.zeros(values_map.shape[:-1] + (1,), values_map.dtype)
    from_left = jnp.concatenate([zero_col, values_map[..., :-1]], -1)
    from_right = jnp.concatenate([values_map[..., 1:], zero_col], -1)
    row_sum = values_map + jnp.where(column > 0, from_left, 0.0) + jnp.where(column < SIDE - 1, from_right, 0.0)
    zero_row = jnp.zeros(values_map.shape[:-1] + (SIDE,), values_map.dtype)
    from_above = jnp.concatenate([zero_row, row_sum[..., :-SIDE]], -1)
    from_below = jnp.concatenate([row_sum[..., SIDE:], zero_row], -1)
    return (row_sum + from_above + from_below) / 9.0

def self_maps(pixels):
    current = lax.optimization_barrier(jnp.sum(pixels * pixels, axis=1)) / 3.0
    variances = []
    for depth in range(LAYERS):
        variance = WEIGHT_VAR * box_sum(current) + BIAS_VAR
        variances.append(variance)
        current = 2.0 / math.pi * jnp.arcsin(2.0 * variance / (1.0 + 2.0 * variance))
    return variances

def cross_layer(current, target_var, support_var):
    covariance = WEIGHT_VAR * box_sum(current) + BIAS_VAR
    denominator = jnp.sqrt((1.0 + 2.0 * target_var)[:, None, :] * (1.0 + 2.0 * support_var)[None, :, :])
    return 2.0 / math.pi * jnp.arcsin(2.0 * covariance / denominator)

def kernel_rows(targets, support):
    target_vars = self_maps(targets)
    support_vars = self_maps(support)
    current = jnp.einsum('icp,jcp->ijp', targets, support, precision=lax.Precision.HIGHEST) / 3.0
    for depth in range(LAYERS):
        current = cross_layer(current, target_vars[depth], support_vars[depth])
    return lax.optimization_barrier(jnp.mean(current, axis=-1))

def reference(image_pool, target_index, labels, support, ridge_coef):
    images = image_pool[target_index].astype(jnp.float32)
    blocks = images.reshape(N_TGT, TGT_DEV, CHAN, SIDE * SIDE)
    label_blocks = labels.reshape(N_TGT, TGT_DEV)
    classes = jnp.arange(CLASSES)
    loss_scale = float(SIDE * SIDE) / TGT_DEV

    def one_block(running, inputs):
        target_block, block_labels = inputs
        kernel_block, pullback = jax.vjp(lambda points: kernel_rows(target_block, points), support)
        predicted = jnp.dot(kernel_block, ridge_coef, precision=lax.Precision.HIGHEST, preferred_element_type=jnp.float32)
        residual = predicted - (block_labels[:, None] == classes[None, :]).astype(jnp.float32)
        kernel_grad = loss_scale * jnp.dot(residual, ridge_coef.T, precision=lax.Precision.HIGHEST, preferred_element_type=jnp.float32)
        return (running + pullback(kernel_grad)[0], residual)
    support_grad, residual = lax.scan(one_block, jnp.zeros_like(support), (blocks, label_blocks))
    return (residual.reshape(TARGETS, CLASSES), support_grad)
```

```python
import functools
import math

import jax
import jax.numpy as jnp
from jax import lax
from jax.experimental import pallas as pl
from jax.experimental.pallas import tpu as pltpu
from jax.sharding import Mesh, PartitionSpec as P

SIDE = 32
CHAN = 3
LAYERS = 4
PIX = SIDE * SIDE
PLANES = 4
SUB = 8
LANES = 128
STEP_COLS = 4

WEIGHT_VAR = 2.0
BIAS_VAR = 0.1
BOX_SCALE = WEIGHT_VAR / 9.0

F32 = jnp.float32
BF16 = jnp.bfloat16
VMEM = pl.BlockSpec(memory_space=pltpu.VMEM)
SMEM = pl.BlockSpec(memory_space=pltpu.SMEM)

ASIN_Q = [
    c * 2.0 / math.pi
    for c in (
        1.5707963050,
        -0.2145988016,
        0.0889789874,
        -0.0501743046,
        0.0308918810,
        -0.0170881256,
        0.0066700901,
        -0.0012624911,
    )
]


def call(body, outs, n_in, scratch=(), smem=(), flops=0, name=None, vmem=32):
    specs = [SMEM if k in smem else VMEM for k in range(n_in)]
    many = isinstance(outs, (list, tuple))
    return pl.pallas_call(
        body,
        out_shape=outs,
        in_specs=specs,
        out_specs=[VMEM] * len(outs) if many else VMEM,
        scratch_shapes=list(scratch),
        compiler_params=pltpu.CompilerParams(vmem_limit_bytes=vmem * 2**20),
        cost_estimate=pl.CostEstimate(flops=flops, bytes_accessed=1 << 20, transcendentals=0),
        name=name,
    )


def three_parts(x):
    high = x.astype(BF16)
    rest = x - high.astype(F32)
    mid = rest.astype(BF16)
    low = (rest - mid.astype(F32)).astype(BF16)
    return high, mid, low


def dot_f32(a, b, dims):
    return lax.dot_general(a, b, (dims, ((), ())), preferred_element_type=F32, precision=lax.Precision.HIGHEST)


def dot_bf16(a, b, dims):
    return lax.dot_general(a, b, (dims, ((), ())), preferred_element_type=F32)


def pack_body(pool_ref, ridge_ref, out_ref, parts_ref):
    rows = pool_ref.shape[0]
    n_sup = ridge_ref.shape[0]
    parts_ref[...] = jnp.zeros_like(parts_ref)
    for k, part in enumerate(three_parts(ridge_ref[...])):
        parts_ref[k * n_sup : (k + 1) * n_sup, :] = part.astype(F32)
    for tile in range(PIX // LANES):
        at = tile * LANES
        pieces = [pool_ref[:, c * PIX + at : c * PIX + at + LANES] for c in range(CHAN)]
        pieces.append(parts_ref[:, at : at + LANES].astype(BF16))
        for r in range(LANES // SIDE):
            cut = [p[:, r * SIDE : (r + 1) * SIDE] for p in pieces]
            out_ref[tile * (LANES // SIDE) + r, :, :] = jnp.concatenate(cut, axis=1)


def select_body(base_ref, index_ref, rows_ref, out_ref):
    n_src, rows, _ = rows_ref.shape
    total = n_src * rows
    data = rows_ref[...].reshape(total, LANES)
    wanted = index_ref[...] - base_ref[0]
    ids = lax.broadcasted_iota(jnp.int32, (wanted.shape[0], total), 1)
    pick = jnp.where(ids == wanted, 1.0, 0.0).astype(BF16)
    got = dot_bf16(pick, data, ((1,), (0,)))
    out_ref[...] = got.astype(BF16).reshape(out_ref.shape)


def merge_body(parts_ref, out_ref):
    total = parts_ref[0].astype(F32)
    for k in range(1, parts_ref.shape[0]):
        total = total + parts_ref[k].astype(F32)
    total = total.astype(BF16)
    for k in range(out_ref.shape[0]):
        out_ref[k] = total


def steps(fn):
    def one(b, carry):
        for plane in range(PLANES):
            fn(plane, b * STEP_COLS)
        return carry

    lax.fori_loop(0, SIDE // STEP_COLS, one, 0)


def box(ref, plane, col):
    wide = pl.ds(col, STEP_COLS + 2)
    tall = ref[plane, wide] + ref[plane + 1, wide] + ref[plane + 2, wide]
    return tall[0:STEP_COLS] + tall[1 : STEP_COLS + 1] + tall[2 : STEP_COLS + 2]


def put(ref, plane, col, x):
    at = pl.ds(col + 1, STEP_COLS)
    ref[plane + 1, at] = x
    if plane == 0 or plane == PLANES - 1:
        sub = lax.broadcasted_iota(jnp.int32, x.shape, 1)
        if plane == 0:
            ref[PLANES + 1, at] = jnp.where(sub < SUB - 1, pltpu.roll(x, SUB - 1, 1), 0.0)
        else:
            ref[0, at] = jnp.where(sub > 0, pltpu.roll(x, 1, 1), 0.0)


def q_poly(a):
    acc = ASIN_Q[-1] * a + ASIN_Q[-2]
    for c in ASIN_Q[-3::-1]:
        acc = acc * a + c
    return acc


def act_of(x):
    a = jnp.abs(x)
    left = 1.0 - a
    inv = lax.rsqrt(left)
    value = 1.0 - left * inv * q_poly(a)
    return jnp.where(x < 0.0, -value, value), a, inv


def self_step(ref, plane, col):
    var = BOX_SCALE * box(ref, plane, col) + BIAS_VAR
    w = 1.0 + 2.0 * var
    inv = lax.rsqrt(w)
    return var, w, inv


def self_act(var, inv):
    x = 2.0 * var * inv * inv
    left = 1.0 - x
    return 1.0 - left * lax.rsqrt(left) * q_poly(x)


def spread(pix_ref, ones, nat_ref):
    def one(d, carry):
        nat_ref[pl.ds(d * LANES, LANES), :] = dot_bf16(pix_ref[d], ones, ((0,), (0,)))
        return carry

    lax.fori_loop(0, SIDE, one, 0, unroll=4)


def target_at(nat_ref, c, plane, col):
    cols = []
    for k in range(STEP_COLS):
        start = plane * LANES + c * SIDE + col + k
        cols.append(nat_ref[pl.ds(start, SUB, stride=PLANES * LANES), :])
    return jnp.stack(cols, axis=0)


def copies_matrix(n_tgt):
    row = lax.broadcasted_iota(jnp.int32, (n_tgt, LANES), 0)
    lane = lax.broadcasted_iota(jnp.int32, (n_tgt, LANES), 1)
    return jnp.where(lane % n_tgt == row, 1.0, 0.0).astype(BF16)


def first_maps(pix_ref, s_ref, nat_ref, self_ref, pair_ref):
    n_tgt = pix_ref.shape[1]
    spread(pix_ref, copies_matrix(n_tgt), nat_ref)

    def one(plane, col):
        own = jnp.zeros((STEP_COLS, SUB, LANES), F32)
        pair = own
        for c in range(CHAN):
            t = target_at(nat_ref, c, plane, col)
            own = own + t * t
            pair = pair + t * s_ref[c, plane, pl.ds(col, STEP_COLS)]
        put(self_ref, plane, col, own * (1.0 / CHAN))
        put(pair_ref, plane, col, pair * (1.0 / CHAN))

    steps(one)


def side_body(
    sup_ref, ridge_ref, labels_ref, rows_ref, s_ref, inv_ref, dself_ref, mine_ref, gram_ref, picked_ref, nat_ref, buf_ref, parts_ref
):
    n_sup = sup_ref.shape[0]
    n_tgt = labels_ref.shape[0]
    n_src = rows_ref.shape[0]
    for j in range(n_sup):
        total = jnp.zeros((n_src, LANES), F32)
        for k in range(3):
            total = total + rows_ref[:, k * n_sup + j, :].astype(F32)
        mine_ref[j * n_src : (j + 1) * n_src, :] = total
    lane = lax.broadcasted_iota(jnp.int32, mine_ref.shape, 1)
    mine = jnp.where(lane >= CHAN * SIDE, mine_ref[...], 0.0)
    mine_ref[...] = mine
    gram_ref[...] = dot_f32(mine, mine, ((1,), (1,)))
    hot = labels_ref[...] == lax.broadcasted_iota(jnp.int32, (n_tgt, ridge_ref.shape[1]), 1)
    hot = jnp.where(hot, 1.0, 0.0)
    hot = jnp.concatenate([hot] * n_sup, axis=0)
    picked_ref[...] = jnp.zeros_like(picked_ref)
    picked_ref[0:n_sup, :] = dot_f32(ridge_ref[...], hot, ((1,), (1,)))
    rows = parts_ref.shape[0]
    row = lax.broadcasted_iota(jnp.int32, (rows, LANES), 0)
    lane = lax.broadcasted_iota(jnp.int32, (rows, LANES), 1)
    ones = jnp.where((row < 3 * n_sup) & (row % n_sup == lane // n_tgt), 1.0, 0.0).astype(BF16)
    buf_ref[...] = jnp.zeros_like(buf_ref)
    for c in range(CHAN):
        parts_ref[...] = jnp.zeros_like(parts_ref)
        for k, part in enumerate(three_parts(sup_ref[:, c, :])):
            parts_ref[k * n_sup : (k + 1) * n_sup, :] = part.astype(F32)
        nat_ref[c * PIX : (c + 1) * PIX, :] = dot_bf16(parts_ref[...].astype(BF16), ones, ((0,), (0,)))

    def start(plane, col):
        own = jnp.zeros((STEP_COLS, SUB, LANES), F32)
        for c in range(CHAN):
            cols = []
            for k in range(STEP_COLS):
                at = c * PIX + plane * SIDE + col + k
                cols.append(nat_ref[pl.ds(at, SUB, stride=PLANES * SIDE), :])
            s = jnp.stack(cols, axis=0)
            s_ref[c, plane, pl.ds(col, STEP_COLS)] = s
            own = own + s * s
        put(buf_ref.at[0], plane, col, own * (1.0 / CHAN))

    steps(start)

    def layer(depth, carry):
        now, later = buf_ref.at[depth % 2], buf_ref.at[(depth + 1) % 2]

        def one(plane, col):
            at = pl.ds(col, STEP_COLS)
            var, w, inv = self_step(now, plane, col)
            inv_ref[depth, plane, at] = inv
            dself_ref[depth, plane, at] = (4.0 / math.pi) * inv * inv * lax.rsqrt(2.0 * w - 1.0)
            put(later, plane, col, self_act(var, inv))

        steps(one)
        return carry

    lax.fori_loop(0, LAYERS, layer, 0)


def forward_body(pix_ref, s_ref, inv_ref, gram_ref, out_ref, nat_ref, self_ref, pair_ref, acc_ref):
    self_ref[...] = jnp.zeros_like(self_ref)
    pair_ref[...] = jnp.zeros_like(pair_ref)
    first_maps(pix_ref, s_ref, nat_ref, self_ref.at[0], pair_ref.at[0])

    def layer(depth, carry):
        now, later = depth % 2, (depth + 1) % 2

        def one(plane, col):
            var, _, inv = self_step(self_ref.at[now], plane, col)
            put(self_ref.at[later], plane, col, self_act(var, inv))
            twice = (2.0 * BOX_SCALE) * box(pair_ref.at[now], plane, col) + 2.0 * BIAS_VAR
            x = twice * (inv * inv_ref[depth, plane, pl.ds(col, STEP_COLS)])
            put(pair_ref.at[later], plane, col, act_of(x)[0])

        steps(one)
        return carry

    lax.fori_loop(0, LAYERS - 1, layer, 0)
    last = LAYERS - 1
    acc_ref[...] = jnp.zeros_like(acc_ref)

    def one(plane, col):
        _, _, inv = self_step(self_ref.at[last % 2], plane, col)
        twice = (2.0 * BOX_SCALE) * box(pair_ref.at[last % 2], plane, col) + 2.0 * BIAS_VAR
        x = twice * (inv * inv_ref[last, plane, pl.ds(col, STEP_COLS)])
        acc_ref[...] += jnp.sum(act_of(x)[0], axis=0)

    steps(one)
    value = jnp.sum(acc_ref[...], axis=0, keepdims=True) * (1.0 / PIX)
    n_dst = out_ref.shape[0]
    n_sup = gram_ref.shape[0] // n_dst
    for j in range(n_sup):
        out_ref[:, j, :] = gram_ref[j * n_dst : (j + 1) * n_dst, :]
    for k in range(n_sup, out_ref.shape[1]):
        out_ref[:, k, :] = jnp.broadcast_to(value, (n_dst, LANES))


def backward_body(
    pix_ref, s_ref, inv_ref, dself_ref, high_ref, low_ref, nat_ref, self_ref, pair_ref, dcov_ref, dvar_ref, out_ref
):
    self_ref[...] = jnp.zeros_like(self_ref)
    pair_ref[...] = jnp.zeros_like(pair_ref)
    first_maps(pix_ref, s_ref, nat_ref, self_ref.at[0], pair_ref.at[0])

    def layer(depth, carry):
        now, later = depth % 2, (depth + 1) % 2

        def one(plane, col):
            at = pl.ds(col, STEP_COLS)
            var, _, inv = self_step(self_ref.at[now], plane, col)
            put(self_ref.at[later], plane, col, self_act(var, inv))
            twice = (2.0 * BOX_SCALE) * box(pair_ref.at[now], plane, col) + 2.0 * BIAS_VAR
            s_inv = inv_ref[depth, plane, at]
            both = inv * s_inv
            x = twice * both
            value, a, left = act_of(x)
            put(pair_ref.at[later], plane, col, value)
            slope = (2.0 / math.pi) * left * lax.rsqrt(1.0 + a)
            dcov_ref[depth, plane, at] = 2.0 * both * slope
            dvar_ref[depth, plane, at] = -(slope * x) * (s_inv * s_inv)

        steps(one)
        return carry

    lax.fori_loop(0, LAYERS, layer, 0)
    last = LAYERS - 1

    def seed(plane, col):
        at = pl.ds(col, STEP_COLS)
        put(pair_ref.at[last % 2], plane, col, dcov_ref[last, plane, at] * (1.0 / PIX))
        put(self_ref.at[last % 2], plane, col, dvar_ref[last, plane, at] * (1.0 / PIX))

    steps(seed)

    def back(k, carry):
        depth = last - 1 - k
        now, later = (depth + 1) % 2, depth % 2

        def one(plane, col):
            at = pl.ds(col, STEP_COLS)
            g_pair = BOX_SCALE * box(pair_ref.at[now], plane, col)
            g_self = BOX_SCALE * box(self_ref.at[now], plane, col)
            put(pair_ref.at[later], plane, col, g_pair * dcov_ref[depth, plane, at])
            g_var = g_self * dself_ref[depth, plane, at] + g_pair * dvar_ref[depth, plane, at]
            put(self_ref.at[later], plane, col, g_var)

        steps(one)
        return carry

    lax.fori_loop(0, LAYERS - 1, back, 0)

    def finish(plane, col):
        g_pair = (BOX_SCALE / CHAN) * box(pair_ref.at[0], plane, col)
        g_self = BOX_SCALE * box(self_ref.at[0], plane, col)
        for c in range(CHAN + 1):
            g = g_pair * target_at(nat_ref, c, plane, col) if c < CHAN else g_self
            for k in range(STEP_COLS):
                at = c * PIX + plane * SIDE + col + k
                out_ref[pl.ds(at, SUB, stride=PLANES * SIDE), :] = g[k]

    steps(finish)

    def split(k, carry):
        at = pl.ds(pl.multiple_of(k * 64, 64), 64)
        g = out_ref[at, :]
        high = g.astype(BF16)
        high_ref[at, :] = high
        low_ref[at, :] = (g - high.astype(F32)).astype(BF16)
        return carry

    lax.fori_loop(0, out_ref.shape[0] // 64, split, 0)


def weigh_body(scale, n_tgt, got_ref, high_ref, low_ref, picked_ref, sup_ref, out_ref):
    n_src = got_ref.shape[0]
    n_sup = sup_ref.shape[0]
    rows = got_ref.shape[1]
    gram = jnp.sum(got_ref[...], axis=0)
    values = got_ref[:, n_sup, :]
    lane = lax.broadcasted_iota(jnp.int32, (n_src, LANES), 1)
    big = jnp.concatenate([jnp.where(lane // n_tgt == j, values, 0.0) for j in range(n_sup)], axis=0)
    part = dot_f32(gram, big, ((1,), (0,)))
    part = part + pltpu.roll(part, 64, 1)
    part = part + pltpu.roll(part, 32, 1)
    row = lax.broadcasted_iota(jnp.int32, (rows, LANES), 0)
    lane = lax.broadcasted_iota(jnp.int32, (rows, LANES), 1)
    weight = jnp.where(lane // n_tgt == row, scale * (part - picked_ref[...]), 0.0)
    w_high = weight.astype(BF16)
    w_low = (weight - w_high.astype(F32)).astype(BF16)
    zero = jnp.zeros_like(w_high)
    first = jnp.concatenate([w_high, w_low], axis=0)
    second = jnp.concatenate([w_high, zero], axis=0)
    sums = []
    for c in range(CHAN + 1):
        at = slice(c * PIX, (c + 1) * PIX)
        one = dot_bf16(first, high_ref[at, :], ((1,), (1,)))
        two = dot_bf16(second, low_ref[at, :], ((1,), (1,)))
        sums.append((one[:rows] + one[rows:] + two[:rows])[:n_sup])
    per = PIX // LANES
    for c in range(CHAN):
        grad = sums[c] + (2.0 / CHAN) * sup_ref[:, c, :] * sums[CHAN]
        for k in range(per):
            out_ref[pl.ds(c * per + k, n_sup, stride=CHAN * per), :] = grad[:, k * LANES : (k + 1) * LANES]


def residual_body(n_sup, start_ref, got_ref, mine_ref, labels_ref, out_ref):
    n_src = got_ref.shape[0]
    n_tgt, classes = out_ref.shape
    values = got_ref[:, n_sup, :]
    total = jnp.zeros((n_tgt, LANES), F32)
    for j in range(n_sup):
        one = dot_f32(values, mine_ref[j * n_src : (j + 1) * n_src, :], ((0,), (0,)))
        total = total + one[j * n_tgt : (j + 1) * n_tgt, :]
    predicted = total[:, CHAN * SIDE :]
    ids = start_ref[0] + lax.broadcasted_iota(jnp.int32, (n_tgt, classes), 1)
    out_ref[...] = predicted - jnp.where(labels_ref[...] == ids, 1.0, 0.0)


def pair_sum_body(a_ref, b_ref, out_ref):
    total = a_ref[...] + b_ref[...]
    for k in range(out_ref.shape[0]):
        out_ref[k] = total


def last_sum_body(parts_ref, out_ref):
    total = parts_ref[0]
    for k in range(1, parts_ref.shape[0]):
        total = total + parts_ref[k]
    n_sup = out_ref.shape[0]
    per = PIX // LANES
    for j in range(n_sup):
        for c in range(CHAN):
            for k in range(per):
                row = (j * CHAN + c) * per + k
                out_ref[j, c : c + 1, k * LANES : (k + 1) * LANES] = total[row : row + 1, :]


def maps(*lead):
    return pltpu.VMEM((*lead, PLANES + 2, SIDE + 2, SUB, LANES), F32)


def local(image_pool, target_index, labels, support, ridge_coef):
    n_chip, n_core, n_sup_dev = lax.axis_size("chip"), lax.axis_size("core"), lax.axis_size("sup")
    n_grp = n_chip * n_core
    pool_rows = image_pool.shape[0]
    n_sup = support.shape[0]
    n_tgt = labels.shape[0]
    classes = ridge_coef.shape[1] // n_sup_dev
    group = lax.axis_index("chip") * n_core + lax.axis_index("core")
    base = (group * (n_sup_dev * pool_rows))[None].astype(jnp.int32)
    start = (lax.axis_index("sup") * classes)[None].astype(jnp.int32)
    label_col = labels[:, None]
    index_col = target_index[:, None]

    packed = call(
        pack_body,
        jax.ShapeDtypeStruct((n_sup_dev, pool_rows, LANES), BF16),
        2,
        scratch=[pltpu.VMEM((pool_rows, PIX), F32)],
        name="pack_pool",
    )(image_pool, ridge_coef)
    rows = lax.all_to_all(packed, "sup", 0, 0, tiled=True)
    chosen = call(
        select_body, jax.ShapeDtypeStruct((n_grp, n_tgt, LANES), BF16), 3, smem=(0,), name="select_targets"
    )(base, index_col, rows)
    got = lax.all_to_all(chosen, ("chip", "core"), 0, 0, tiled=True)
    side_maps = (PLANES, SIDE, SUB, LANES)
    s_maps, s_inv, dself, mine, gram, picked = call(
        side_body,
        [
            jax.ShapeDtypeStruct((CHAN, *side_maps), F32),
            jax.ShapeDtypeStruct((LAYERS, *side_maps), F32),
            jax.ShapeDtypeStruct((LAYERS, *side_maps), F32),
            jax.ShapeDtypeStruct((n_sup * n_sup_dev, LANES), F32),
            jax.ShapeDtypeStruct((n_sup * n_sup_dev, n_sup * n_sup_dev), F32),
            jax.ShapeDtypeStruct((SUB, LANES), F32),
        ],
        4,
        scratch=[pltpu.VMEM((CHAN * PIX, LANES), F32), maps(2), pltpu.VMEM((16, PIX), F32)],
        flops=10**8,
        name="support_maps",
    )(support, ridge_coef, label_col, rows)
    merged = call(
        merge_body, jax.ShapeDtypeStruct((n_sup_dev, n_tgt, LANES), BF16), 1, name="merge_targets"
    )(got)
    pixels = lax.all_to_all(merged, "sup", 0, 0, tiled=True)
    nat = pltpu.VMEM((SIDE * LANES, LANES), F32)
    sent = call(
        forward_body,
        jax.ShapeDtypeStruct((n_sup_dev, SUB, LANES), F32),
        4,
        scratch=[nat, maps(2), maps(2), pltpu.VMEM((SUB, LANES), F32)],
        flops=10**8,
        name="forward_maps",
    )(pixels, s_maps, s_inv, gram)
    arrived = lax.all_to_all(sent, "sup", 0, 0, tiled=True)
    layer_maps = pltpu.VMEM((LAYERS, *side_maps), F32)
    flat = (CHAN + 1) * PIX
    high, low = call(
        backward_body,
        [jax.ShapeDtypeStruct((flat, LANES), BF16)] * 2,
        4,
        scratch=[nat, maps(2), maps(2), layer_maps, layer_maps, pltpu.VMEM((flat, LANES), F32)],
        flops=10**10,
        name="backward_maps",
    )(pixels, s_maps, s_inv, dself)
    loss_scale = float(PIX) / n_tgt
    wide = n_sup * CHAN * PIX // LANES
    grad = call(
        functools.partial(weigh_body, loss_scale, n_tgt),
        jax.ShapeDtypeStruct((wide, LANES), F32),
        5,
        name="weigh_gradient",
    )(arrived, high, low, picked, support)
    other = lax.ppermute(grad, "core", [(k, (k + 1) % n_core) for k in range(n_core)])
    summed = call(pair_sum_body, jax.ShapeDtypeStruct((n_chip, wide, LANES), F32), 2, name="sum_cores")(grad, other)
    shares = lax.all_to_all(summed, "chip", 0, 0, tiled=True)
    residual = call(
        functools.partial(residual_body, n_sup),
        jax.ShapeDtypeStruct((n_tgt, classes), F32),
        4,
        smem=(0,),
        flops=10**7,
        name="residual",
    )(start, arrived, mine, label_col)
    support_grad = call(last_sum_body, jax.ShapeDtypeStruct(support.shape, F32), 1, name="sum_chips")(shares)
    return (residual, support_grad)


def solution(mesh):
    n_tgt, n_sup = mesh.devices.shape
    parts = Mesh(mesh.devices.reshape(n_tgt // 2, 2, n_sup), ("chip", "core", "sup"))
    tgt = ("chip", "core")
    in_specs = (P((*tgt, "sup"), None), P(), P(tgt), P("sup", None, None), P("sup", None))
    out_specs = (P(tgt, "sup"), P("sup", None, None))
    return jax.shard_map(local, mesh=parts, in_specs=in_specs, out_specs=out_specs, check_vma=False)
```

```python
import functools
import math

import jax
import jax.numpy as jnp
from jax import lax
from jax.experimental import pallas as pl
from jax.experimental.pallas import tpu as pltpu
from jax.sharding import Mesh, PartitionSpec as P

SIDE = 32
CHAN = 3
LAYERS = 4
PIX = SIDE * SIDE
PLANES = 4
SUB = 8
LANES = 128
STEP_COLS = 4

WEIGHT_VAR = 2.0
BIAS_VAR = 0.1
BOX_SCALE = WEIGHT_VAR / 9.0

F32 = jnp.float32
BF16 = jnp.bfloat16
VMEM = pl.BlockSpec(memory_space=pltpu.VMEM)
SMEM = pl.BlockSpec(memory_space=pltpu.SMEM)

ASIN_Q = [
    c * 2.0 / math.pi
    for c in (
        1.5707963050,
        -0.2145988016,
        0.0889789874,
        -0.0501743046,
        0.0308918810,
        -0.0170881256,
        0.0066700901,
        -0.0012624911,
    )
]


def call(body, outs, n_in, scratch=(), smem=(), flops=0, name=None, vmem=4):
    specs = [SMEM if k in smem else VMEM for k in range(n_in)]
    many = isinstance(outs, (list, tuple))
    return pl.pallas_call(
        body,
        out_shape=outs,
        in_specs=specs,
        out_specs=[VMEM] * len(outs) if many else VMEM,
        scratch_shapes=list(scratch),
        compiler_params=pltpu.CompilerParams(vmem_limit_bytes=vmem * 2**20),
        cost_estimate=pl.CostEstimate(flops=flops, bytes_accessed=1 << 20, transcendentals=0),
        name=name,
    )


def three_parts(x):
    high = x.astype(BF16)
    rest = x - high.astype(F32)
    mid = rest.astype(BF16)
    low = (rest - mid.astype(F32)).astype(BF16)
    return high, mid, low


def dot_f32(a, b, dims):
    return lax.dot_general(a, b, (dims, ((), ())), preferred_element_type=F32, precision=lax.Precision.HIGHEST)


def dot_bf16(a, b, dims):
    return lax.dot_general(a, b, (dims, ((), ())), preferred_element_type=F32)


def pack_body(pool_ref, ridge_ref, out_ref, parts_ref):
    rows = pool_ref.shape[0]
    n_sup = ridge_ref.shape[0]
    parts_ref[...] = jnp.zeros_like(parts_ref)
    for k, part in enumerate(three_parts(ridge_ref[...])):
        parts_ref[k * n_sup : (k + 1) * n_sup, :] = part.astype(F32)
    for tile in range(PIX // LANES):
        at = tile * LANES
        pieces = [pool_ref[:, c * PIX + at : c * PIX + at + LANES] for c in range(CHAN)]
        pieces.append(parts_ref[:, at : at + LANES].astype(BF16))
        for r in range(LANES // SIDE):
            cut = [p[:, r * SIDE : (r + 1) * SIDE] for p in pieces]
            out_ref[tile * (LANES // SIDE) + r, :, :] = jnp.concatenate(cut, axis=1)


def select_body(base_ref, index_ref, rows_ref, out_ref):
    n_src, rows, _ = rows_ref.shape
    total = n_src * rows
    data = rows_ref[...].reshape(total, LANES)
    wanted = index_ref[...] - base_ref[0]
    ids = lax.broadcasted_iota(jnp.int32, (wanted.shape[0], total), 1)
    pick = jnp.where(ids == wanted, 1.0, 0.0).astype(BF16)
    got = dot_bf16(pick, data, ((1,), (0,)))
    out_ref[...] = got.astype(BF16).reshape(out_ref.shape)


def merge_body(parts_ref, out_ref):
    total = parts_ref[0].astype(F32)
    for k in range(1, parts_ref.shape[0]):
        total = total + parts_ref[k].astype(F32)
    total = total.astype(BF16)
    for k in range(out_ref.shape[0]):
        out_ref[k] = total


def steps(fn):
    def one(b, carry):
        fn(b * STEP_COLS)
        return carry

    lax.fori_loop(0, SIDE // STEP_COLS, one, 0)


def box(ref, col):
    x = ref[:, pl.ds(col, STEP_COLS + 2)]
    x = x[:, 0:STEP_COLS] + x[:, 1 : STEP_COLS + 1] + x[:, 2 : STEP_COLS + 2]
    return x[0:PLANES] + x[1 : PLANES + 1] + x[2 : PLANES + 2]


def put(ref, col, x):
    at = pl.ds(col + 1, STEP_COLS)
    ref[1 : PLANES + 1, at] = x
    sub = lax.broadcasted_iota(jnp.int32, x.shape[1:], 1)
    ref[PLANES + 1, at] = jnp.where(sub < SUB - 1, pltpu.roll(x[0], SUB - 1, 1), 0.0)
    ref[0, at] = jnp.where(sub > 0, pltpu.roll(x[PLANES - 1], 1, 1), 0.0)


def take(ref, start, step, col):
    planes = []
    for plane in range(PLANES):
        at = start + step * plane + col
        cols = [ref[pl.ds(at + k, SUB, stride=PLANES * step), :] for k in range(STEP_COLS)]
        planes.append(jnp.stack(cols, axis=0))
    return jnp.stack(planes, axis=0)


def q_poly(a):
    acc = ASIN_Q[-1] * a + ASIN_Q[-2]
    for c in ASIN_Q[-3::-1]:
        acc = acc * a + c
    return acc


def act_of(x):
    a = jnp.abs(x)
    left = 1.0 - a
    inv = lax.rsqrt(left)
    value = 1.0 - left * inv * q_poly(a)
    return jnp.where(x < 0.0, -value, value), a, inv


def self_act(var, inv):
    x = 2.0 * var * inv * inv
    left = 1.0 - x
    return 1.0 - left * lax.rsqrt(left) * q_poly(x)


def self_step(ref, col):
    var = BOX_SCALE * box(ref, col) + BIAS_VAR
    return var, lax.rsqrt(1.0 + 2.0 * var)


def spread(pix_ref, nat_ref):
    n_tgt = pix_ref.shape[1]
    row = lax.broadcasted_iota(jnp.int32, (n_tgt, LANES), 0)
    lane = lax.broadcasted_iota(jnp.int32, (n_tgt, LANES), 1)
    ones = jnp.where(lane % n_tgt == row, 1.0, 0.0).astype(BF16)

    def one(d, carry):
        nat_ref[pl.ds(d * LANES, LANES), :] = dot_bf16(pix_ref[d], ones, ((0,), (0,)))
        return carry

    lax.fori_loop(0, SIDE, one, 0, unroll=4)


def spread_support(maps_ref, n_tgt, n_sup, nat_ref):
    rows = maps_ref.shape[1]
    row = lax.broadcasted_iota(jnp.int32, (rows, LANES), 0)
    lane = lax.broadcasted_iota(jnp.int32, (rows, LANES), 1)
    ones = jnp.where((row < 3 * n_sup) & (row % n_sup == lane // n_tgt), 1.0, 0.0).astype(BF16)
    for k in range(nat_ref.shape[0] // PIX):
        nat_ref[k * PIX : (k + 1) * PIX, :] = dot_bf16(maps_ref[k], ones, ((0,), (0,)))


def take_target(nat_ref, c, col):
    return take(nat_ref, c * SIDE, LANES, col)


def take_support(nat_ref, k, col):
    return take(nat_ref, k * PIX, SIDE, col)


def first_maps(tgt_ref, sup_ref, self_ref, pair_ref):
    def one(col):
        own = pair = 0.0
        for c in range(CHAN):
            t = take_target(tgt_ref, c, col)
            own = own + t * t
            pair = pair + t * take_support(sup_ref, c, col)
        put(self_ref, col, own * (1.0 / CHAN))
        put(pair_ref, col, pair * (1.0 / CHAN))

    steps(one)


def flat_box(x):
    at = lax.broadcasted_iota(jnp.int32, x.shape, 1)
    col = at % SIDE
    left = jnp.where(col > 0, pltpu.roll(x, 1, 1), 0.0)
    right = jnp.where(col < SIDE - 1, pltpu.roll(x, PIX - 1, 1), 0.0)
    x = x + left + right
    above = jnp.where(at >= SIDE, pltpu.roll(x, SIDE, 1), 0.0)
    below = jnp.where(at < PIX - SIDE, pltpu.roll(x, PIX - SIDE, 1), 0.0)
    return x + above + below


def side_body(sup_ref, ridge_ref, labels_ref, rows_ref, maps_ref, mine_ref, gram_ref, picked_ref, parts_ref):
    n_sup = sup_ref.shape[1]
    n_tgt = labels_ref.shape[0]
    n_src = rows_ref.shape[0]
    for j in range(n_sup):
        total = jnp.zeros((n_src, LANES), F32)
        for k in range(3):
            total = total + rows_ref[:, k * n_sup + j, :].astype(F32)
        mine_ref[j * n_src : (j + 1) * n_src, :] = total
    lane = lax.broadcasted_iota(jnp.int32, mine_ref.shape, 1)
    mine = jnp.where(lane >= CHAN * SIDE, mine_ref[...], 0.0)
    mine_ref[...] = mine
    gram_ref[...] = dot_f32(mine, mine, ((1,), (1,)))
    hot = labels_ref[...] == lax.broadcasted_iota(jnp.int32, (n_tgt, ridge_ref.shape[1]), 1)
    hot = jnp.where(hot, 1.0, 0.0)
    hot = jnp.concatenate([hot] * n_sup, axis=0)
    picked_ref[...] = jnp.zeros_like(picked_ref)
    picked_ref[0:n_sup, :] = dot_f32(ridge_ref[...], hot, ((1,), (1,)))
    parts_ref[...] = jnp.zeros_like(parts_ref)

    def keep(k, x):
        for i, part in enumerate(three_parts(x)):
            parts_ref[i * n_sup : (i + 1) * n_sup, :] = part.astype(F32)
        maps_ref[k] = parts_ref[...].astype(BF16)

    current = 0.0
    for c in range(CHAN):
        s = sup_ref[c]
        keep(c, s)
        current = current + s * s
    current = current * (1.0 / CHAN)
    for depth in range(LAYERS):
        var = BOX_SCALE * flat_box(current) + BIAS_VAR
        inv = lax.rsqrt(1.0 + 2.0 * var)
        keep(CHAN + depth, inv)
        if depth < LAYERS - 1:
            keep(CHAN + LAYERS + depth, (4.0 / math.pi) * inv * inv * lax.rsqrt(1.0 + 4.0 * var))
            current = self_act(var, inv)


def forward_body(n_sup, pix_ref, maps_ref, gram_ref, out_ref, tgt_ref, sup_ref, self_a, self_b, pair_a, pair_b, acc_ref):
    for ref in (self_a, self_b, pair_a, pair_b):
        ref[...] = jnp.zeros_like(ref)
    spread(pix_ref, tgt_ref)
    spread_support(maps_ref, pix_ref.shape[1], n_sup, sup_ref)
    first_maps(tgt_ref, sup_ref, self_a, pair_a)
    acc_ref[...] = jnp.zeros_like(acc_ref)
    for depth in range(LAYERS):
        self_now, self_later = (self_a, self_b) if depth % 2 == 0 else (self_b, self_a)
        pair_now, pair_later = (pair_a, pair_b) if depth % 2 == 0 else (pair_b, pair_a)

        def one(col, depth=depth, self_now=self_now, self_later=self_later, pair_now=pair_now, pair_later=pair_later):
            var, inv = self_step(self_now, col)
            twice = (2.0 * BOX_SCALE) * box(pair_now, col) + 2.0 * BIAS_VAR
            x = twice * (inv * take_support(sup_ref, CHAN + depth, col))
            value = act_of(x)[0]
            if depth < LAYERS - 1:
                put(self_later, col, self_act(var, inv))
                put(pair_later, col, value)
            else:
                acc_ref[...] += jnp.sum(value, axis=(0, 1))

        steps(one)
    value = jnp.sum(acc_ref[...], axis=0, keepdims=True) * (1.0 / PIX)
    n_dst = out_ref.shape[0]
    for j in range(n_sup):
        out_ref[:, j, :] = gram_ref[j * n_dst : (j + 1) * n_dst, :]
    for k in range(n_sup, out_ref.shape[1]):
        out_ref[:, k, :] = jnp.broadcast_to(value, (n_dst, LANES))


def backward_body(
    n_sup,
    pix_ref,
    maps_ref,
    high_ref,
    low_ref,
    tgt_ref,
    sup_ref,
    self_a,
    self_b,
    pair_a,
    pair_b,
    dcov_ref,
    dvar_ref,
    out_ref,
):
    for ref in (self_a, self_b, pair_a, pair_b):
        ref[...] = jnp.zeros_like(ref)
    spread(pix_ref, tgt_ref)
    spread_support(maps_ref, pix_ref.shape[1], n_sup, sup_ref)
    first_maps(tgt_ref, sup_ref, self_a, pair_a)
    last = LAYERS - 1
    for depth in range(LAYERS):
        self_now, self_later = (self_a, self_b) if depth % 2 == 0 else (self_b, self_a)
        pair_now, pair_later = (pair_a, pair_b) if depth % 2 == 0 else (pair_b, pair_a)

        def one(col, depth=depth, self_now=self_now, self_later=self_later, pair_now=pair_now, pair_later=pair_later):
            at = pl.ds(col, STEP_COLS)
            var, inv = self_step(self_now, col)
            twice = (2.0 * BOX_SCALE) * box(pair_now, col) + 2.0 * BIAS_VAR
            s_inv = take_support(sup_ref, CHAN + depth, col)
            both = inv * s_inv
            x = twice * both
            value, a, left = act_of(x)
            slope = (2.0 / math.pi) * left * lax.rsqrt(1.0 + a)
            d_cov = 2.0 * both * slope
            d_var = -(slope * x) * (s_inv * s_inv)
            if depth < last:
                put(self_later, col, self_act(var, inv))
                put(pair_later, col, value)
                dcov_ref[depth, :, at] = d_cov
                dvar_ref[depth, :, at] = d_var
            else:
                put(pair_later, col, d_cov * (1.0 / PIX))
                put(self_later, col, d_var * (1.0 / PIX))

        steps(one)
    for depth in range(last - 1, -1, -1):
        self_now, self_later = (self_a, self_b) if depth % 2 == 0 else (self_b, self_a)
        pair_now, pair_later = (pair_a, pair_b) if depth % 2 == 0 else (pair_b, pair_a)

        def one(col, depth=depth, self_now=self_now, self_later=self_later, pair_now=pair_now, pair_later=pair_later):
            at = pl.ds(col, STEP_COLS)
            g_pair = BOX_SCALE * box(pair_now, col)
            g_self = BOX_SCALE * box(self_now, col)
            slope = take_support(sup_ref, CHAN + LAYERS + depth, col)
            put(pair_later, col, g_pair * dcov_ref[depth, :, at])
            put(self_later, col, g_self * slope + g_pair * dvar_ref[depth, :, at])

        steps(one)

    def finish(col):
        g_pair = (BOX_SCALE / CHAN) * box(pair_b, col)
        g_self = BOX_SCALE * box(self_b, col)
        for c in range(CHAN + 1):
            g = g_pair * take_target(tgt_ref, c, col) if c < CHAN else g_self
            for plane in range(PLANES):
                for k in range(STEP_COLS):
                    at = c * PIX + plane * SIDE + col + k
                    out_ref[pl.ds(at, SUB, stride=PLANES * SIDE), :] = g[plane, k]

    steps(finish)

    def split(k, carry):
        at = pl.ds(pl.multiple_of(k * 128, 128), 128)
        g = out_ref[at, :]
        high = g.astype(BF16)
        high_ref[at, :] = high
        low_ref[at, :] = (g - high.astype(F32)).astype(BF16)
        return carry

    lax.fori_loop(0, out_ref.shape[0] // 128, split, 0)


def weigh_body(scale, n_tgt, got_ref, high_ref, low_ref, picked_ref, sup_ref, out_ref):
    n_src = got_ref.shape[0]
    n_sup = sup_ref.shape[1]
    rows = got_ref.shape[1]
    gram = jnp.sum(got_ref[...], axis=0)
    values = got_ref[:, n_sup, :]
    lane = lax.broadcasted_iota(jnp.int32, (n_src, LANES), 1)
    big = jnp.concatenate([jnp.where(lane // n_tgt == j, values, 0.0) for j in range(n_sup)], axis=0)
    part = dot_f32(gram, big, ((1,), (0,)))
    part = part + pltpu.roll(part, 64, 1)
    part = part + pltpu.roll(part, 32, 1)
    row = lax.broadcasted_iota(jnp.int32, (rows, LANES), 0)
    lane = lax.broadcasted_iota(jnp.int32, (rows, LANES), 1)
    weight = jnp.where(lane // n_tgt == row, scale * (part - picked_ref[...]), 0.0)
    w_high = weight.astype(BF16)
    w_low = (weight - w_high.astype(F32)).astype(BF16)
    zero = jnp.zeros_like(w_high)
    first = jnp.concatenate([w_high, w_low], axis=0)
    second = jnp.concatenate([w_high, zero], axis=0)
    sums = []
    for c in range(CHAN + 1):
        at = slice(c * PIX, (c + 1) * PIX)
        one = dot_bf16(first, high_ref[at, :], ((1,), (1,)))
        two = dot_bf16(second, low_ref[at, :], ((1,), (1,)))
        sums.append((one[:rows] + one[rows:] + two[:rows])[:n_sup])
    per = PIX // LANES
    for c in range(CHAN):
        grad = sums[c] + (2.0 / CHAN) * sup_ref[c] * sums[CHAN]
        for k in range(per):
            out_ref[pl.ds(c * per + k, n_sup, stride=CHAN * per), :] = grad[:, k * LANES : (k + 1) * LANES]


def residual_body(n_sup, start_ref, got_ref, mine_ref, labels_ref, out_ref):
    n_src = got_ref.shape[0]
    n_tgt, classes = out_ref.shape
    values = got_ref[:, n_sup, :]
    total = jnp.zeros((n_tgt, LANES), F32)
    for j in range(n_sup):
        one = dot_f32(values, mine_ref[j * n_src : (j + 1) * n_src, :], ((0,), (0,)))
        total = total + one[j * n_tgt : (j + 1) * n_tgt, :]
    predicted = total[:, CHAN * SIDE :]
    ids = start_ref[0] + lax.broadcasted_iota(jnp.int32, (n_tgt, classes), 1)
    out_ref[...] = predicted - jnp.where(labels_ref[...] == ids, 1.0, 0.0)


def pair_sum_body(a_ref, b_ref, out_ref):
    total = a_ref[...] + b_ref[...]
    for k in range(out_ref.shape[0]):
        out_ref[k] = total


def last_sum_body(parts_ref, out_ref):
    total = parts_ref[0]
    for k in range(1, parts_ref.shape[0]):
        total = total + parts_ref[k]
    n_sup = out_ref.shape[1]
    per = PIX // LANES
    for j in range(n_sup):
        for c in range(CHAN):
            for k in range(per):
                row = (j * CHAN + c) * per + k
                out_ref[c, j : j + 1, k * LANES : (k + 1) * LANES] = total[row : row + 1, :]


def maps(*lead):
    return pltpu.VMEM((*lead, PLANES + 2, SIDE + 2, SUB, LANES), F32)


def local(image_pool, target_index, labels, support, ridge_coef):
    n_chip, n_core, n_sup_dev = lax.axis_size("chip"), lax.axis_size("core"), lax.axis_size("sup")
    n_grp = n_chip * n_core
    pool_rows = image_pool.shape[0]
    n_sup = support.shape[0]
    n_tgt = labels.shape[0]
    classes = ridge_coef.shape[1] // n_sup_dev
    group = lax.axis_index("chip") * n_core + lax.axis_index("core")
    base = (group * (n_sup_dev * pool_rows))[None].astype(jnp.int32)
    start = (lax.axis_index("sup") * classes)[None].astype(jnp.int32)
    label_col = labels[:, None]
    index_col = target_index[:, None]

    packed = call(
        pack_body,
        jax.ShapeDtypeStruct((n_sup_dev, pool_rows, LANES), BF16),
        2,
        scratch=[pltpu.VMEM((pool_rows, PIX), F32)],
        name="pack_pool",
    )(image_pool, ridge_coef)
    packed, index_col = lax.optimization_barrier((packed, index_col))
    rows = lax.all_to_all(packed, "sup", 0, 0, tiled=True)
    chosen = call(
        select_body, jax.ShapeDtypeStruct((n_grp, n_tgt, LANES), BF16), 3, smem=(0,), name="select_targets"
    )(base, index_col, rows)
    got = lax.all_to_all(chosen, ("chip", "core"), 0, 0, tiled=True)
    by_channel = jnp.swapaxes(support, 0, 1)
    n_maps = CHAN + 2 * LAYERS - 1
    s_maps, mine, gram, picked = call(
        side_body,
        [
            jax.ShapeDtypeStruct((n_maps, 16, PIX), BF16),
            jax.ShapeDtypeStruct((n_sup * n_sup_dev, LANES), F32),
            jax.ShapeDtypeStruct((n_sup * n_sup_dev, n_sup * n_sup_dev), F32),
            jax.ShapeDtypeStruct((SUB, LANES), F32),
        ],
        4,
        scratch=[pltpu.VMEM((16, PIX), F32)],
        flops=10**8,
        name="support_maps",
    )(by_channel, ridge_coef, label_col, rows)
    merged = call(
        merge_body, jax.ShapeDtypeStruct((n_sup_dev, n_tgt, LANES), BF16), 1, name="merge_targets"
    )(got)
    pixels = lax.all_to_all(merged, "sup", 0, 0, tiled=True)
    tgt_nat = pltpu.VMEM((SIDE * LANES, LANES), F32)
    sent = call(
        functools.partial(forward_body, n_sup),
        jax.ShapeDtypeStruct((n_sup_dev, SUB, LANES), F32),
        3,
        scratch=[tgt_nat, pltpu.VMEM(((CHAN + LAYERS) * PIX, LANES), F32), *[maps()] * 4, pltpu.VMEM((SUB, LANES), F32)],
        flops=10**8,
        name="forward_maps",
        vmem=12,
    )(pixels, s_maps, gram)
    arrived = lax.all_to_all(sent, "sup", 0, 0, tiled=True)
    layer_maps = pltpu.VMEM((LAYERS - 1, PLANES, SIDE, SUB, LANES), F32)
    flat = (CHAN + 1) * PIX
    high, low = call(
        functools.partial(backward_body, n_sup),
        [jax.ShapeDtypeStruct((flat, LANES), BF16)] * 2,
        2,
        scratch=[
            tgt_nat,
            pltpu.VMEM((n_maps * PIX, LANES), F32),
            *[maps()] * 4,
            layer_maps,
            layer_maps,
            pltpu.VMEM((flat, LANES), F32),
        ],
        flops=10**10,
        name="backward_maps",
        vmem=20,
    )(pixels, s_maps)
    loss_scale = float(PIX) / n_tgt
    wide = n_sup * CHAN * PIX // LANES
    grad = call(
        functools.partial(weigh_body, loss_scale, n_tgt),
        jax.ShapeDtypeStruct((wide, LANES), F32),
        5,
        name="weigh_gradient",
        vmem=8,
    )(arrived, high, low, picked, by_channel)
    other = lax.ppermute(grad, "core", [(k, (k + 1) % n_core) for k in range(n_core)])
    summed = call(pair_sum_body, jax.ShapeDtypeStruct((n_chip, wide, LANES), F32), 2, name="sum_cores")(grad, other)
    shares = lax.all_to_all(summed, "chip", 0, 0, tiled=True)
    residual = call(
        functools.partial(residual_body, n_sup),
        jax.ShapeDtypeStruct((n_tgt, classes), F32),
        4,
        smem=(0,),
        flops=10**7,
        name="residual",
    )(start, arrived, mine, label_col)
    total = call(last_sum_body, jax.ShapeDtypeStruct(by_channel.shape, F32), 1, name="sum_chips")(shares)
    return (residual, jnp.swapaxes(total, 0, 1))


def solution(mesh):
    n_tgt, n_sup = mesh.devices.shape
    parts = Mesh(mesh.devices.reshape(n_tgt // 2, 2, n_sup), ("chip", "core", "sup"))
    tgt = ("chip", "core")
    in_specs = (P((*tgt, "sup"), None), P(), P(tgt), P("sup", None, None), P("sup", None))
    out_specs = (P(tgt, "sup"), P("sup", None, None))
    return jax.shard_map(local, mesh=parts, in_specs=in_specs, out_specs=out_specs, check_vma=False)
```

```python
import functools
import math

import jax
import jax.numpy as jnp
from jax import lax
from jax.experimental import pallas as pl
from jax.experimental.pallas import tpu as pltpu
from jax.sharding import Mesh, PartitionSpec as P

SIDE = 32
CHAN = 3
LAYERS = 4
PIX = SIDE * SIDE
SUB = 8
LANES = 128
TILES = SIDE // SUB
STEP_ROWS = 8
STEP_PIX = STEP_ROWS * SIDE
PARTS = 3

WEIGHT_VAR = 2.0
BIAS_VAR = 0.1
BOX_SCALE = WEIGHT_VAR / 9.0

F32 = jnp.float32
BF16 = jnp.bfloat16
VMEM = pl.BlockSpec(memory_space=pltpu.VMEM)
SMEM = pl.BlockSpec(memory_space=pltpu.SMEM)

ASIN_Q = [
    c * 2.0 / math.pi
    for c in (
        1.5707963050,
        -0.2145988016,
        0.0889789874,
        -0.0501743046,
        0.0308918810,
        -0.0170881256,
        0.0066700901,
        -0.0012624911,
    )
]


def call(body, outs, n_in, scratch=(), smem=(), flops=0, name=None, vmem=4):
    specs = [SMEM if k in smem else VMEM for k in range(n_in)]
    many = isinstance(outs, (list, tuple))
    return pl.pallas_call(
        body,
        out_shape=outs,
        in_specs=specs,
        out_specs=[VMEM] * len(outs) if many else VMEM,
        scratch_shapes=list(scratch),
        compiler_params=pltpu.CompilerParams(vmem_limit_bytes=vmem * 2**20),
        cost_estimate=pl.CostEstimate(flops=flops, bytes_accessed=1 << 20, transcendentals=0),
        name=name,
    )


def three_parts(x):
    high = x.astype(BF16)
    rest = x - high.astype(F32)
    mid = rest.astype(BF16)
    low = (rest - mid.astype(F32)).astype(BF16)
    return high, mid, low


def dot_f32(a, b, dims):
    return lax.dot_general(a, b, (dims, ((), ())), preferred_element_type=F32, precision=lax.Precision.HIGHEST)


def dot_bf16(a, b, dims):
    return lax.dot_general(a, b, (dims, ((), ())), preferred_element_type=F32)


def pack_body(pool_ref, ridge_ref, out_ref, parts_ref):
    rows = pool_ref.shape[0]
    n_sup = ridge_ref.shape[0]
    parts_ref[...] = jnp.zeros_like(parts_ref)
    for k, part in enumerate(three_parts(ridge_ref[...])):
        parts_ref[k * n_sup : (k + 1) * n_sup, :] = part.astype(F32)
    for tile in range(PIX // LANES):
        at = tile * LANES
        pieces = [pool_ref[:, c * PIX + at : c * PIX + at + LANES] for c in range(CHAN)]
        pieces.append(parts_ref[:, at : at + LANES].astype(BF16))
        for r in range(LANES // SIDE):
            cut = [p[:, r * SIDE : (r + 1) * SIDE] for p in pieces]
            out_ref[tile * (LANES // SIDE) + r, :, :] = jnp.concatenate(cut, axis=1)


def select_body(base_ref, index_ref, rows_ref, out_ref):
    n_src, rows, _ = rows_ref.shape
    total = n_src * rows
    data = rows_ref[...].reshape(total, LANES)
    wanted = index_ref[...] - base_ref[0]
    ids = lax.broadcasted_iota(jnp.int32, (wanted.shape[0], total), 1)
    pick = jnp.where(ids == wanted, 1.0, 0.0).astype(BF16)
    got = dot_bf16(pick, data, ((1,), (0,)))
    out_ref[...] = got.astype(BF16).reshape(out_ref.shape)


def merge_body(parts_ref, out_ref):
    total = parts_ref[0].astype(F32)
    for k in range(1, parts_ref.shape[0]):
        total = total + parts_ref[k].astype(F32)
    turned = total.T
    n_tgt = turned.shape[1]
    cut = [turned[c * SIDE : (c + 1) * SIDE, :] for c in range(CHAN)]
    cut.append(jnp.zeros((SIDE, LANES - CHAN * n_tgt), F32))
    message = jnp.concatenate(cut, axis=1).astype(BF16)
    for k in range(out_ref.shape[0]):
        out_ref[k] = message


def steps(fn):
    for b in range(SIDE // STEP_ROWS):
        fn(b)


def rows_of(b):
    return pl.ds(b * STEP_ROWS, STEP_ROWS)


def pixels_of(b):
    return pl.ds(b * STEP_PIX, STEP_PIX)


def as_map(x):
    return x.reshape(x.shape[0] // SIDE, TILES, SUB, LANES)


def box(ref, row, n):
    x = ref[pl.ds(row, n + 2)]
    x = x[0:n] + x[1 : n + 1] + x[2 : n + 2]
    sub = lax.broadcasted_iota(jnp.int32, x.shape, 2)
    zero = jnp.zeros_like(x[:, 0:1])
    left = pltpu.roll(x, 1, 2)
    right = pltpu.roll(x, SUB - 1, 2)
    left = jnp.where(sub == 0, jnp.concatenate([zero, left[:, : TILES - 1]], axis=1), left)
    right = jnp.where(sub == SUB - 1, jnp.concatenate([right[:, 1:], zero], axis=1), right)
    return x + left + right


def step_box(ref, b):
    return box(ref, b * STEP_ROWS, STEP_ROWS)


def put(ref, b, x):
    ref[pl.ds(b * STEP_ROWS + 1, STEP_ROWS)] = x


def q_poly(a):
    acc = ASIN_Q[-1] * a + ASIN_Q[-2]
    for c in ASIN_Q[-3::-1]:
        acc = acc * a + c
    return acc


def act_of(x):
    a = jnp.abs(x)
    left = 1.0 - a
    inv = lax.rsqrt(left)
    value = 1.0 - left * inv * q_poly(a)
    return jnp.where(x < 0.0, -value, value), a, inv


def self_act(var, inv):
    x = 2.0 * var * inv * inv
    left = 1.0 - x
    return 1.0 - left * lax.rsqrt(left) * q_poly(x)


def flat_box(x):
    at = lax.broadcasted_iota(jnp.int32, x.shape, 1)
    col = at % SIDE
    left = jnp.where(col > 0, pltpu.roll(x, 1, 1), 0.0)
    right = jnp.where(col < SIDE - 1, pltpu.roll(x, PIX - 1, 1), 0.0)
    x = x + left + right
    above = jnp.where(at >= SIDE, pltpu.roll(x, SIDE, 1), 0.0)
    below = jnp.where(at < PIX - SIDE, pltpu.roll(x, PIX - SIDE, 1), 0.0)
    return x + above + below


def side_body(sup_ref, ridge_ref, labels_ref, rows_ref, maps_ref, mine_ref, gram_ref, picked_ref, parts_ref):
    n_sup = sup_ref.shape[1]
    n_tgt = labels_ref.shape[0]
    n_src = rows_ref.shape[0]
    for j in range(n_sup):
        total = jnp.zeros((n_src, LANES), F32)
        for k in range(PARTS):
            total = total + rows_ref[:, k * n_sup + j, :].astype(F32)
        mine_ref[j * n_src : (j + 1) * n_src, :] = total
    lane = lax.broadcasted_iota(jnp.int32, mine_ref.shape, 1)
    mine = jnp.where(lane >= CHAN * SIDE, mine_ref[...], 0.0)
    mine_ref[...] = mine
    gram_ref[...] = dot_f32(mine, mine, ((1,), (1,)))
    hot = labels_ref[...] == lax.broadcasted_iota(jnp.int32, (n_tgt, ridge_ref.shape[1]), 1)
    hot = jnp.where(hot, 1.0, 0.0)
    hot = jnp.concatenate([hot] * n_sup, axis=0)
    picked_ref[...] = jnp.zeros_like(picked_ref)
    picked_ref[0:n_sup, :] = dot_f32(ridge_ref[...], hot, ((1,), (1,)))
    parts_ref[...] = jnp.zeros_like(parts_ref)

    def keep(k, x):
        for i, part in enumerate(three_parts(x)):
            at = (k * PARTS + i) * n_sup
            parts_ref[at : at + n_sup, :] = part.astype(F32)

    current = 0.0
    for c in range(CHAN):
        s = sup_ref[c]
        keep(c, s)
        current = current + s * s
    current = current * (1.0 / CHAN)
    for depth in range(LAYERS):
        var = BOX_SCALE * flat_box(current) + BIAS_VAR
        inv = lax.rsqrt(1.0 + 2.0 * var)
        keep(CHAN + depth, inv)
        if depth < LAYERS - 1:
            keep(CHAN + LAYERS + depth, (4.0 / math.pi) * inv * inv * lax.rsqrt(1.0 + 4.0 * var))
            current = self_act(var, inv)
    row = lax.broadcasted_iota(jnp.int32, (LANES, LANES), 0)
    lane = lax.broadcasted_iota(jnp.int32, (LANES, LANES), 1)
    same = jnp.where(row == lane, 1.0, 0.0).astype(BF16)
    maps_ref[...] = dot_bf16(parts_ref[...].astype(BF16), same, ((0,), (0,))).astype(BF16)


def fill_spreads(n_sup, n_tgt, tgt_ref, sup_ref):
    row = lax.broadcasted_iota(jnp.int32, (LANES, LANES), 0)
    lane = lax.broadcasted_iota(jnp.int32, (LANES, LANES), 1)
    own = row % n_tgt == lane % n_tgt
    for c in range(CHAN):
        tgt_ref[c] = jnp.where((row // n_tgt == c) & own, 1.0, 0.0).astype(BF16)
    own = row % n_sup == lane // n_tgt
    for k in range(sup_ref.shape[0]):
        sup_ref[k] = jnp.where((row // (PARTS * n_sup) == k) & own, 1.0, 0.0).astype(BF16)


def target_map(pix_ref, tgt_ref, c, b):
    pix = pix_ref[rows_of(b)].reshape(STEP_PIX, LANES)
    return as_map(dot_bf16(pix, tgt_ref[c], ((1,), (0,))))


def support_map(maps_ref, sup_ref, k, b):
    return as_map(dot_bf16(maps_ref[pixels_of(b), :], sup_ref[k], ((1,), (0,))))


QUARTERS = 4
QUARTER_ROWS = SIDE // QUARTERS
PER_QUARTER = QUARTER_ROWS // STEP_ROWS


def lane_block(shape):
    return lax.broadcasted_iota(jnp.int32, shape, len(shape) - 1) // (LANES // QUARTERS)


def put_edges(ref, first, final):
    width = LANES // QUARTERS
    block = lane_block(first.shape)
    ref[0] = jnp.where(block > 0, pltpu.roll(final, width, 2), 0.0)
    ref[QUARTER_ROWS + 1] = jnp.where(block < QUARTERS - 1, pltpu.roll(first, LANES - width, 2), 0.0)


def first_maps(pix_ref, maps_ref, tgt_ref, sup_ref, self_a, self_b, inv_ref, pair_ref):
    def one(b):
        own = pair = 0.0
        for c in range(CHAN):
            t = target_map(pix_ref, tgt_ref, c, b)
            own = own + t * t
            pair = pair + t * support_map(maps_ref, sup_ref, c, b)
        put(pair_ref, b, pair * (1.0 / CHAN))
        at = pl.ds((b % PER_QUARTER) * STEP_ROWS + 1, STEP_ROWS)
        self_a[at] = jnp.where(lane_block(own.shape) == b // PER_QUARTER, own * (1.0 / CHAN), self_a[at])

    steps(one)
    put_edges(self_a, self_a[1], self_a[QUARTER_ROWS])
    for depth in range(LAYERS):
        now, later = (self_a, self_b) if depth % 2 == 0 else (self_b, self_a)
        for part in range(PER_QUARTER):
            var = BOX_SCALE * box(now, part * STEP_ROWS, STEP_ROWS) + BIAS_VAR
            inv = lax.rsqrt(1.0 + 2.0 * var)
            inv_ref[depth, part] = inv
            if depth < LAYERS - 1:
                value = self_act(var, inv)
                later[part * STEP_ROWS + 1 : (part + 1) * STEP_ROWS + 1] = value
        if depth < LAYERS - 1:
            put_edges(later, later[1], later[QUARTER_ROWS])


def target_inv(inv_ref, depth, b):
    x = inv_ref[depth, b % PER_QUARTER]
    x = jnp.where(lane_block(x.shape) == b // PER_QUARTER, x, 0.0)
    x = x + pltpu.roll(x, LANES // 2, 3)
    return x + pltpu.roll(x, LANES // 4, 3)


def forward_body(
    n_sup, pix_ref, maps_ref, gram_ref, out_ref, tgt_ref, sup_ref, self_a, self_b, inv_ref, pair_a, pair_b, acc_ref
):
    n_tgt = LANES // n_sup
    for ref in (self_a, self_b, pair_a, pair_b):
        ref[...] = jnp.zeros_like(ref)
    fill_spreads(n_sup, n_tgt, tgt_ref, sup_ref)
    first_maps(pix_ref, maps_ref, tgt_ref, sup_ref, self_a, self_b, inv_ref, pair_a)
    acc_ref[...] = jnp.zeros_like(acc_ref)
    for depth in range(LAYERS):
        now, later = (pair_a, pair_b) if depth % 2 == 0 else (pair_b, pair_a)

        def one(b, depth=depth, now=now, later=later):
            twice = (2.0 * BOX_SCALE) * step_box(now, b) + 2.0 * BIAS_VAR
            both = target_inv(inv_ref, depth, b) * support_map(maps_ref, sup_ref, CHAN + depth, b)
            value = act_of(twice * both)[0]
            if depth < LAYERS - 1:
                put(later, b, value)
            else:
                acc_ref[...] += jnp.sum(value, axis=(0, 1))

        steps(one)
    value = jnp.sum(acc_ref[...], axis=0, keepdims=True) * (1.0 / PIX)
    n_dst = out_ref.shape[0]
    for j in range(n_sup):
        out_ref[:, j, :] = gram_ref[j * n_dst : (j + 1) * n_dst, :]
    for k in range(n_sup, out_ref.shape[1]):
        out_ref[:, k, :] = jnp.broadcast_to(value, (n_dst, LANES))


def backward_body(
    n_sup,
    pix_ref,
    maps_ref,
    high_ref,
    low_ref,
    tgt_ref,
    sup_ref,
    self_a,
    self_b,
    inv_ref,
    pair_a,
    pair_b,
    grad_a,
    grad_b,
    dcov_ref,
    dvar_ref,
):
    n_tgt = LANES // n_sup
    for ref in (self_a, self_b, pair_a, pair_b, grad_a, grad_b):
        ref[...] = jnp.zeros_like(ref)
    fill_spreads(n_sup, n_tgt, tgt_ref, sup_ref)
    first_maps(pix_ref, maps_ref, tgt_ref, sup_ref, self_a, self_b, inv_ref, pair_a)
    last = LAYERS - 1
    for depth in range(LAYERS):
        now, later = (pair_a, pair_b) if depth % 2 == 0 else (pair_b, pair_a)

        def one(b, depth=depth, now=now, later=later):
            twice = (2.0 * BOX_SCALE) * step_box(now, b) + 2.0 * BIAS_VAR
            s_inv = support_map(maps_ref, sup_ref, CHAN + depth, b)
            both = target_inv(inv_ref, depth, b) * s_inv
            x = twice * both
            if depth < last:
                value, a, left = act_of(x)
                put(later, b, value)
            else:
                a = jnp.abs(x)
                left = lax.rsqrt(1.0 - a)
            slope = (2.0 / math.pi) * left * lax.rsqrt(1.0 + a)
            d_cov = 2.0 * both * slope
            d_var = -(slope * x) * (s_inv * s_inv)
            if depth < last:
                dcov_ref[depth, rows_of(b)] = d_cov
                dvar_ref[depth, rows_of(b)] = d_var
            else:
                put(later, b, d_cov * (1.0 / PIX))
                put(grad_a, b, d_var * (1.0 / PIX))

        steps(one)
    for depth in range(last - 1, -1, -1):
        now, later = (pair_a, pair_b) if depth % 2 == 0 else (pair_b, pair_a)
        own_now, own_later = (grad_a, grad_b) if depth % 2 == 0 else (grad_b, grad_a)

        def one(b, depth=depth, now=now, later=later, own_now=own_now, own_later=own_later):
            g_pair = BOX_SCALE * step_box(now, b)
            g_self = BOX_SCALE * step_box(own_now, b)
            slope = support_map(maps_ref, sup_ref, CHAN + LAYERS + depth, b)
            put(later, b, g_pair * dcov_ref[depth, rows_of(b)])
            put(own_later, b, g_self * slope + g_pair * dvar_ref[depth, rows_of(b)])

        steps(one)

    def finish(b):
        g_pair = (BOX_SCALE / CHAN) * step_box(pair_b, b)
        for c in range(CHAN + 1):
            g = g_pair * target_map(pix_ref, tgt_ref, c, b) if c < CHAN else BOX_SCALE * step_box(grad_b, b)
            g = g.reshape(STEP_PIX, LANES)
            high = g.astype(BF16)
            at = pl.ds(c * PIX + b * STEP_PIX, STEP_PIX)
            high_ref[at, :] = high
            low_ref[at, :] = (g - high.astype(F32)).astype(BF16)

    steps(finish)


def weigh_body(scale, n_tgt, got_ref, high_ref, low_ref, picked_ref, sup_ref, out_ref):
    n_src = got_ref.shape[0]
    n_sup = sup_ref.shape[1]
    rows = got_ref.shape[1]
    gram = jnp.sum(got_ref[...], axis=0)
    values = got_ref[:, n_sup, :]
    lane = lax.broadcasted_iota(jnp.int32, (n_src, LANES), 1)
    big = jnp.concatenate([jnp.where(lane // n_tgt == j, values, 0.0) for j in range(n_sup)], axis=0)
    part = dot_f32(gram, big, ((1,), (0,)))
    part = part + pltpu.roll(part, 64, 1)
    part = part + pltpu.roll(part, 32, 1)
    row = lax.broadcasted_iota(jnp.int32, (rows, LANES), 0)
    lane = lax.broadcasted_iota(jnp.int32, (rows, LANES), 1)
    weight = jnp.where(lane // n_tgt == row, scale * (part - picked_ref[...]), 0.0)
    w_high = weight.astype(BF16)
    w_low = (weight - w_high.astype(F32)).astype(BF16)
    zero = jnp.zeros_like(w_high)
    first = jnp.concatenate([w_high, w_low], axis=0)
    second = jnp.concatenate([w_high, zero], axis=0)
    sums = []
    for c in range(CHAN + 1):
        at = slice(c * PIX, (c + 1) * PIX)
        one = dot_bf16(first, high_ref[at, :], ((1,), (1,)))
        two = dot_bf16(second, low_ref[at, :], ((1,), (1,)))
        sums.append((one[:rows] + one[rows:] + two[:rows])[:n_sup])
    per = PIX // LANES
    for c in range(CHAN):
        grad = sums[c] + (2.0 / CHAN) * sup_ref[c] * sums[CHAN]
        for k in range(per):
            out_ref[pl.ds(c * per + k, n_sup, stride=CHAN * per), :] = grad[:, k * LANES : (k + 1) * LANES]


def residual_body(n_sup, start_ref, got_ref, mine_ref, labels_ref, out_ref):
    n_src = got_ref.shape[0]
    n_tgt, classes = out_ref.shape
    values = got_ref[:, n_sup, :]
    total = jnp.zeros((n_tgt, LANES), F32)
    for j in range(n_sup):
        one = dot_f32(values, mine_ref[j * n_src : (j + 1) * n_src, :], ((0,), (0,)))
        total = total + one[j * n_tgt : (j + 1) * n_tgt, :]
    predicted = total[:, CHAN * SIDE :]
    ids = start_ref[0] + lax.broadcasted_iota(jnp.int32, (n_tgt, classes), 1)
    out_ref[...] = predicted - jnp.where(labels_ref[...] == ids, 1.0, 0.0)


def pair_sum_body(a_ref, b_ref, out_ref):
    total = a_ref[...] + b_ref[...]
    for k in range(out_ref.shape[0]):
        out_ref[k] = total


def last_sum_body(parts_ref, out_ref):
    total = parts_ref[0]
    for k in range(1, parts_ref.shape[0]):
        total = total + parts_ref[k]
    n_sup = out_ref.shape[1]
    per = PIX // LANES
    for j in range(n_sup):
        for c in range(CHAN):
            for k in range(per):
                row = (j * CHAN + c) * per + k
                out_ref[c, j : j + 1, k * LANES : (k + 1) * LANES] = total[row : row + 1, :]


def maps(rows):
    return pltpu.VMEM((rows, TILES, SUB, LANES), F32)


def map_scratch(n_maps):
    return [
        pltpu.VMEM((CHAN, LANES, LANES), BF16),
        pltpu.VMEM((n_maps, LANES, LANES), BF16),
        maps(QUARTER_ROWS + 2),
        maps(QUARTER_ROWS + 2),
        pltpu.VMEM((LAYERS, PER_QUARTER, STEP_ROWS, TILES, SUB, LANES), F32),
        maps(SIDE + 2),
        maps(SIDE + 2),
    ]


def local(image_pool, target_index, labels, support, ridge_coef):
    n_chip, n_core, n_sup_dev = lax.axis_size("chip"), lax.axis_size("core"), lax.axis_size("sup")
    n_grp = n_chip * n_core
    pool_rows = image_pool.shape[0]
    n_sup = support.shape[0]
    n_tgt = labels.shape[0]
    classes = ridge_coef.shape[1] // n_sup_dev
    group = lax.axis_index("chip") * n_core + lax.axis_index("core")
    base = (group * (n_sup_dev * pool_rows))[None].astype(jnp.int32)
    start = (lax.axis_index("sup") * classes)[None].astype(jnp.int32)
    label_col = labels[:, None]
    index_col = target_index[:, None]

    packed = call(
        pack_body,
        jax.ShapeDtypeStruct((n_sup_dev, pool_rows, LANES), BF16),
        2,
        scratch=[pltpu.VMEM((pool_rows, PIX), F32)],
        name="pack_pool",
    )(image_pool, ridge_coef)
    packed, index_col = lax.optimization_barrier((packed, index_col))
    rows = lax.all_to_all(packed, "sup", 0, 0, tiled=True)
    chosen = call(
        select_body, jax.ShapeDtypeStruct((n_grp, n_tgt, LANES), BF16), 3, smem=(0,), name="select_targets"
    )(base, index_col, rows)
    got = lax.all_to_all(chosen, ("chip", "core"), 0, 0, tiled=True)
    by_channel = jnp.swapaxes(support, 0, 1)
    n_maps = CHAN + 2 * LAYERS - 1
    s_maps, mine, gram, picked = call(
        side_body,
        [
            jax.ShapeDtypeStruct((PIX, LANES), BF16),
            jax.ShapeDtypeStruct((n_sup * n_sup_dev, LANES), F32),
            jax.ShapeDtypeStruct((n_sup * n_sup_dev, n_sup * n_sup_dev), F32),
            jax.ShapeDtypeStruct((SUB, LANES), F32),
        ],
        4,
        scratch=[pltpu.VMEM((LANES, PIX), F32)],
        flops=10**8,
        name="support_maps",
    )(by_channel, ridge_coef, label_col, rows)
    merged = call(
        merge_body, jax.ShapeDtypeStruct((n_sup_dev, SIDE, LANES), BF16), 1, name="merge_targets"
    )(got)
    pixels = lax.all_to_all(merged, "sup", 0, 0, tiled=True)
    sent = call(
        functools.partial(forward_body, n_sup),
        jax.ShapeDtypeStruct((n_sup_dev, SUB, LANES), F32),
        3,
        scratch=[*map_scratch(CHAN + LAYERS), pltpu.VMEM((SUB, LANES), F32)],
        flops=10**8,
        name="forward_maps",
        vmem=12,
    )(pixels, s_maps, gram)
    arrived = lax.all_to_all(sent, "sup", 0, 0, tiled=True)
    layer_maps = pltpu.VMEM((LAYERS - 1, SIDE, TILES, SUB, LANES), F32)
    flat = (CHAN + 1) * PIX
    high, low = call(
        functools.partial(backward_body, n_sup),
        [jax.ShapeDtypeStruct((flat, LANES), BF16)] * 2,
        2,
        scratch=[*map_scratch(n_maps), maps(SIDE + 2), maps(SIDE + 2), layer_maps, layer_maps],
        flops=10**10,
        name="backward_maps",
        vmem=20,
    )(pixels, s_maps)
    loss_scale = float(PIX) / n_tgt
    wide = n_sup * CHAN * PIX // LANES
    grad = call(
        functools.partial(weigh_body, loss_scale, n_tgt),
        jax.ShapeDtypeStruct((wide, LANES), F32),
        5,
        name="weigh_gradient",
        vmem=8,
    )(arrived, high, low, picked, by_channel)
    other = lax.ppermute(grad, "core", [(k, (k + 1) % n_core) for k in range(n_core)])
    summed = call(pair_sum_body, jax.ShapeDtypeStruct((n_chip, wide, LANES), F32), 2, name="sum_cores")(grad, other)
    shares = lax.all_to_all(summed, "chip", 0, 0, tiled=True)
    residual = call(
        functools.partial(residual_body, n_sup),
        jax.ShapeDtypeStruct((n_tgt, classes), F32),
        4,
        smem=(0,),
        flops=10**7,
        name="residual",
    )(start, arrived, mine, label_col)
    total = call(last_sum_body, jax.ShapeDtypeStruct(by_channel.shape, F32), 1, name="sum_chips")(shares)
    return (residual, jnp.swapaxes(total, 0, 1))


def solution(mesh):
    n_tgt, n_sup = mesh.devices.shape
    parts = Mesh(mesh.devices.reshape(n_tgt // 2, 2, n_sup), ("chip", "core", "sup"))
    tgt = ("chip", "core")
    in_specs = (P((*tgt, "sup"), None), P(), P(tgt), P("sup", None, None), P("sup", None))
    out_specs = (P(tgt, "sup"), P("sup", None, None))
    return jax.shard_map(local, mesh=parts, in_specs=in_specs, out_specs=out_specs, check_vma=False)
```

```python
import functools
import math

import jax
import jax.numpy as jnp
from jax import lax
from jax.experimental import pallas as pl
from jax.experimental.pallas import tpu as pltpu
from jax.sharding import Mesh, PartitionSpec as P

SIDE = 32
CHAN = 3
LAYERS = 4
PIX = SIDE * SIDE
SUB = 8
LANES = 128
TILES = SIDE // SUB
STEP_ROWS = 8
STEP_PIX = STEP_ROWS * SIDE
PARTS = 3

WEIGHT_VAR = 2.0
BIAS_VAR = 0.1
BOX_SCALE = WEIGHT_VAR / 9.0

F32 = jnp.float32
BF16 = jnp.bfloat16
VMEM = pl.BlockSpec(memory_space=pltpu.VMEM)
SMEM = pl.BlockSpec(memory_space=pltpu.SMEM)

ASIN_Q = [
    c * 2.0 / math.pi
    for c in (
        1.5707963050,
        -0.2145988016,
        0.0889789874,
        -0.0501743046,
        0.0308918810,
        -0.0170881256,
        0.0066700901,
        -0.0012624911,
    )
]


def call(body, outs, n_in, scratch=(), smem=(), flops=0, name=None, vmem=4):
    specs = [SMEM if k in smem else VMEM for k in range(n_in)]
    many = isinstance(outs, (list, tuple))
    return pl.pallas_call(
        body,
        out_shape=outs,
        in_specs=specs,
        out_specs=[VMEM] * len(outs) if many else VMEM,
        scratch_shapes=list(scratch),
        compiler_params=pltpu.CompilerParams(vmem_limit_bytes=vmem * 2**20),
        cost_estimate=pl.CostEstimate(flops=flops, bytes_accessed=1 << 20, transcendentals=0),
        name=name,
    )


def three_parts(x):
    high = x.astype(BF16)
    rest = x - high.astype(F32)
    mid = rest.astype(BF16)
    low = (rest - mid.astype(F32)).astype(BF16)
    return high, mid, low


def dot_f32(a, b, dims):
    return lax.dot_general(a, b, (dims, ((), ())), preferred_element_type=F32, precision=lax.Precision.HIGHEST)


def dot_bf16(a, b, dims):
    return lax.dot_general(a, b, (dims, ((), ())), preferred_element_type=F32)


def pack_body(pool_ref, ridge_ref, out_ref, parts_ref):
    n_sup = ridge_ref.shape[0]
    halves = out_ref.shape[1]
    parts_ref[...] = jnp.zeros_like(parts_ref)
    for k, part in enumerate(three_parts(ridge_ref[...])):
        parts_ref[k * n_sup : (k + 1) * n_sup, :] = part.astype(F32)
    for tile in range(PIX // LANES):
        at = tile * LANES
        pieces = [pool_ref[:, c * PIX + at : c * PIX + at + LANES] for c in range(CHAN)]
        for r in range(LANES // SIDE):
            cut = [p[:, r * SIDE : (r + 1) * SIDE] for p in pieces]
            image_row = tile * (LANES // SIDE) + r
            owner, half = image_row // halves, image_row % halves
            first = (half * (SIDE // halves) + owner) * SIDE
            cut.append(parts_ref[:, first : first + SIDE].astype(BF16))
            out_ref[owner, half] = jnp.concatenate(cut, axis=1)


def select_body(at_ref, index_ref, rows_ref, out_ref):
    n_src, halves, rows, _ = rows_ref.shape
    n_dst, _, n_tgt, _ = out_ref.shape
    total = n_src * rows
    wanted = index_ref[...] - at_ref[0]
    ids = lax.broadcasted_iota(jnp.int32, (wanted.shape[0], total), 1)
    pick = jnp.where(ids == wanted, 1.0, 0.0).astype(BF16)
    lane = lax.broadcasted_iota(jnp.int32, (n_tgt, LANES), 1)
    share = n_src // (n_dst // halves)
    for half in range(halves):
        data = rows_ref[:, half].reshape(total, LANES)
        got = dot_bf16(pick, data, ((1,), (0,)))
        ridge = rows_ref[pl.ds(at_ref[1] * share, share), half, 0 : n_tgt // share].reshape(n_tgt, LANES).astype(F32)
        for k in range(n_dst // halves):
            message = jnp.where(lane < CHAN * SIDE, got[k * n_tgt : (k + 1) * n_tgt], ridge).astype(BF16)
            for twin in range(halves):
                out_ref[k * halves + twin, half] = message


def merge_body(parts_ref, out_ref):
    n_dst, halves, _, _ = out_ref.shape
    for half in range(halves):
        total = parts_ref[0, half].astype(F32)
        for k in range(1, parts_ref.shape[0]):
            total = total + parts_ref[k, half].astype(F32)
        turned = total.T
        n_tgt = turned.shape[1]
        cut = [turned[c * SIDE : (c + 1) * SIDE, :] for c in range(CHAN)]
        cut.append(jnp.zeros((SIDE, LANES - CHAN * n_tgt), F32))
        message = jnp.concatenate(cut, axis=1).astype(BF16)
        for k in range(n_dst):
            out_ref[k, half] = message


def steps(fn):
    for b in range(SIDE // STEP_ROWS):
        fn(b)


def rows_of(b):
    return pl.ds(b * STEP_ROWS, STEP_ROWS)


def pixels_of(b):
    return pl.ds(b * STEP_PIX, STEP_PIX)


def as_map(x):
    return x.reshape(x.shape[0] // SIDE, TILES, SUB, LANES)


def box(ref, row, n):
    x = ref[pl.ds(row, n + 2)]
    x = x[0:n] + x[1 : n + 1] + x[2 : n + 2]
    sub = lax.broadcasted_iota(jnp.int32, x.shape, 2)
    zero = jnp.zeros_like(x[:, 0:1])
    left = pltpu.roll(x, 1, 2)
    right = pltpu.roll(x, SUB - 1, 2)
    left = jnp.where(sub == 0, jnp.concatenate([zero, left[:, : TILES - 1]], axis=1), left)
    right = jnp.where(sub == SUB - 1, jnp.concatenate([right[:, 1:], zero], axis=1), right)
    return x + left + right


def step_box(ref, b):
    return box(ref, b * STEP_ROWS, STEP_ROWS)


def put(ref, b, x):
    ref[pl.ds(b * STEP_ROWS + 1, STEP_ROWS)] = x


def q_poly(a):
    acc = ASIN_Q[-1] * a + ASIN_Q[-2]
    for c in ASIN_Q[-3::-1]:
        acc = acc * a + c
    return acc


def act_of(x):
    a = jnp.abs(x)
    left = 1.0 - a
    inv = lax.rsqrt(left)
    value = 1.0 - left * inv * q_poly(a)
    return jnp.where(x < 0.0, -value, value), a, inv


def self_act(var, inv):
    x = 2.0 * var * inv * inv
    left = 1.0 - x
    return 1.0 - left * lax.rsqrt(left) * q_poly(x)


def flat_box(x):
    at = lax.broadcasted_iota(jnp.int32, x.shape, 1)
    col = at % SIDE
    left = jnp.where(col > 0, pltpu.roll(x, 1, 1), 0.0)
    right = jnp.where(col < SIDE - 1, pltpu.roll(x, PIX - 1, 1), 0.0)
    x = x + left + right
    above = jnp.where(at >= SIDE, pltpu.roll(x, SIDE, 1), 0.0)
    below = jnp.where(at < PIX - SIDE, pltpu.roll(x, PIX - SIDE, 1), 0.0)
    return x + above + below


def side_body(half_ref, sup_ref, ridge_ref, labels_ref, got_ref, maps_ref, mine_ref, gram_ref, picked_ref, parts_ref):
    n_sup = sup_ref.shape[1]
    n_tgt = labels_ref.shape[0]
    n_parts, halves, n_rows, _ = got_ref.shape
    got = got_ref[:, half_ref[0]].astype(F32)
    n_src = mine_ref.shape[0] // n_sup
    share = n_src // n_parts
    for k in range(n_parts):
        for i in range(share):
            at = i * (n_rows // share)
            total = got[k, at : at + n_sup]
            for p in range(1, PARTS):
                total = total + got[k, at + p * n_sup : at + (p + 1) * n_sup]
            source = (k % halves) * (n_src // halves) + (k // halves) * share + i
            mine_ref[pl.ds(source, n_sup, stride=n_src), :] = total
    lane = lax.broadcasted_iota(jnp.int32, mine_ref.shape, 1)
    mine = jnp.where(lane >= CHAN * SIDE, mine_ref[...], 0.0)
    mine_ref[...] = mine
    gram_ref[...] = dot_f32(mine, mine, ((1,), (1,)))
    hot = labels_ref[...] == lax.broadcasted_iota(jnp.int32, (n_tgt, ridge_ref.shape[1]), 1)
    hot = jnp.where(hot, 1.0, 0.0)
    hot = jnp.concatenate([hot] * n_sup, axis=0)
    picked_ref[...] = jnp.zeros_like(picked_ref)
    picked_ref[0:n_sup, :] = dot_f32(ridge_ref[...], hot, ((1,), (1,)))
    parts_ref[...] = jnp.zeros_like(parts_ref)

    def keep(k, x):
        for i, part in enumerate(three_parts(x)):
            at = (k * PARTS + i) * n_sup
            parts_ref[at : at + n_sup, :] = part.astype(F32)

    current = 0.0
    for c in range(CHAN):
        s = sup_ref[c]
        keep(c, s)
        current = current + s * s
    current = current * (1.0 / CHAN)
    for depth in range(LAYERS):
        var = BOX_SCALE * flat_box(current) + BIAS_VAR
        inv = lax.rsqrt(1.0 + 2.0 * var)
        keep(CHAN + depth, inv)
        if depth < LAYERS - 1:
            keep(CHAN + LAYERS + depth, (4.0 / math.pi) * inv * inv * lax.rsqrt(1.0 + 4.0 * var))
            current = self_act(var, inv)
    row = lax.broadcasted_iota(jnp.int32, (LANES, LANES), 0)
    lane = lax.broadcasted_iota(jnp.int32, (LANES, LANES), 1)
    same = jnp.where(row == lane, 1.0, 0.0).astype(BF16)
    maps_ref[...] = dot_bf16(parts_ref[...].astype(BF16), same, ((0,), (0,))).astype(BF16)


def fill_spreads(n_sup, n_tgt, tgt_ref, sup_ref):
    row = lax.broadcasted_iota(jnp.int32, (LANES, LANES), 0)
    lane = lax.broadcasted_iota(jnp.int32, (LANES, LANES), 1)
    own = row % n_tgt == lane % n_tgt
    for c in range(CHAN):
        tgt_ref[c] = jnp.where((row // n_tgt == c) & own, 1.0, 0.0).astype(BF16)
    own = row % n_sup == lane // n_tgt
    for k in range(sup_ref.shape[0]):
        sup_ref[k] = jnp.where((row // (PARTS * n_sup) == k) & own, 1.0, 0.0).astype(BF16)


def target_map(pix_ref, tgt_ref, c, b):
    pix = pix_ref[rows_of(b)].reshape(STEP_PIX, LANES)
    return as_map(dot_bf16(pix, tgt_ref[c], ((1,), (0,))))


def support_map(maps_ref, sup_ref, k, b):
    return as_map(dot_bf16(maps_ref[pixels_of(b), :], sup_ref[k], ((1,), (0,))))


QUARTERS = 4
QUARTER_ROWS = SIDE // QUARTERS
PER_QUARTER = QUARTER_ROWS // STEP_ROWS


def lane_block(shape):
    return lax.broadcasted_iota(jnp.int32, shape, len(shape) - 1) // (LANES // QUARTERS)


def put_edges(ref, first, final):
    width = LANES // QUARTERS
    block = lane_block(first.shape)
    ref[0] = jnp.where(block > 0, pltpu.roll(final, width, 2), 0.0)
    ref[QUARTER_ROWS + 1] = jnp.where(block < QUARTERS - 1, pltpu.roll(first, LANES - width, 2), 0.0)


def first_maps(pix_ref, maps_ref, tgt_ref, sup_ref, self_a, self_b, inv_ref, pair_ref):
    def one(b):
        own = pair = 0.0
        for c in range(CHAN):
            t = target_map(pix_ref, tgt_ref, c, b)
            own = own + t * t
            pair = pair + t * support_map(maps_ref, sup_ref, c, b)
        put(pair_ref, b, pair * (1.0 / CHAN))
        at = pl.ds((b % PER_QUARTER) * STEP_ROWS + 1, STEP_ROWS)
        self_a[at] = jnp.where(lane_block(own.shape) == b // PER_QUARTER, own * (1.0 / CHAN), self_a[at])

    steps(one)
    put_edges(self_a, self_a[1], self_a[QUARTER_ROWS])
    for depth in range(LAYERS):
        now, later = (self_a, self_b) if depth % 2 == 0 else (self_b, self_a)
        for part in range(PER_QUARTER):
            var = BOX_SCALE * box(now, part * STEP_ROWS, STEP_ROWS) + BIAS_VAR
            inv = lax.rsqrt(1.0 + 2.0 * var)
            inv_ref[depth, part] = inv
            if depth < LAYERS - 1:
                value = self_act(var, inv)
                later[part * STEP_ROWS + 1 : (part + 1) * STEP_ROWS + 1] = value
        if depth < LAYERS - 1:
            put_edges(later, later[1], later[QUARTER_ROWS])


def target_inv(inv_ref, depth, b):
    x = inv_ref[depth, b % PER_QUARTER]
    x = jnp.where(lane_block(x.shape) == b // PER_QUARTER, x, 0.0)
    x = x + pltpu.roll(x, LANES // 2, 3)
    return x + pltpu.roll(x, LANES // 4, 3)


def forward_body(
    n_sup, pix_ref, maps_ref, gram_ref, out_ref, tgt_ref, sup_ref, self_a, self_b, inv_ref, pair_a, pair_b, acc_ref
):
    n_tgt = LANES // n_sup
    for ref in (self_a, self_b, pair_a, pair_b):
        ref[...] = jnp.zeros_like(ref)
    fill_spreads(n_sup, n_tgt, tgt_ref, sup_ref)
    first_maps(pix_ref, maps_ref, tgt_ref, sup_ref, self_a, self_b, inv_ref, pair_a)
    acc_ref[...] = jnp.zeros_like(acc_ref)
    for depth in range(LAYERS):
        now, later = (pair_a, pair_b) if depth % 2 == 0 else (pair_b, pair_a)

        def one(b, depth=depth, now=now, later=later):
            twice = (2.0 * BOX_SCALE) * step_box(now, b) + 2.0 * BIAS_VAR
            both = target_inv(inv_ref, depth, b) * support_map(maps_ref, sup_ref, CHAN + depth, b)
            value = act_of(twice * both)[0]
            if depth < LAYERS - 1:
                put(later, b, value)
            else:
                acc_ref[...] += jnp.sum(value, axis=(0, 1))

        steps(one)
    value = jnp.sum(acc_ref[...], axis=0, keepdims=True) * (1.0 / PIX)
    n_dst = out_ref.shape[0]
    for j in range(n_sup):
        out_ref[:, j, :] = gram_ref[j * n_dst : (j + 1) * n_dst, :]
    for k in range(n_sup, out_ref.shape[1]):
        out_ref[:, k, :] = jnp.broadcast_to(value, (n_dst, LANES))


def backward_body(
    n_sup,
    pix_ref,
    maps_ref,
    high_ref,
    low_ref,
    tgt_ref,
    sup_ref,
    self_a,
    self_b,
    inv_ref,
    pair_a,
    pair_b,
    grad_a,
    grad_b,
    dcov_ref,
    dvar_ref,
):
    n_tgt = LANES // n_sup
    for ref in (self_a, self_b, pair_a, pair_b, grad_a, grad_b):
        ref[...] = jnp.zeros_like(ref)
    fill_spreads(n_sup, n_tgt, tgt_ref, sup_ref)
    first_maps(pix_ref, maps_ref, tgt_ref, sup_ref, self_a, self_b, inv_ref, pair_a)
    last = LAYERS - 1
    for depth in range(LAYERS):
        now, later = (pair_a, pair_b) if depth % 2 == 0 else (pair_b, pair_a)

        def one(b, depth=depth, now=now, later=later):
            twice = (2.0 * BOX_SCALE) * step_box(now, b) + 2.0 * BIAS_VAR
            s_inv = support_map(maps_ref, sup_ref, CHAN + depth, b)
            both = target_inv(inv_ref, depth, b) * s_inv
            x = twice * both
            if depth < last:
                value, a, left = act_of(x)
                put(later, b, value)
            else:
                a = jnp.abs(x)
                left = lax.rsqrt(1.0 - a)
            slope = (2.0 / math.pi) * left * lax.rsqrt(1.0 + a)
            d_cov = 2.0 * both * slope
            d_var = -(slope * x) * (s_inv * s_inv)
            if depth < last:
                dcov_ref[depth, rows_of(b)] = d_cov
                dvar_ref[depth, rows_of(b)] = d_var
            else:
                put(later, b, d_cov * (1.0 / PIX))
                put(grad_a, b, d_var * (1.0 / PIX))

        steps(one)
    for depth in range(last - 1, -1, -1):
        now, later = (pair_a, pair_b) if depth % 2 == 0 else (pair_b, pair_a)
        own_now, own_later = (grad_a, grad_b) if depth % 2 == 0 else (grad_b, grad_a)

        def one(b, depth=depth, now=now, later=later, own_now=own_now, own_later=own_later):
            g_pair = BOX_SCALE * step_box(now, b)
            g_self = BOX_SCALE * step_box(own_now, b)
            slope = support_map(maps_ref, sup_ref, CHAN + LAYERS + depth, b)
            put(later, b, g_pair * dcov_ref[depth, rows_of(b)])
            put(own_later, b, g_self * slope + g_pair * dvar_ref[depth, rows_of(b)])

        steps(one)

    def finish(b):
        g_pair = (BOX_SCALE / CHAN) * step_box(pair_b, b)
        for c in range(CHAN + 1):
            g = g_pair * target_map(pix_ref, tgt_ref, c, b) if c < CHAN else BOX_SCALE * step_box(grad_b, b)
            g = g.reshape(STEP_PIX, LANES)
            high = g.astype(BF16)
            at = pl.ds(c * PIX + b * STEP_PIX, STEP_PIX)
            high_ref[at, :] = high
            low_ref[at, :] = (g - high.astype(F32)).astype(BF16)

    steps(finish)


def weigh_body(scale, n_tgt, got_ref, high_ref, low_ref, picked_ref, sup_ref, out_ref):
    n_src = got_ref.shape[0]
    n_sup = sup_ref.shape[1]
    rows = got_ref.shape[1]
    gram = jnp.sum(got_ref[...], axis=0)
    values = got_ref[:, n_sup, :]
    lane = lax.broadcasted_iota(jnp.int32, (n_src, LANES), 1)
    big = jnp.concatenate([jnp.where(lane // n_tgt == j, values, 0.0) for j in range(n_sup)], axis=0)
    part = dot_f32(gram, big, ((1,), (0,)))
    part = part + pltpu.roll(part, 64, 1)
    part = part + pltpu.roll(part, 32, 1)
    row = lax.broadcasted_iota(jnp.int32, (rows, LANES), 0)
    lane = lax.broadcasted_iota(jnp.int32, (rows, LANES), 1)
    weight = jnp.where(lane // n_tgt == row, scale * (part - picked_ref[...]), 0.0)
    w_high = weight.astype(BF16)
    w_low = (weight - w_high.astype(F32)).astype(BF16)
    zero = jnp.zeros_like(w_high)
    first = jnp.concatenate([w_high, w_low], axis=0)
    second = jnp.concatenate([w_high, zero], axis=0)
    sums = []
    for c in range(CHAN + 1):
        at = slice(c * PIX, (c + 1) * PIX)
        one = dot_bf16(first, high_ref[at, :], ((1,), (1,)))
        two = dot_bf16(second, low_ref[at, :], ((1,), (1,)))
        sums.append((one[:rows] + one[rows:] + two[:rows])[:n_sup])
    per = PIX // LANES
    for c in range(CHAN):
        grad = sums[c] + (2.0 / CHAN) * sup_ref[c] * sums[CHAN]
        for k in range(per):
            out_ref[pl.ds(c * per + k, n_sup, stride=CHAN * per), :] = grad[:, k * LANES : (k + 1) * LANES]


def residual_body(n_sup, start_ref, got_ref, mine_ref, labels_ref, out_ref):
    n_src = got_ref.shape[0]
    n_tgt, classes = out_ref.shape
    values = got_ref[:, n_sup, :]
    total = jnp.zeros((n_tgt, LANES), F32)
    for j in range(n_sup):
        one = dot_f32(values, mine_ref[j * n_src : (j + 1) * n_src, :], ((0,), (0,)))
        total = total + one[j * n_tgt : (j + 1) * n_tgt, :]
    predicted = total[:, CHAN * SIDE :]
    ids = start_ref[0] + lax.broadcasted_iota(jnp.int32, (n_tgt, classes), 1)
    out_ref[...] = predicted - jnp.where(labels_ref[...] == ids, 1.0, 0.0)


def pair_sum_body(a_ref, b_ref, out_ref):
    total = a_ref[...] + b_ref[...]
    for k in range(out_ref.shape[0]):
        out_ref[k] = total


def last_sum_body(parts_ref, out_ref):
    total = parts_ref[0]
    for k in range(1, parts_ref.shape[0]):
        total = total + parts_ref[k]
    n_sup = out_ref.shape[1]
    per = PIX // LANES
    for j in range(n_sup):
        for c in range(CHAN):
            for k in range(per):
                row = (j * CHAN + c) * per + k
                out_ref[c, j : j + 1, k * LANES : (k + 1) * LANES] = total[row : row + 1, :]


def maps(rows):
    return pltpu.VMEM((rows, TILES, SUB, LANES), F32)


def map_scratch(n_maps):
    return [
        pltpu.VMEM((CHAN, LANES, LANES), BF16),
        pltpu.VMEM((n_maps, LANES, LANES), BF16),
        maps(QUARTER_ROWS + 2),
        maps(QUARTER_ROWS + 2),
        pltpu.VMEM((LAYERS, PER_QUARTER, STEP_ROWS, TILES, SUB, LANES), F32),
        maps(SIDE + 2),
        maps(SIDE + 2),
    ]


def local(image_pool, target_index, labels, support, ridge_coef):
    n_chip, n_core, n_half, n_flat = (lax.axis_size(k) for k in ("chip", "core", "zh", "xy"))
    n_grp, n_sup_dev = n_chip * n_core, n_half * n_flat
    pool_rows = image_pool.shape[0]
    n_sup = support.shape[0]
    n_tgt = labels.shape[0]
    classes = ridge_coef.shape[1] // n_sup_dev
    group = lax.axis_index("chip") * n_core + lax.axis_index("core")
    half = lax.axis_index("zh")
    at = jnp.stack([(group * n_half + half) * (n_flat * pool_rows), group]).astype(jnp.int32)
    start = ((half * n_flat + lax.axis_index("xy")) * classes)[None].astype(jnp.int32)
    label_col = labels[:, None]
    index_col = target_index[:, None]

    packed = call(
        pack_body,
        jax.ShapeDtypeStruct((n_flat, n_half, pool_rows, LANES), BF16),
        2,
        scratch=[pltpu.VMEM((pool_rows, PIX), F32)],
        name="pack_pool",
    )(image_pool, ridge_coef)
    rows = lax.all_to_all(packed, "xy", 0, 0, tiled=True)
    chosen = call(
        select_body,
        jax.ShapeDtypeStruct((n_grp * n_half, n_half, n_tgt, LANES), BF16),
        3,
        smem=(0,),
        name="select_targets",
    )(at, index_col, rows)
    got = lax.all_to_all(chosen, ("chip", "core", "zh"), 0, 0, tiled=True)
    by_channel = jnp.swapaxes(support, 0, 1)
    n_maps = CHAN + 2 * LAYERS - 1
    s_maps, mine, gram, picked = call(
        side_body,
        [
            jax.ShapeDtypeStruct((PIX, LANES), BF16),
            jax.ShapeDtypeStruct((n_sup * n_sup_dev, LANES), F32),
            jax.ShapeDtypeStruct((n_sup * n_sup_dev, n_sup * n_sup_dev), F32),
            jax.ShapeDtypeStruct((SUB, LANES), F32),
        ],
        5,
        scratch=[pltpu.VMEM((LANES, PIX), F32)],
        smem=(0,),
        flops=10**8,
        name="support_maps",
    )(half[None].astype(jnp.int32), by_channel, ridge_coef, label_col, got)
    merged = call(
        merge_body, jax.ShapeDtypeStruct((n_flat, n_half, SIDE, LANES), BF16), 1, name="merge_targets"
    )(got)
    pixels = lax.all_to_all(merged, "xy", 0, 0, tiled=True).reshape(SIDE, SIDE, LANES)
    sent = call(
        functools.partial(forward_body, n_sup),
        jax.ShapeDtypeStruct((n_sup_dev, SUB, LANES), F32),
        3,
        scratch=[*map_scratch(CHAN + LAYERS), pltpu.VMEM((SUB, LANES), F32)],
        flops=10**8,
        name="forward_maps",
        vmem=12,
    )(pixels, s_maps, gram)
    arrived = lax.all_to_all(sent, ("zh", "xy"), 0, 0, tiled=True)
    layer_maps = pltpu.VMEM((LAYERS - 1, SIDE, TILES, SUB, LANES), F32)
    flat = (CHAN + 1) * PIX
    high, low = call(
        functools.partial(backward_body, n_sup),
        [jax.ShapeDtypeStruct((flat, LANES), BF16)] * 2,
        2,
        scratch=[*map_scratch(n_maps), maps(SIDE + 2), maps(SIDE + 2), layer_maps, layer_maps],
        flops=10**10,
        name="backward_maps",
        vmem=20,
    )(pixels, s_maps)
    loss_scale = float(PIX) / n_tgt
    wide = n_sup * CHAN * PIX // LANES
    grad = call(
        functools.partial(weigh_body, loss_scale, n_tgt),
        jax.ShapeDtypeStruct((wide, LANES), F32),
        5,
        name="weigh_gradient",
        vmem=8,
    )(arrived, high, low, picked, by_channel)
    other = lax.ppermute(grad, "core", [(k, (k + 1) % n_core) for k in range(n_core)])
    summed = call(pair_sum_body, jax.ShapeDtypeStruct((n_chip, wide, LANES), F32), 2, name="sum_cores")(grad, other)
    shares = lax.all_to_all(summed, "chip", 0, 0, tiled=True)
    residual = call(
        functools.partial(residual_body, n_sup),
        jax.ShapeDtypeStruct((n_tgt, classes), F32),
        4,
        smem=(0,),
        flops=10**7,
        name="residual",
    )(start, arrived, mine, label_col)
    total = call(last_sum_body, jax.ShapeDtypeStruct(by_channel.shape, F32), 1, name="sum_chips")(shares)
    return (residual, jnp.swapaxes(total, 0, 1))


def solution(mesh):
    n_tgt, n_sup = mesh.devices.shape
    parts = Mesh(mesh.devices.reshape(n_tgt // 2, 2, 2, n_sup // 2), ("chip", "core", "zh", "xy"))
    tgt, sup = ("chip", "core"), ("zh", "xy")
    in_specs = (P((*tgt, *sup), None), P(), P(tgt), P(sup, None, None), P(sup, None))
    out_specs = (P(tgt, sup), P(sup, None, None))
    return jax.shard_map(local, mesh=parts, in_specs=in_specs, out_specs=out_specs, check_vma=False)
```

```python
import functools
import math

import jax
import jax.numpy as jnp
from jax import lax
from jax.experimental import pallas as pl
from jax.experimental.pallas import tpu as pltpu
from jax.sharding import Mesh, PartitionSpec as P

SIDE = 32
CHAN = 3
LAYERS = 4
PIX = SIDE * SIDE
SUB = 8
LANES = 128
TILES = SIDE // SUB
STEP_ROWS = 8
STEP_PIX = STEP_ROWS * SIDE
PARTS = 3

WEIGHT_VAR = 2.0
BIAS_VAR = 0.1
BOX_SCALE = WEIGHT_VAR / 9.0

F32 = jnp.float32
BF16 = jnp.bfloat16
VMEM = pl.BlockSpec(memory_space=pltpu.VMEM)
SMEM = pl.BlockSpec(memory_space=pltpu.SMEM)

ASIN_Q = [
    c * 2.0 / math.pi
    for c in (
        1.5707963050,
        -0.2145988016,
        0.0889789874,
        -0.0501743046,
        0.0308918810,
        -0.0170881256,
        0.0066700901,
        -0.0012624911,
    )
]


def call(body, outs, n_in, scratch=(), smem=(), flops=0, name=None, vmem=4):
    specs = [SMEM if k in smem else VMEM for k in range(n_in)]
    many = isinstance(outs, (list, tuple))
    return pl.pallas_call(
        body,
        out_shape=outs,
        in_specs=specs,
        out_specs=[VMEM] * len(outs) if many else VMEM,
        scratch_shapes=list(scratch),
        compiler_params=pltpu.CompilerParams(vmem_limit_bytes=vmem * 2**20),
        cost_estimate=pl.CostEstimate(flops=flops, bytes_accessed=1 << 20, transcendentals=0),
        name=name,
    )


def three_parts(x):
    high = x.astype(BF16)
    rest = x - high.astype(F32)
    mid = rest.astype(BF16)
    low = (rest - mid.astype(F32)).astype(BF16)
    return high, mid, low


def dot_f32(a, b, dims):
    return lax.dot_general(a, b, (dims, ((), ())), preferred_element_type=F32, precision=lax.Precision.HIGHEST)


def dot_bf16(a, b, dims):
    return lax.dot_general(a, b, (dims, ((), ())), preferred_element_type=F32)


def pack_body(pool_ref, ridge_ref, out_ref, parts_ref):
    n_sup = ridge_ref.shape[0]
    halves = out_ref.shape[1]
    parts_ref[...] = jnp.zeros_like(parts_ref)
    for k, part in enumerate(three_parts(ridge_ref[...])):
        parts_ref[k * n_sup : (k + 1) * n_sup, :] = part.astype(F32)
    for tile in range(PIX // LANES):
        at = tile * LANES
        pieces = [pool_ref[:, c * PIX + at : c * PIX + at + LANES] for c in range(CHAN)]
        for r in range(LANES // SIDE):
            cut = [p[:, r * SIDE : (r + 1) * SIDE] for p in pieces]
            image_row = tile * (LANES // SIDE) + r
            owner, half = image_row // halves, image_row % halves
            first = (half * (SIDE // halves) + owner) * SIDE
            cut.append(parts_ref[:, first : first + SIDE].astype(BF16))
            out_ref[owner, half] = jnp.concatenate(cut, axis=1)


def select_body(at_ref, index_ref, rows_ref, keep_ref, send_ref):
    n_src, halves, rows, _ = rows_ref.shape
    n_chip, _, _, n_tgt, _ = keep_ref.shape
    total = n_src * rows
    wanted = index_ref[...] - at_ref[0]
    ids = lax.broadcasted_iota(jnp.int32, (wanted.shape[0], total), 1)
    pick = jnp.where(ids == wanted, 1.0, 0.0).astype(BF16)
    lane = lax.broadcasted_iota(jnp.int32, (n_tgt, LANES), 1)
    pixel = lane < CHAN * SIDE
    low_core = at_ref[2] == 0
    share = n_src // n_chip // halves
    ridge = [[None] * halves for _ in range(halves)]
    for half in range(halves):
        for part in range(halves):
            first = (at_ref[1] * halves + part) * share
            block = rows_ref[pl.ds(first, share), half, 0 : n_tgt // share]
            ridge[half][part] = block.reshape(n_tgt, LANES).astype(F32)
    for part in range(halves):
        data = rows_ref[:, part].reshape(total, LANES)
        got = dot_bf16(pick, data, ((1,), (0,)))
        for chip in range(n_chip):
            low = got[2 * chip * n_tgt : (2 * chip + 1) * n_tgt]
            high = got[(2 * chip + 1) * n_tgt : (2 * chip + 2) * n_tgt]
            mine = jnp.where(low_core, low, high)
            send_ref[chip, part] = jnp.where(pixel, jnp.where(low_core, high, low), 0.0).astype(BF16)
            for half in range(halves):
                keep_ref[chip, half, part] = jnp.where(pixel, mine, ridge[half][part]).astype(BF16)


def add_body(keep_ref, other_ref, out_ref):
    n_chip, halves = keep_ref.shape[:2]
    for chip in range(n_chip):
        other = other_ref[chip].astype(F32)
        for half in range(halves):
            out_ref[chip * halves + half] = (keep_ref[chip, half].astype(F32) + other).astype(BF16)


def merge_body(parts_ref, out_ref):
    n_dst, halves, _, _ = out_ref.shape
    for half in range(halves):
        total = parts_ref[0, half].astype(F32)
        for k in range(1, parts_ref.shape[0]):
            total = total + parts_ref[k, half].astype(F32)
        turned = total.T
        n_tgt = turned.shape[1]
        cut = [turned[c * SIDE : (c + 1) * SIDE, :] for c in range(CHAN)]
        cut.append(jnp.zeros((SIDE, LANES - CHAN * n_tgt), F32))
        message = jnp.concatenate(cut, axis=1).astype(BF16)
        for k in range(n_dst):
            out_ref[k, half] = message


def steps(fn):
    for b in range(SIDE // STEP_ROWS):
        fn(b)


def rows_of(b):
    return pl.ds(b * STEP_ROWS, STEP_ROWS)


def pixels_of(b):
    return pl.ds(b * STEP_PIX, STEP_PIX)


def as_map(x):
    return x.reshape(x.shape[0] // SIDE, TILES, SUB, LANES)


def box(ref, row, n):
    x = ref[pl.ds(row, n + 2)]
    x = x[0:n] + x[1 : n + 1] + x[2 : n + 2]
    sub = lax.broadcasted_iota(jnp.int32, x.shape, 2)
    zero = jnp.zeros_like(x[:, 0:1])
    left = pltpu.roll(x, 1, 2)
    right = pltpu.roll(x, SUB - 1, 2)
    left = jnp.where(sub == 0, jnp.concatenate([zero, left[:, : TILES - 1]], axis=1), left)
    right = jnp.where(sub == SUB - 1, jnp.concatenate([right[:, 1:], zero], axis=1), right)
    return x + left + right


def step_box(ref, b):
    return box(ref, b * STEP_ROWS, STEP_ROWS)


def put(ref, b, x):
    ref[pl.ds(b * STEP_ROWS + 1, STEP_ROWS)] = x


def q_poly(a):
    acc = ASIN_Q[-1] * a + ASIN_Q[-2]
    for c in ASIN_Q[-3::-1]:
        acc = acc * a + c
    return acc


def act_of(x):
    a = jnp.abs(x)
    left = 1.0 - a
    inv = lax.rsqrt(left)
    value = 1.0 - left * inv * q_poly(a)
    return jnp.where(x < 0.0, -value, value), a, inv


def self_act(var, inv):
    x = 2.0 * var * inv * inv
    left = 1.0 - x
    return 1.0 - left * lax.rsqrt(left) * q_poly(x)


def flat_box(x):
    at = lax.broadcasted_iota(jnp.int32, x.shape, 1)
    col = at % SIDE
    left = jnp.where(col > 0, pltpu.roll(x, 1, 1), 0.0)
    right = jnp.where(col < SIDE - 1, pltpu.roll(x, PIX - 1, 1), 0.0)
    x = x + left + right
    above = jnp.where(at >= SIDE, pltpu.roll(x, SIDE, 1), 0.0)
    below = jnp.where(at < PIX - SIDE, pltpu.roll(x, PIX - SIDE, 1), 0.0)
    return x + above + below


def side_body(sup_ref, ridge_ref, labels_ref, got_ref, maps_ref, mine_ref, gram_ref, picked_ref, parts_ref):
    n_sup = sup_ref.shape[1]
    n_tgt = labels_ref.shape[0]
    n_parts, halves, n_rows, _ = got_ref.shape
    n_src = mine_ref.shape[0] // n_sup
    share = n_src // n_parts // halves
    for k in range(n_parts):
        for part in range(halves):
            got = got_ref[k, part].astype(F32)
            for i in range(share):
                at = i * (n_rows // share)
                total = got[at : at + n_sup]
                for p in range(1, PARTS):
                    total = total + got[at + p * n_sup : at + (p + 1) * n_sup]
                source = (k % halves) * (n_src // halves) + ((k // halves) * halves + part) * share + i
                mine_ref[pl.ds(source, n_sup, stride=n_src), :] = total
    lane = lax.broadcasted_iota(jnp.int32, mine_ref.shape, 1)
    mine = jnp.where(lane >= CHAN * SIDE, mine_ref[...], 0.0)
    mine_ref[...] = mine
    gram_ref[...] = dot_f32(mine, mine, ((1,), (1,)))
    hot = labels_ref[...] == lax.broadcasted_iota(jnp.int32, (n_tgt, ridge_ref.shape[1]), 1)
    hot = jnp.where(hot, 1.0, 0.0)
    hot = jnp.concatenate([hot] * n_sup, axis=0)
    picked_ref[...] = jnp.zeros_like(picked_ref)
    picked_ref[0:n_sup, :] = dot_f32(ridge_ref[...], hot, ((1,), (1,)))
    parts_ref[...] = jnp.zeros_like(parts_ref)

    def keep(k, x):
        for i, part in enumerate(three_parts(x)):
            at = (k * PARTS + i) * n_sup
            parts_ref[at : at + n_sup, :] = part.astype(F32)

    current = 0.0
    for c in range(CHAN):
        s = sup_ref[c]
        keep(c, s)
        current = current + s * s
    current = current * (1.0 / CHAN)
    for depth in range(LAYERS):
        var = BOX_SCALE * flat_box(current) + BIAS_VAR
        inv = lax.rsqrt(1.0 + 2.0 * var)
        keep(CHAN + depth, inv)
        if depth < LAYERS - 1:
            keep(CHAN + LAYERS + depth, (4.0 / math.pi) * inv * inv * lax.rsqrt(1.0 + 4.0 * var))
            current = self_act(var, inv)
    row = lax.broadcasted_iota(jnp.int32, (LANES, LANES), 0)
    lane = lax.broadcasted_iota(jnp.int32, (LANES, LANES), 1)
    same = jnp.where(row == lane, 1.0, 0.0).astype(BF16)
    maps_ref[...] = dot_bf16(parts_ref[...].astype(BF16), same, ((0,), (0,))).astype(BF16)


def fill_spreads(n_sup, n_tgt, tgt_ref, sup_ref):
    row = lax.broadcasted_iota(jnp.int32, (LANES, LANES), 0)
    lane = lax.broadcasted_iota(jnp.int32, (LANES, LANES), 1)
    own = row % n_tgt == lane % n_tgt
    for c in range(CHAN):
        tgt_ref[c] = jnp.where((row // n_tgt == c) & own, 1.0, 0.0).astype(BF16)
    own = row % n_sup == lane // n_tgt
    for k in range(sup_ref.shape[0]):
        sup_ref[k] = jnp.where((row // (PARTS * n_sup) == k) & own, 1.0, 0.0).astype(BF16)


def target_map(pix_ref, tgt_ref, c, b):
    pix = pix_ref[rows_of(b)].reshape(STEP_PIX, LANES)
    return as_map(dot_bf16(pix, tgt_ref[c], ((1,), (0,))))


def support_map(maps_ref, sup_ref, k, b):
    return as_map(dot_bf16(maps_ref[pixels_of(b), :], sup_ref[k], ((1,), (0,))))


QUARTERS = 4
QUARTER_ROWS = SIDE // QUARTERS
PER_QUARTER = QUARTER_ROWS // STEP_ROWS


def lane_block(shape):
    return lax.broadcasted_iota(jnp.int32, shape, len(shape) - 1) // (LANES // QUARTERS)


def put_edges(ref, first, final):
    width = LANES // QUARTERS
    block = lane_block(first.shape)
    ref[0] = jnp.where(block > 0, pltpu.roll(final, width, 2), 0.0)
    ref[QUARTER_ROWS + 1] = jnp.where(block < QUARTERS - 1, pltpu.roll(first, LANES - width, 2), 0.0)


def first_maps(pix_ref, maps_ref, tgt_ref, sup_ref, self_a, self_b, inv_ref, pair_ref):
    def one(b):
        own = pair = 0.0
        for c in range(CHAN):
            t = target_map(pix_ref, tgt_ref, c, b)
            own = own + t * t
            pair = pair + t * support_map(maps_ref, sup_ref, c, b)
        put(pair_ref, b, pair * (1.0 / CHAN))
        at = pl.ds((b % PER_QUARTER) * STEP_ROWS + 1, STEP_ROWS)
        self_a[at] = jnp.where(lane_block(own.shape) == b // PER_QUARTER, own * (1.0 / CHAN), self_a[at])

    steps(one)
    put_edges(self_a, self_a[1], self_a[QUARTER_ROWS])
    for depth in range(LAYERS):
        now, later = (self_a, self_b) if depth % 2 == 0 else (self_b, self_a)
        for part in range(PER_QUARTER):
            var = BOX_SCALE * box(now, part * STEP_ROWS, STEP_ROWS) + BIAS_VAR
            inv = lax.rsqrt(1.0 + 2.0 * var)
            inv_ref[depth, part] = inv
            if depth < LAYERS - 1:
                value = self_act(var, inv)
                later[part * STEP_ROWS + 1 : (part + 1) * STEP_ROWS + 1] = value
        if depth < LAYERS - 1:
            put_edges(later, later[1], later[QUARTER_ROWS])


def target_inv(inv_ref, depth, b):
    x = inv_ref[depth, b % PER_QUARTER]
    x = jnp.where(lane_block(x.shape) == b // PER_QUARTER, x, 0.0)
    x = x + pltpu.roll(x, LANES // 2, 3)
    return x + pltpu.roll(x, LANES // 4, 3)


def forward_body(
    n_sup, pix_ref, maps_ref, gram_ref, out_ref, tgt_ref, sup_ref, self_a, self_b, inv_ref, pair_a, pair_b, acc_ref
):
    n_tgt = LANES // n_sup
    for ref in (self_a, self_b, pair_a, pair_b):
        ref[...] = jnp.zeros_like(ref)
    fill_spreads(n_sup, n_tgt, tgt_ref, sup_ref)
    first_maps(pix_ref, maps_ref, tgt_ref, sup_ref, self_a, self_b, inv_ref, pair_a)
    acc_ref[...] = jnp.zeros_like(acc_ref)
    for depth in range(LAYERS):
        now, later = (pair_a, pair_b) if depth % 2 == 0 else (pair_b, pair_a)

        def one(b, depth=depth, now=now, later=later):
            twice = (2.0 * BOX_SCALE) * step_box(now, b) + 2.0 * BIAS_VAR
            both = target_inv(inv_ref, depth, b) * support_map(maps_ref, sup_ref, CHAN + depth, b)
            value = act_of(twice * both)[0]
            if depth < LAYERS - 1:
                put(later, b, value)
            else:
                acc_ref[...] += jnp.sum(value, axis=(0, 1))

        steps(one)
    value = jnp.sum(acc_ref[...], axis=0, keepdims=True) * (1.0 / PIX)
    n_dst = out_ref.shape[0]
    for j in range(n_sup):
        out_ref[:, j, :] = gram_ref[j * n_dst : (j + 1) * n_dst, :]
    for k in range(n_sup, out_ref.shape[1]):
        out_ref[:, k, :] = jnp.broadcast_to(value, (n_dst, LANES))


def backward_body(
    n_sup,
    pix_ref,
    maps_ref,
    high_ref,
    low_ref,
    tgt_ref,
    sup_ref,
    self_a,
    self_b,
    inv_ref,
    pair_a,
    pair_b,
    grad_a,
    grad_b,
    dcov_ref,
    dvar_ref,
):
    n_tgt = LANES // n_sup
    for ref in (self_a, self_b, pair_a, pair_b, grad_a, grad_b):
        ref[...] = jnp.zeros_like(ref)
    fill_spreads(n_sup, n_tgt, tgt_ref, sup_ref)
    first_maps(pix_ref, maps_ref, tgt_ref, sup_ref, self_a, self_b, inv_ref, pair_a)
    last = LAYERS - 1
    for depth in range(LAYERS):
        now, later = (pair_a, pair_b) if depth % 2 == 0 else (pair_b, pair_a)

        def one(b, depth=depth, now=now, later=later):
            twice = (2.0 * BOX_SCALE) * step_box(now, b) + 2.0 * BIAS_VAR
            s_inv = support_map(maps_ref, sup_ref, CHAN + depth, b)
            both = target_inv(inv_ref, depth, b) * s_inv
            x = twice * both
            if depth < last:
                value, a, left = act_of(x)
                put(later, b, value)
            else:
                a = jnp.abs(x)
                left = lax.rsqrt(1.0 - a)
            slope = (2.0 / math.pi) * left * lax.rsqrt(1.0 + a)
            d_cov = 2.0 * both * slope
            d_var = -(slope * x) * (s_inv * s_inv)
            if depth < last:
                dcov_ref[depth, rows_of(b)] = d_cov
                dvar_ref[depth, rows_of(b)] = d_var
            else:
                put(later, b, d_cov * (1.0 / PIX))
                put(grad_a, b, d_var * (1.0 / PIX))

        steps(one)
    for depth in range(last - 1, -1, -1):
        now, later = (pair_a, pair_b) if depth % 2 == 0 else (pair_b, pair_a)
        own_now, own_later = (grad_a, grad_b) if depth % 2 == 0 else (grad_b, grad_a)

        def one(b, depth=depth, now=now, later=later, own_now=own_now, own_later=own_later):
            g_pair = BOX_SCALE * step_box(now, b)
            g_self = BOX_SCALE * step_box(own_now, b)
            slope = support_map(maps_ref, sup_ref, CHAN + LAYERS + depth, b)
            put(later, b, g_pair * dcov_ref[depth, rows_of(b)])
            put(own_later, b, g_self * slope + g_pair * dvar_ref[depth, rows_of(b)])

        steps(one)

    def finish(b):
        g_pair = (BOX_SCALE / CHAN) * step_box(pair_b, b)
        for c in range(CHAN + 1):
            g = g_pair * target_map(pix_ref, tgt_ref, c, b) if c < CHAN else BOX_SCALE * step_box(grad_b, b)
            g = g.reshape(STEP_PIX, LANES)
            high = g.astype(BF16)
            at = pl.ds(c * PIX + b * STEP_PIX, STEP_PIX)
            high_ref[at, :] = high
            low_ref[at, :] = (g - high.astype(F32)).astype(BF16)

    steps(finish)


def weigh_body(scale, n_tgt, got_ref, high_ref, low_ref, picked_ref, sup_ref, out_ref):
    n_src = got_ref.shape[0]
    n_sup = sup_ref.shape[1]
    rows = got_ref.shape[1]
    gram = jnp.sum(got_ref[...], axis=0)
    values = got_ref[:, n_sup, :]
    lane = lax.broadcasted_iota(jnp.int32, (n_src, LANES), 1)
    big = jnp.concatenate([jnp.where(lane // n_tgt == j, values, 0.0) for j in range(n_sup)], axis=0)
    part = dot_f32(gram, big, ((1,), (0,)))
    part = part + pltpu.roll(part, 64, 1)
    part = part + pltpu.roll(part, 32, 1)
    row = lax.broadcasted_iota(jnp.int32, (rows, LANES), 0)
    lane = lax.broadcasted_iota(jnp.int32, (rows, LANES), 1)
    weight = jnp.where(lane // n_tgt == row, scale * (part - picked_ref[...]), 0.0)
    w_high = weight.astype(BF16)
    w_low = (weight - w_high.astype(F32)).astype(BF16)
    zero = jnp.zeros_like(w_high)
    first = jnp.concatenate([w_high, w_low], axis=0)
    second = jnp.concatenate([w_high, zero], axis=0)
    sums = []
    for c in range(CHAN + 1):
        at = slice(c * PIX, (c + 1) * PIX)
        one = dot_bf16(first, high_ref[at, :], ((1,), (1,)))
        two = dot_bf16(second, low_ref[at, :], ((1,), (1,)))
        sums.append((one[:rows] + one[rows:] + two[:rows])[:n_sup])
    per = PIX // LANES
    for c in range(CHAN):
        grad = sums[c] + (2.0 / CHAN) * sup_ref[c] * sums[CHAN]
        for k in range(per):
            out_ref[pl.ds(c * per + k, n_sup, stride=CHAN * per), :] = grad[:, k * LANES : (k + 1) * LANES]


def residual_body(n_sup, start_ref, got_ref, mine_ref, labels_ref, out_ref):
    n_src = got_ref.shape[0]
    n_tgt, classes = out_ref.shape
    values = got_ref[:, n_sup, :]
    total = jnp.zeros((n_tgt, LANES), F32)
    for j in range(n_sup):
        one = dot_f32(values, mine_ref[j * n_src : (j + 1) * n_src, :], ((0,), (0,)))
        total = total + one[j * n_tgt : (j + 1) * n_tgt, :]
    predicted = total[:, CHAN * SIDE :]
    ids = start_ref[0] + lax.broadcasted_iota(jnp.int32, (n_tgt, classes), 1)
    out_ref[...] = predicted - jnp.where(labels_ref[...] == ids, 1.0, 0.0)


def pair_sum_body(a_ref, b_ref, out_ref):
    total = a_ref[...] + b_ref[...]
    for k in range(out_ref.shape[0]):
        out_ref[k] = total


def last_sum_body(parts_ref, out_ref):
    total = parts_ref[0]
    for k in range(1, parts_ref.shape[0]):
        total = total + parts_ref[k]
    n_sup = out_ref.shape[1]
    per = PIX // LANES
    for j in range(n_sup):
        for c in range(CHAN):
            for k in range(per):
                row = (j * CHAN + c) * per + k
                out_ref[c, j : j + 1, k * LANES : (k + 1) * LANES] = total[row : row + 1, :]


def maps(rows):
    return pltpu.VMEM((rows, TILES, SUB, LANES), F32)


def map_scratch(n_maps):
    return [
        pltpu.VMEM((CHAN, LANES, LANES), BF16),
        pltpu.VMEM((n_maps, LANES, LANES), BF16),
        maps(QUARTER_ROWS + 2),
        maps(QUARTER_ROWS + 2),
        pltpu.VMEM((LAYERS, PER_QUARTER, STEP_ROWS, TILES, SUB, LANES), F32),
        maps(SIDE + 2),
        maps(SIDE + 2),
    ]


def local(image_pool, target_index, labels, support, ridge_coef):
    n_chip, n_core, n_half, n_flat = (lax.axis_size(k) for k in ("chip", "core", "zh", "xy"))
    n_sup_dev = n_half * n_flat
    pool_rows = image_pool.shape[0]
    n_sup = support.shape[0]
    n_tgt = labels.shape[0]
    classes = ridge_coef.shape[1] // n_sup_dev
    chip, core, half = (lax.axis_index(k) for k in ("chip", "core", "zh"))
    first_row = ((chip * n_core + core) * n_half + half) * (n_flat * pool_rows)
    at = jnp.stack([first_row, chip, core]).astype(jnp.int32)
    start = ((half * n_flat + lax.axis_index("xy")) * classes)[None].astype(jnp.int32)
    label_col = labels[:, None]
    index_col = target_index[:, None]

    packed = call(
        pack_body,
        jax.ShapeDtypeStruct((n_flat, n_half, pool_rows, LANES), BF16),
        2,
        scratch=[pltpu.VMEM((pool_rows, PIX), F32)],
        name="pack_pool",
    )(image_pool, ridge_coef)
    rows = lax.all_to_all(packed, "xy", 0, 0, tiled=True)
    keep, send = call(
        select_body,
        [
            jax.ShapeDtypeStruct((n_chip, n_half, n_half, n_tgt, LANES), BF16),
            jax.ShapeDtypeStruct((n_chip, n_half, n_tgt, LANES), BF16),
        ],
        3,
        smem=(0,),
        name="select_targets",
    )(at, index_col, rows)
    swap = [(k, (k + 1) % n_core) for k in range(n_core)]
    other = lax.ppermute(send, "core", swap)
    chosen = call(
        add_body,
        jax.ShapeDtypeStruct((n_chip * n_half, n_half, n_tgt, LANES), BF16),
        2,
        name="add_core_targets",
    )(keep, other)
    got = lax.all_to_all(chosen, ("chip", "zh"), 0, 0, tiled=True)
    by_channel = jnp.swapaxes(support, 0, 1)
    n_maps = CHAN + 2 * LAYERS - 1
    s_maps, mine, gram, picked = call(
        side_body,
        [
            jax.ShapeDtypeStruct((PIX, LANES), BF16),
            jax.ShapeDtypeStruct((n_sup * n_sup_dev, LANES), F32),
            jax.ShapeDtypeStruct((n_sup * n_sup_dev, n_sup * n_sup_dev), F32),
            jax.ShapeDtypeStruct((SUB, LANES), F32),
        ],
        4,
        scratch=[pltpu.VMEM((LANES, PIX), F32)],
        flops=10**8,
        name="support_maps",
    )(by_channel, ridge_coef, label_col, got)
    merged = call(
        merge_body, jax.ShapeDtypeStruct((n_flat, n_half, SIDE, LANES), BF16), 1, name="merge_targets"
    )(got)
    pixels = lax.all_to_all(merged, "xy", 0, 0, tiled=True).reshape(SIDE, SIDE, LANES)
    sent = call(
        functools.partial(forward_body, n_sup),
        jax.ShapeDtypeStruct((n_sup_dev, SUB, LANES), F32),
        3,
        scratch=[*map_scratch(CHAN + LAYERS), pltpu.VMEM((SUB, LANES), F32)],
        flops=10**8,
        name="forward_maps",
        vmem=12,
    )(pixels, s_maps, gram)
    arrived = lax.all_to_all(sent, ("zh", "xy"), 0, 0, tiled=True)
    layer_maps = pltpu.VMEM((LAYERS - 1, SIDE, TILES, SUB, LANES), F32)
    flat = (CHAN + 1) * PIX
    high, low = call(
        functools.partial(backward_body, n_sup),
        [jax.ShapeDtypeStruct((flat, LANES), BF16)] * 2,
        2,
        scratch=[*map_scratch(n_maps), maps(SIDE + 2), maps(SIDE + 2), layer_maps, layer_maps],
        flops=10**10,
        name="backward_maps",
        vmem=20,
    )(pixels, s_maps)
    loss_scale = float(PIX) / n_tgt
    wide = n_sup * CHAN * PIX // LANES
    grad = call(
        functools.partial(weigh_body, loss_scale, n_tgt),
        jax.ShapeDtypeStruct((wide, LANES), F32),
        5,
        name="weigh_gradient",
        vmem=8,
    )(arrived, high, low, picked, by_channel)
    other = lax.ppermute(grad, "core", swap)
    summed = call(pair_sum_body, jax.ShapeDtypeStruct((n_chip, wide, LANES), F32), 2, name="sum_cores")(grad, other)
    shares = lax.all_to_all(summed, "chip", 0, 0, tiled=True)
    residual = call(
        functools.partial(residual_body, n_sup),
        jax.ShapeDtypeStruct((n_tgt, classes), F32),
        4,
        smem=(0,),
        flops=10**7,
        name="residual",
    )(start, arrived, mine, label_col)
    total = call(last_sum_body, jax.ShapeDtypeStruct(by_channel.shape, F32), 1, name="sum_chips")(shares)
    return (residual, jnp.swapaxes(total, 0, 1))


def solution(mesh):
    n_tgt, n_sup = mesh.devices.shape
    parts = Mesh(mesh.devices.reshape(n_tgt // 2, 2, 2, n_sup // 2), ("chip", "core", "zh", "xy"))
    tgt, sup = ("chip", "core"), ("zh", "xy")
    in_specs = (P((*tgt, *sup), None), P(), P(tgt), P(sup, None, None), P(sup, None))
    out_specs = (P(tgt, sup), P(sup, None, None))
    return jax.shard_map(local, mesh=parts, in_specs=in_specs, out_specs=out_specs, check_vma=False)
```

```python
import functools
import math

import jax
import jax.numpy as jnp
from jax import lax
from jax.experimental import pallas as pl
from jax.experimental.pallas import tpu as pltpu
from jax.sharding import Mesh, PartitionSpec as P

SIDE = 32
CHAN = 3
LAYERS = 4
PIX = SIDE * SIDE
SUB = 8
LANES = 128
TILES = SIDE // SUB
STEP_ROWS = 8
STEP_PIX = STEP_ROWS * SIDE
PARTS = 3
PACK_CUTS = 1

WEIGHT_VAR = 2.0
BIAS_VAR = 0.1
BOX_SCALE = WEIGHT_VAR / 9.0

F32 = jnp.float32
BF16 = jnp.bfloat16
VMEM = pl.BlockSpec(memory_space=pltpu.VMEM)
SMEM = pl.BlockSpec(memory_space=pltpu.SMEM)

ASIN_Q = (
    0.9999999439523269,
    -0.13661292782489154,
    0.05655466043182583,
    -0.03131997834776645,
    0.01767426424200143,
    -0.007641460751180656,
    0.0016626264836763138,
)


def call(body, outs, n_in, scratch=(), smem=(), flops=0, name=None, vmem=4):
    specs = [SMEM if k in smem else VMEM for k in range(n_in)]
    many = isinstance(outs, (list, tuple))
    return pl.pallas_call(
        body,
        out_shape=outs,
        in_specs=specs,
        out_specs=[VMEM] * len(outs) if many else VMEM,
        scratch_shapes=list(scratch),
        compiler_params=pltpu.CompilerParams(vmem_limit_bytes=vmem * 2**20),
        cost_estimate=pl.CostEstimate(flops=flops, bytes_accessed=1 << 20, transcendentals=0),
        name=name,
    )


def three_parts(x):
    high = x.astype(BF16)
    rest = x - high.astype(F32)
    mid = rest.astype(BF16)
    low = (rest - mid.astype(F32)).astype(BF16)
    return high, mid, low


def dot_f32(a, b, dims):
    return lax.dot_general(a, b, (dims, ((), ())), preferred_element_type=F32, precision=lax.Precision.HIGHEST)


def dot_bf16(a, b, dims):
    return lax.dot_general(a, b, (dims, ((), ())), preferred_element_type=F32)


def pack_body(pool_ref, ridge_ref, out_ref, pool_here, ridge_here, parts_ref, pool_sems, ridge_sem):
    n_sup = ridge_ref.shape[0]
    halves = out_ref.shape[1]
    width = PIX // PACK_CUTS
    copies = [
        [
            pltpu.make_async_copy(
                pool_ref.at[:, pl.ds(c * PIX + k * width, width)],
                pool_here.at[:, pl.ds(c * PIX + k * width, width)],
                pool_sems.at[k, c],
            )
            for c in range(CHAN)
        ]
        for k in range(PACK_CUTS)
    ]
    ridge_copy = pltpu.make_async_copy(ridge_ref, ridge_here, ridge_sem)
    ridge_copy.start()
    for group in copies:
        for copy in group:
            copy.start()
    parts_ref[...] = jnp.zeros_like(parts_ref)
    ridge_copy.wait()
    for k, part in enumerate(three_parts(ridge_here[...])):
        parts_ref[k * n_sup : (k + 1) * n_sup, :] = part.astype(F32)
    for tile in range(PIX // LANES):
        at = tile * LANES
        if at % width == 0:
            for copy in copies[at // width]:
                copy.wait()
        pieces = [pool_here[:, c * PIX + at : c * PIX + at + LANES] for c in range(CHAN)]
        for r in range(LANES // SIDE):
            cut = [p[:, r * SIDE : (r + 1) * SIDE] for p in pieces]
            image_row = tile * (LANES // SIDE) + r
            owner, half = image_row // halves, image_row % halves
            first = (half * (SIDE // halves) + owner) * SIDE
            cut.append(parts_ref[:, first : first + SIDE].astype(BF16))
            out_ref[owner, half] = jnp.concatenate(cut, axis=1)


def select_body(at_ref, index_ref, rows_ref, keep_ref, send_ref):
    n_src, halves, rows, _ = rows_ref.shape
    n_chip, _, _, n_tgt, _ = keep_ref.shape
    total = n_src * rows
    wanted = index_ref[...] - at_ref[0]
    ids = lax.broadcasted_iota(jnp.int32, (wanted.shape[0], total), 1)
    pick = jnp.where(ids == wanted, 1.0, 0.0).astype(BF16)
    lane = lax.broadcasted_iota(jnp.int32, (n_tgt, LANES), 1)
    pixel = lane < CHAN * SIDE
    low_core = at_ref[2] == 0
    share = n_src // n_chip // halves
    ridge = [[None] * halves for _ in range(halves)]
    for half in range(halves):
        for part in range(halves):
            first = (at_ref[1] * halves + part) * share
            block = rows_ref[pl.ds(first, share), half, 0 : n_tgt // share]
            ridge[half][part] = block.reshape(n_tgt, LANES).astype(F32)
    for part in range(halves):
        data = rows_ref[:, part].reshape(total, LANES)
        got = dot_bf16(pick, data, ((1,), (0,)))
        for chip in range(n_chip):
            low = got[2 * chip * n_tgt : (2 * chip + 1) * n_tgt]
            high = got[(2 * chip + 1) * n_tgt : (2 * chip + 2) * n_tgt]
            mine = jnp.where(low_core, low, high)
            send_ref[chip, part] = jnp.where(pixel, jnp.where(low_core, high, low), 0.0).astype(BF16)
            for half in range(halves):
                keep_ref[chip, half, part] = jnp.where(pixel, mine, ridge[half][part]).astype(BF16)


def add_body(keep_ref, other_ref, out_ref):
    n_chip, halves = keep_ref.shape[:2]
    for chip in range(n_chip):
        other = other_ref[chip].astype(F32)
        for half in range(halves):
            out_ref[chip * halves + half] = (keep_ref[chip, half].astype(F32) + other).astype(BF16)


def merge_body(parts_ref, out_ref):
    n_dst, halves, _, _ = out_ref.shape
    for half in range(halves):
        total = parts_ref[0, half].astype(F32)
        for k in range(1, parts_ref.shape[0]):
            total = total + parts_ref[k, half].astype(F32)
        turned = total.T
        n_tgt = turned.shape[1]
        cut = [turned[c * SIDE : (c + 1) * SIDE, :] for c in range(CHAN)]
        cut.append(jnp.zeros((SIDE, LANES - CHAN * n_tgt), F32))
        message = jnp.concatenate(cut, axis=1).astype(BF16)
        for k in range(n_dst):
            out_ref[k, half] = message


def steps(fn):
    for b in range(SIDE // STEP_ROWS):
        fn(b)


def rows_of(b):
    return pl.ds(b * STEP_ROWS, STEP_ROWS)


def pixels_of(b):
    return pl.ds(b * STEP_PIX, STEP_PIX)


def as_map(x):
    return x.reshape(x.shape[0] // SIDE, TILES, SUB, LANES)


def box(ref, row, n):
    x = ref[pl.ds(row, n + 2)]
    x = x[0:n] + x[1 : n + 1] + x[2 : n + 2]
    sub = lax.broadcasted_iota(jnp.int32, x.shape, 2)
    zero = jnp.zeros_like(x[:, 0:1])
    left = pltpu.roll(x, 1, 2)
    right = pltpu.roll(x, SUB - 1, 2)
    left = jnp.where(sub == 0, jnp.concatenate([zero, left[:, : TILES - 1]], axis=1), left)
    right = jnp.where(sub == SUB - 1, jnp.concatenate([right[:, 1:], zero], axis=1), right)
    return x + left + right


def step_box(ref, b):
    return box(ref, b * STEP_ROWS, STEP_ROWS)


def put(ref, b, x):
    ref[pl.ds(b * STEP_ROWS + 1, STEP_ROWS)] = x


def q_poly(a, scale=1.0):
    acc = (scale * ASIN_Q[-1]) * a + scale * ASIN_Q[-2]
    for c in ASIN_Q[-3::-1]:
        acc = acc * a + scale * c
    return acc


def act_of(x, scale):
    a = jnp.abs(x)
    left = 1.0 - a
    inv = lax.rsqrt(left)
    value = scale - left * inv * q_poly(a, scale)
    return jnp.where(x < 0.0, -value, value), a, inv


def self_act(var, inv, scale=1.0):
    x = 2.0 * var * inv * inv
    left = 1.0 - x
    return scale - left * lax.rsqrt(left) * q_poly(x, scale)


def flat_box(x):
    at = lax.broadcasted_iota(jnp.int32, x.shape, 1)
    col = at % SIDE
    left = jnp.where(col > 0, pltpu.roll(x, 1, 1), 0.0)
    right = jnp.where(col < SIDE - 1, pltpu.roll(x, PIX - 1, 1), 0.0)
    x = x + left + right
    above = jnp.where(at >= SIDE, pltpu.roll(x, SIDE, 1), 0.0)
    below = jnp.where(at < PIX - SIDE, pltpu.roll(x, PIX - SIDE, 1), 0.0)
    return x + above + below


def side_body(sup_ref, ridge_ref, labels_ref, got_ref, maps_ref, mine_ref, gram_ref, picked_ref, parts_ref):
    n_sup = sup_ref.shape[1]
    n_tgt = labels_ref.shape[0]
    n_parts, halves, n_rows, _ = got_ref.shape
    n_src = mine_ref.shape[0] // n_sup
    share = n_src // n_parts // halves
    for k in range(n_parts):
        for part in range(halves):
            got = got_ref[k, part].astype(F32)
            for i in range(share):
                at = i * (n_rows // share)
                total = got[at : at + n_sup]
                for p in range(1, PARTS):
                    total = total + got[at + p * n_sup : at + (p + 1) * n_sup]
                source = (k % halves) * (n_src // halves) + ((k // halves) * halves + part) * share + i
                mine_ref[pl.ds(source, n_sup, stride=n_src), :] = total
    lane = lax.broadcasted_iota(jnp.int32, mine_ref.shape, 1)
    mine = jnp.where(lane >= CHAN * SIDE, mine_ref[...], 0.0)
    mine_ref[...] = mine
    gram_ref[...] = dot_f32(mine, mine, ((1,), (1,)))
    hot = labels_ref[...] == lax.broadcasted_iota(jnp.int32, (n_tgt, ridge_ref.shape[1]), 1)
    hot = jnp.where(hot, 1.0, 0.0)
    hot = jnp.concatenate([hot] * n_sup, axis=0)
    picked_ref[...] = jnp.zeros_like(picked_ref)
    picked_ref[0:n_sup, :] = dot_f32(ridge_ref[...], hot, ((1,), (1,)))
    parts_ref[...] = jnp.zeros_like(parts_ref)

    def keep(k, x):
        for i, part in enumerate(three_parts(x)):
            at = (k * PARTS + i) * n_sup
            parts_ref[at : at + n_sup, :] = part.astype(F32)

    current = 0.0
    for c in range(CHAN):
        s = sup_ref[c]
        keep(c, s)
        current = current + s * s
    current = current * (1.0 / CHAN)
    for depth in range(LAYERS):
        var = BOX_SCALE * flat_box(current) + BIAS_VAR
        inv = lax.rsqrt(1.0 + 2.0 * var)
        keep(CHAN + depth, inv)
        if depth < LAYERS - 1:
            keep(CHAN + LAYERS + depth, (4.0 / math.pi) * inv * inv * lax.rsqrt(1.0 + 4.0 * var))
            current = self_act(var, inv)
    row = lax.broadcasted_iota(jnp.int32, (LANES, LANES), 0)
    lane = lax.broadcasted_iota(jnp.int32, (LANES, LANES), 1)
    same = jnp.where(row == lane, 1.0, 0.0).astype(BF16)
    maps_ref[...] = dot_bf16(parts_ref[...].astype(BF16), same, ((0,), (0,))).astype(BF16)


def fill_spreads(n_sup, n_tgt, tgt_ref, sup_ref):
    row = lax.broadcasted_iota(jnp.int32, (LANES, LANES), 0)
    lane = lax.broadcasted_iota(jnp.int32, (LANES, LANES), 1)
    own = row % n_tgt == lane % n_tgt
    for c in range(CHAN):
        tgt_ref[c] = jnp.where((row // n_tgt == c) & own, 1.0, 0.0).astype(BF16)
    own = row % n_sup == lane // n_tgt
    for k in range(sup_ref.shape[0]):
        sup_ref[k] = jnp.where((row // (PARTS * n_sup) == k) & own, 1.0, 0.0).astype(BF16)


def target_map(pix_ref, tgt_ref, c, b):
    pix = pix_ref[rows_of(b)].reshape(STEP_PIX, LANES)
    return as_map(dot_bf16(pix, tgt_ref[c], ((1,), (0,))))


def support_map(maps_ref, sup_ref, k, b):
    return as_map(dot_bf16(maps_ref[pixels_of(b), :], sup_ref[k], ((1,), (0,))))


QUARTERS = 4
QUARTER_ROWS = SIDE // QUARTERS
PER_QUARTER = QUARTER_ROWS // STEP_ROWS


def lane_block(shape):
    return lax.broadcasted_iota(jnp.int32, shape, len(shape) - 1) // (LANES // QUARTERS)


def put_edges(ref, first, final):
    width = LANES // QUARTERS
    block = lane_block(first.shape)
    ref[0] = jnp.where(block > 0, pltpu.roll(final, width, 2), 0.0)
    ref[QUARTER_ROWS + 1] = jnp.where(block < QUARTERS - 1, pltpu.roll(first, LANES - width, 2), 0.0)


def first_maps(pix_ref, maps_ref, tgt_ref, sup_ref, self_a, self_b, inv_ref, pair_ref):
    def one(b):
        own = pair = 0.0
        for c in range(CHAN):
            t = target_map(pix_ref, tgt_ref, c, b)
            own = own + t * t
            pair = pair + t * support_map(maps_ref, sup_ref, c, b)
        put(pair_ref, b, pair * (2.0 * BOX_SCALE / CHAN))
        at = pl.ds((b % PER_QUARTER) * STEP_ROWS + 1, STEP_ROWS)
        self_a[at] = jnp.where(lane_block(own.shape) == b // PER_QUARTER, own * (BOX_SCALE / CHAN), self_a[at])

    steps(one)
    put_edges(self_a, self_a[1], self_a[QUARTER_ROWS])
    for depth in range(LAYERS):
        now, later = (self_a, self_b) if depth % 2 == 0 else (self_b, self_a)
        for part in range(PER_QUARTER):
            var = box(now, part * STEP_ROWS, STEP_ROWS) + BIAS_VAR
            inv = lax.rsqrt(1.0 + 2.0 * var)
            inv_ref[depth, part] = inv
            if depth < LAYERS - 1:
                value = self_act(var, inv, BOX_SCALE)
                later[part * STEP_ROWS + 1 : (part + 1) * STEP_ROWS + 1] = value
        if depth < LAYERS - 1:
            put_edges(later, later[1], later[QUARTER_ROWS])


def target_inv(inv_ref, depth, b):
    x = inv_ref[depth, b % PER_QUARTER]
    x = jnp.where(lane_block(x.shape) == b // PER_QUARTER, x, 0.0)
    x = x + pltpu.roll(x, LANES // 2, 3)
    return x + pltpu.roll(x, LANES // 4, 3)


def forward_body(
    n_sup, pix_ref, maps_ref, gram_ref, out_ref, tgt_ref, sup_ref, self_a, self_b, inv_ref, pair_a, pair_b, acc_ref
):
    n_tgt = LANES // n_sup
    for ref in (self_a, self_b, pair_a, pair_b):
        ref[...] = jnp.zeros_like(ref)
    fill_spreads(n_sup, n_tgt, tgt_ref, sup_ref)
    first_maps(pix_ref, maps_ref, tgt_ref, sup_ref, self_a, self_b, inv_ref, pair_a)
    acc_ref[...] = jnp.zeros_like(acc_ref)
    for depth in range(LAYERS):
        now, later = (pair_a, pair_b) if depth % 2 == 0 else (pair_b, pair_a)

        def one(b, depth=depth, now=now, later=later):
            twice = step_box(now, b) + 2.0 * BIAS_VAR
            both = target_inv(inv_ref, depth, b) * support_map(maps_ref, sup_ref, CHAN + depth, b)
            value = act_of(twice * both, 2.0 * BOX_SCALE if depth < LAYERS - 1 else 1.0)[0]
            if depth < LAYERS - 1:
                put(later, b, value)
            else:
                acc_ref[...] += jnp.sum(value, axis=(0, 1))

        steps(one)
    value = jnp.sum(acc_ref[...], axis=0, keepdims=True) * (1.0 / PIX)
    n_dst = out_ref.shape[0]
    for j in range(n_sup):
        out_ref[:, j, :] = gram_ref[j * n_dst : (j + 1) * n_dst, :]
    for k in range(n_sup, out_ref.shape[1]):
        out_ref[:, k, :] = jnp.broadcast_to(value, (n_dst, LANES))


def backward_body(
    n_sup,
    pix_ref,
    maps_ref,
    high_ref,
    low_ref,
    tgt_ref,
    sup_ref,
    self_a,
    self_b,
    inv_ref,
    pair_a,
    pair_b,
    grad_a,
    grad_b,
    dcov_ref,
    dvar_ref,
):
    n_tgt = LANES // n_sup
    for ref in (self_a, self_b, pair_a, pair_b, grad_a, grad_b):
        ref[...] = jnp.zeros_like(ref)
    fill_spreads(n_sup, n_tgt, tgt_ref, sup_ref)
    first_maps(pix_ref, maps_ref, tgt_ref, sup_ref, self_a, self_b, inv_ref, pair_a)
    last = LAYERS - 1
    for depth in range(LAYERS):
        now, later = (pair_a, pair_b) if depth % 2 == 0 else (pair_b, pair_a)

        def one(b, depth=depth, now=now, later=later):
            twice = step_box(now, b) + 2.0 * BIAS_VAR
            s_inv = support_map(maps_ref, sup_ref, CHAN + depth, b)
            both = target_inv(inv_ref, depth, b) * s_inv
            x = twice * both
            if depth < last:
                value, a, left = act_of(x, 2.0 * BOX_SCALE)
                put(later, b, value)
            else:
                a = jnp.abs(x)
                left = lax.rsqrt(1.0 - a)
            slope = (2.0 / math.pi) * left * lax.rsqrt(1.0 + a)
            d_cov = 2.0 * both * slope
            d_var = -(slope * x) * (s_inv * s_inv)
            if depth < last:
                dcov_ref[depth, rows_of(b)] = d_cov
                dvar_ref[depth, rows_of(b)] = d_var
            else:
                put(later, b, d_cov * (1.0 / PIX))
                put(grad_a, b, d_var * (1.0 / PIX))

        steps(one)
    for depth in range(last - 1, -1, -1):
        now, later = (pair_a, pair_b) if depth % 2 == 0 else (pair_b, pair_a)
        own_now, own_later = (grad_a, grad_b) if depth % 2 == 0 else (grad_b, grad_a)

        def one(b, depth=depth, now=now, later=later, own_now=own_now, own_later=own_later):
            g_pair = BOX_SCALE * step_box(now, b)
            g_self = BOX_SCALE * step_box(own_now, b)
            slope = support_map(maps_ref, sup_ref, CHAN + LAYERS + depth, b)
            put(later, b, g_pair * dcov_ref[depth, rows_of(b)])
            put(own_later, b, g_self * slope + g_pair * dvar_ref[depth, rows_of(b)])

        steps(one)

    def finish(b):
        g_pair = (BOX_SCALE / CHAN) * step_box(pair_b, b)
        for c in range(CHAN + 1):
            g = g_pair * target_map(pix_ref, tgt_ref, c, b) if c < CHAN else BOX_SCALE * step_box(grad_b, b)
            g = g.reshape(STEP_PIX, LANES)
            high = g.astype(BF16)
            at = pl.ds(c * PIX + b * STEP_PIX, STEP_PIX)
            high_ref[at, :] = high
            low_ref[at, :] = (g - high.astype(F32)).astype(BF16)

    steps(finish)


def weigh_body(scale, n_tgt, got_ref, high_ref, low_ref, picked_ref, sup_ref, out_ref):
    n_src = got_ref.shape[0]
    n_sup = sup_ref.shape[1]
    rows = got_ref.shape[1]
    gram = jnp.sum(got_ref[...], axis=0)
    values = got_ref[:, n_sup, :]
    lane = lax.broadcasted_iota(jnp.int32, (n_src, LANES), 1)
    big = jnp.concatenate([jnp.where(lane // n_tgt == j, values, 0.0) for j in range(n_sup)], axis=0)
    part = dot_f32(gram, big, ((1,), (0,)))
    part = part + pltpu.roll(part, 64, 1)
    part = part + pltpu.roll(part, 32, 1)
    row = lax.broadcasted_iota(jnp.int32, (rows, LANES), 0)
    lane = lax.broadcasted_iota(jnp.int32, (rows, LANES), 1)
    weight = jnp.where(lane // n_tgt == row, scale * (part - picked_ref[...]), 0.0)
    w_high = weight.astype(BF16)
    w_low = (weight - w_high.astype(F32)).astype(BF16)
    zero = jnp.zeros_like(w_high)
    first = jnp.concatenate([w_high, w_low], axis=0)
    second = jnp.concatenate([w_high, zero], axis=0)
    sums = []
    for c in range(CHAN + 1):
        at = slice(c * PIX, (c + 1) * PIX)
        one = dot_bf16(first, high_ref[at, :], ((1,), (1,)))
        two = dot_bf16(second, low_ref[at, :], ((1,), (1,)))
        sums.append((one[:rows] + one[rows:] + two[:rows])[:n_sup])
    per = PIX // LANES
    for c in range(CHAN):
        grad = sums[c] + (2.0 / CHAN) * sup_ref[c] * sums[CHAN]
        for k in range(per):
            out_ref[pl.ds(c * per + k, n_sup, stride=CHAN * per), :] = grad[:, k * LANES : (k + 1) * LANES]


def residual_body(n_sup, start_ref, got_ref, mine_ref, labels_ref, out_ref):
    n_src = got_ref.shape[0]
    n_tgt, classes = out_ref.shape
    values = got_ref[:, n_sup, :]
    total = jnp.zeros((n_tgt, LANES), F32)
    for j in range(n_sup):
        one = dot_f32(values, mine_ref[j * n_src : (j + 1) * n_src, :], ((0,), (0,)))
        total = total + one[j * n_tgt : (j + 1) * n_tgt, :]
    predicted = total[:, CHAN * SIDE :]
    ids = start_ref[0] + lax.broadcasted_iota(jnp.int32, (n_tgt, classes), 1)
    out_ref[...] = predicted - jnp.where(labels_ref[...] == ids, 1.0, 0.0)


def pair_sum_body(a_ref, b_ref, out_ref):
    total = a_ref[...] + b_ref[...]
    for k in range(out_ref.shape[0]):
        out_ref[k] = total


def last_sum_body(parts_ref, out_ref):
    total = parts_ref[0]
    for k in range(1, parts_ref.shape[0]):
        total = total + parts_ref[k]
    n_sup = out_ref.shape[1]
    per = PIX // LANES
    for j in range(n_sup):
        for c in range(CHAN):
            for k in range(per):
                row = (j * CHAN + c) * per + k
                out_ref[c, j : j + 1, k * LANES : (k + 1) * LANES] = total[row : row + 1, :]


def maps(rows):
    return pltpu.VMEM((rows, TILES, SUB, LANES), F32)


def map_scratch(n_maps):
    return [
        pltpu.VMEM((CHAN, LANES, LANES), BF16),
        pltpu.VMEM((n_maps, LANES, LANES), BF16),
        maps(QUARTER_ROWS + 2),
        maps(QUARTER_ROWS + 2),
        pltpu.VMEM((LAYERS, PER_QUARTER, STEP_ROWS, TILES, SUB, LANES), F32),
        maps(SIDE + 2),
        maps(SIDE + 2),
    ]


def local(image_pool, target_index, labels, support, ridge_coef):
    n_chip, n_core, n_half, n_flat = (lax.axis_size(k) for k in ("chip", "core", "zh", "xy"))
    n_sup_dev = n_half * n_flat
    pool_rows = image_pool.shape[0]
    n_sup = support.shape[0]
    n_tgt = labels.shape[0]
    classes = ridge_coef.shape[1] // n_sup_dev
    chip, core, half = (lax.axis_index(k) for k in ("chip", "core", "zh"))
    first_row = ((chip * n_core + core) * n_half + half) * (n_flat * pool_rows)
    at = jnp.stack([first_row, chip, core]).astype(jnp.int32)
    start = ((half * n_flat + lax.axis_index("xy")) * classes)[None].astype(jnp.int32)
    label_col = labels[:, None]
    index_col = target_index[:, None]

    hbm = pl.BlockSpec(memory_space=pltpu.HBM)
    packed = pl.pallas_call(
        pack_body,
        out_shape=jax.ShapeDtypeStruct((n_flat, n_half, pool_rows, LANES), BF16),
        in_specs=[hbm, hbm],
        out_specs=VMEM,
        scratch_shapes=[
            pltpu.VMEM(image_pool.shape, BF16),
            pltpu.VMEM(ridge_coef.shape, F32),
            pltpu.VMEM((pool_rows, PIX), F32),
            pltpu.SemaphoreType.DMA((PACK_CUTS, CHAN)),
            pltpu.SemaphoreType.DMA,
        ],
        compiler_params=pltpu.CompilerParams(vmem_limit_bytes=56 * 2**20),
        name="pack_pool",
    )(image_pool, ridge_coef)
    rows = lax.all_to_all(packed, "xy", 0, 0, tiled=True)
    keep, send = call(
        select_body,
        [
            jax.ShapeDtypeStruct((n_chip, n_half, n_half, n_tgt, LANES), BF16),
            jax.ShapeDtypeStruct((n_chip, n_half, n_tgt, LANES), BF16),
        ],
        3,
        smem=(0,),
        name="select_targets",
    )(at, index_col, rows)
    swap = [(k, (k + 1) % n_core) for k in range(n_core)]
    other = lax.ppermute(send, "core", swap)
    chosen = call(
        add_body,
        jax.ShapeDtypeStruct((n_chip * n_half, n_half, n_tgt, LANES), BF16),
        2,
        name="add_core_targets",
    )(keep, other)
    got = lax.all_to_all(chosen, ("chip", "zh"), 0, 0, tiled=True)
    by_channel = jnp.swapaxes(support, 0, 1)
    n_maps = CHAN + 2 * LAYERS - 1
    s_maps, mine, gram, picked = call(
        side_body,
        [
            jax.ShapeDtypeStruct((PIX, LANES), BF16),
            jax.ShapeDtypeStruct((n_sup * n_sup_dev, LANES), F32),
            jax.ShapeDtypeStruct((n_sup * n_sup_dev, n_sup * n_sup_dev), F32),
            jax.ShapeDtypeStruct((SUB, LANES), F32),
        ],
        4,
        scratch=[pltpu.VMEM((LANES, PIX), F32)],
        flops=10**8,
        name="support_maps",
    )(by_channel, ridge_coef, label_col, got)
    merged = call(
        merge_body, jax.ShapeDtypeStruct((n_flat, n_half, SIDE, LANES), BF16), 1, name="merge_targets"
    )(got)
    pixels = lax.all_to_all(merged, "xy", 0, 0, tiled=True).reshape(SIDE, SIDE, LANES)
    sent = call(
        functools.partial(forward_body, n_sup),
        jax.ShapeDtypeStruct((n_sup_dev, SUB, LANES), F32),
        3,
        scratch=[*map_scratch(CHAN + LAYERS), pltpu.VMEM((SUB, LANES), F32)],
        flops=10**8,
        name="forward_maps",
        vmem=12,
    )(pixels, s_maps, gram)
    arrived = lax.all_to_all(sent, ("zh", "xy"), 0, 0, tiled=True)
    layer_maps = pltpu.VMEM((LAYERS - 1, SIDE, TILES, SUB, LANES), F32)
    flat = (CHAN + 1) * PIX
    high, low = call(
        functools.partial(backward_body, n_sup),
        [jax.ShapeDtypeStruct((flat, LANES), BF16)] * 2,
        2,
        scratch=[*map_scratch(n_maps), maps(SIDE + 2), maps(SIDE + 2), layer_maps, layer_maps],
        flops=10**10,
        name="backward_maps",
        vmem=20,
    )(pixels, s_maps)
    loss_scale = float(PIX) / n_tgt
    wide = n_sup * CHAN * PIX // LANES
    grad = call(
        functools.partial(weigh_body, loss_scale, n_tgt),
        jax.ShapeDtypeStruct((wide, LANES), F32),
        5,
        name="weigh_gradient",
        vmem=8,
    )(arrived, high, low, picked, by_channel)
    other = lax.ppermute(grad, "core", swap)
    summed = call(pair_sum_body, jax.ShapeDtypeStruct((n_chip, wide, LANES), F32), 2, name="sum_cores")(grad, other)
    shares = lax.all_to_all(summed, "chip", 0, 0, tiled=True)
    residual = call(
        functools.partial(residual_body, n_sup),
        jax.ShapeDtypeStruct((n_tgt, classes), F32),
        4,
        smem=(0,),
        flops=10**7,
        name="residual",
    )(start, arrived, mine, label_col)
    total = call(last_sum_body, jax.ShapeDtypeStruct(by_channel.shape, F32), 1, name="sum_chips")(shares)
    return (residual, jnp.swapaxes(total, 0, 1))


def solution(mesh):
    n_tgt, n_sup = mesh.devices.shape
    parts = Mesh(mesh.devices.reshape(n_tgt // 2, 2, 2, n_sup // 2), ("chip", "core", "zh", "xy"))
    tgt, sup = ("chip", "core"), ("zh", "xy")
    in_specs = (P((*tgt, *sup), None), P(), P(tgt), P(sup, None, None), P(sup, None))
    out_specs = (P(tgt, sup), P(sup, None, None))
    return jax.shard_map(local, mesh=parts, in_specs=in_specs, out_specs=out_specs, check_vma=False)
```

```python
import functools
import math

import jax
import jax.numpy as jnp
from jax import lax
from jax.experimental import pallas as pl
from jax.experimental.pallas import tpu as pltpu
from jax.sharding import Mesh, PartitionSpec as P

SIDE = 32
CHAN = 3
LAYERS = 4
PIX = SIDE * SIDE
SUB = 8
LANES = 128
TILES = SIDE // SUB
STEP_ROWS = 8
STEP_PIX = STEP_ROWS * SIDE
PARTS = 3
PACK_CUTS = 1

WEIGHT_VAR = 2.0
BIAS_VAR = 0.1
BOX_SCALE = WEIGHT_VAR / 9.0

F32 = jnp.float32
BF16 = jnp.bfloat16
VMEM = pl.BlockSpec(memory_space=pltpu.VMEM)
SMEM = pl.BlockSpec(memory_space=pltpu.SMEM)

ASIN_Q = (
    0.9999999439523269,
    -0.13661292782489154,
    0.05655466043182583,
    -0.03131997834776645,
    0.01767426424200143,
    -0.007641460751180656,
    0.0016626264836763138,
)


def call(body, outs, n_in, scratch=(), smem=(), flops=0, name=None, vmem=4):
    specs = [SMEM if k in smem else VMEM for k in range(n_in)]
    many = isinstance(outs, (list, tuple))
    return pl.pallas_call(
        body,
        out_shape=outs,
        in_specs=specs,
        out_specs=[VMEM] * len(outs) if many else VMEM,
        scratch_shapes=list(scratch),
        compiler_params=pltpu.CompilerParams(vmem_limit_bytes=vmem * 2**20),
        cost_estimate=pl.CostEstimate(flops=flops, bytes_accessed=1 << 20, transcendentals=0),
        name=name,
    )


def three_parts(x):
    high = x.astype(BF16)
    rest = x - high.astype(F32)
    mid = rest.astype(BF16)
    low = (rest - mid.astype(F32)).astype(BF16)
    return high, mid, low


def dot_f32(a, b, dims):
    return lax.dot_general(a, b, (dims, ((), ())), preferred_element_type=F32, precision=lax.Precision.HIGHEST)


def dot_bf16(a, b, dims):
    return lax.dot_general(a, b, (dims, ((), ())), preferred_element_type=F32)


def pack_body(pool_ref, ridge_ref, out_ref, pool_here, ridge_here, parts_ref, out_here, pool_sems, ridge_sem, out_sems):
    n_sup = ridge_ref.shape[0]
    halves = out_ref.shape[1]
    width = PIX // PACK_CUTS
    copies = [
        [
            pltpu.make_async_copy(
                pool_ref.at[:, pl.ds(c * PIX + k * width, width)],
                pool_here.at[:, pl.ds(c * PIX + k * width, width)],
                pool_sems.at[k, c],
            )
            for c in range(CHAN)
        ]
        for k in range(PACK_CUTS)
    ]
    ridge_copy = pltpu.make_async_copy(ridge_ref, ridge_here, ridge_sem)
    ridge_copy.start()
    for group in copies:
        for copy in group:
            copy.start()
    parts_ref[...] = jnp.zeros_like(parts_ref)
    ridge_copy.wait()
    for k, part in enumerate(three_parts(ridge_here[...])):
        parts_ref[k * n_sup : (k + 1) * n_sup, :] = part.astype(F32)
    writes = []
    for tile in range(PIX // LANES):
        at = tile * LANES
        if at % width == 0:
            for copy in copies[at // width]:
                copy.wait()
        pieces = [pool_here[:, c * PIX + at : c * PIX + at + LANES] for c in range(CHAN)]
        for r in range(LANES // SIDE):
            cut = [p[:, r * SIDE : (r + 1) * SIDE] for p in pieces]
            image_row = tile * (LANES // SIDE) + r
            owner, half = image_row // halves, image_row % halves
            first = (half * (SIDE // halves) + owner) * SIDE
            cut.append(parts_ref[:, first : first + SIDE].astype(BF16))
            out_here[owner, half] = jnp.concatenate(cut, axis=1)
        owners = LANES // SIDE // halves
        done = pl.ds(tile * owners, owners)
        writes.append(pltpu.make_async_copy(out_here.at[done], out_ref.at[done], out_sems.at[tile]))
        writes[-1].start()
    for write in writes:
        write.wait()


def pick_body(at_ref, index_ref, out_ref):
    wanted = index_ref[...] - at_ref[0]
    ids = lax.broadcasted_iota(jnp.int32, out_ref.shape, 1)
    out_ref[...] = jnp.where(ids == wanted, 1.0, 0.0).astype(BF16)


def select_body(at_ref, pick_ref, rows_ref, keep_ref, send_ref):
    n_src, halves, rows, _ = rows_ref.shape
    n_chip, _, _, n_tgt, _ = keep_ref.shape
    total = n_src * rows
    pick = pick_ref[...]
    lane = lax.broadcasted_iota(jnp.int32, (n_tgt, LANES), 1)
    pixel = lane < CHAN * SIDE
    low_core = at_ref[2] == 0
    share = n_src // n_chip // halves
    ridge = [[None] * halves for _ in range(halves)]
    for half in range(halves):
        for part in range(halves):
            first = (at_ref[1] * halves + part) * share
            block = rows_ref[pl.ds(first, share), half, 0 : n_tgt // share]
            ridge[half][part] = block.reshape(n_tgt, LANES).astype(F32)
    for part in range(halves):
        data = rows_ref[:, part].reshape(total, LANES)
        got = dot_bf16(pick, data, ((1,), (0,)))
        for chip in range(n_chip):
            low = got[2 * chip * n_tgt : (2 * chip + 1) * n_tgt]
            high = got[(2 * chip + 1) * n_tgt : (2 * chip + 2) * n_tgt]
            mine = jnp.where(low_core, low, high)
            send_ref[chip, part] = jnp.where(pixel, jnp.where(low_core, high, low), 0.0).astype(BF16)
            for half in range(halves):
                keep_ref[chip, half, part] = jnp.where(pixel, mine, ridge[half][part]).astype(BF16)


def add_body(keep_ref, other_ref, out_ref):
    n_chip, halves = keep_ref.shape[:2]
    for chip in range(n_chip):
        other = other_ref[chip].astype(F32)
        for half in range(halves):
            out_ref[chip * halves + half] = (keep_ref[chip, half].astype(F32) + other).astype(BF16)


def merge_body(parts_ref, out_ref):
    n_dst, halves, _, _ = out_ref.shape
    for half in range(halves):
        total = parts_ref[0, half].astype(F32)
        for k in range(1, parts_ref.shape[0]):
            total = total + parts_ref[k, half].astype(F32)
        turned = total.T
        n_tgt = turned.shape[1]
        cut = [turned[c * SIDE : (c + 1) * SIDE, :] for c in range(CHAN)]
        cut.append(jnp.zeros((SIDE, LANES - CHAN * n_tgt), F32))
        message = jnp.concatenate(cut, axis=1).astype(BF16)
        for k in range(n_dst):
            out_ref[k, half] = message


def steps(fn):
    for b in range(SIDE // STEP_ROWS):
        fn(b)


def rows_of(b):
    return pl.ds(b * STEP_ROWS, STEP_ROWS)


def pixels_of(b):
    return pl.ds(b * STEP_PIX, STEP_PIX)


def as_map(x):
    return x.reshape(x.shape[0] // SIDE, TILES, SUB, LANES)


def box(ref, row, n):
    x = ref[pl.ds(row, n + 2)]
    x = x[0:n] + x[1 : n + 1] + x[2 : n + 2]
    sub = lax.broadcasted_iota(jnp.int32, x.shape, 2)
    zero = jnp.zeros_like(x[:, 0:1])
    left = pltpu.roll(x, 1, 2)
    right = pltpu.roll(x, SUB - 1, 2)
    left = jnp.where(sub == 0, jnp.concatenate([zero, left[:, : TILES - 1]], axis=1), left)
    right = jnp.where(sub == SUB - 1, jnp.concatenate([right[:, 1:], zero], axis=1), right)
    return x + left + right


def step_box(ref, b):
    return box(ref, b * STEP_ROWS, STEP_ROWS)


def put(ref, b, x):
    ref[pl.ds(b * STEP_ROWS + 1, STEP_ROWS)] = x


def clear_halo(*refs):
    for ref in refs:
        for row in (0, SIDE + 1):
            ref[row] = jnp.zeros((TILES, SUB, LANES), F32)


def q_poly(a, scale=1.0):
    acc = (scale * ASIN_Q[-1]) * a + scale * ASIN_Q[-2]
    for c in ASIN_Q[-3::-1]:
        acc = acc * a + scale * c
    return acc


def act_of(x, scale):
    a = jnp.abs(x)
    left = 1.0 - a
    inv = lax.rsqrt(left)
    value = scale - left * inv * q_poly(a, scale)
    return jnp.where(x < 0.0, -value, value), a, inv


def self_act(var, inv, scale=1.0):
    x = 2.0 * var * inv * inv
    left = 1.0 - x
    return scale - left * lax.rsqrt(left) * q_poly(x, scale)


def flat_box(x):
    at = lax.broadcasted_iota(jnp.int32, x.shape, 1)
    col = at % SIDE
    left = jnp.where(col > 0, pltpu.roll(x, 1, 1), 0.0)
    right = jnp.where(col < SIDE - 1, pltpu.roll(x, PIX - 1, 1), 0.0)
    x = x + left + right
    above = jnp.where(at >= SIDE, pltpu.roll(x, SIDE, 1), 0.0)
    below = jnp.where(at < PIX - SIDE, pltpu.roll(x, PIX - SIDE, 1), 0.0)
    return x + above + below


def side_body(sup_ref, ridge_ref, labels_ref, got_ref, maps_ref, mine_ref, gram_ref, picked_ref, parts_ref):
    n_sup = sup_ref.shape[1]
    n_tgt = labels_ref.shape[0]
    n_parts, halves, n_rows, _ = got_ref.shape
    n_src = mine_ref.shape[0] // n_sup
    share = n_src // n_parts // halves
    for k in range(n_parts):
        for part in range(halves):
            got = got_ref[k, part].astype(F32)
            for i in range(share):
                at = i * (n_rows // share)
                total = got[at : at + n_sup]
                for p in range(1, PARTS):
                    total = total + got[at + p * n_sup : at + (p + 1) * n_sup]
                source = (k % halves) * (n_src // halves) + ((k // halves) * halves + part) * share + i
                mine_ref[pl.ds(source, n_sup, stride=n_src), :] = total
    lane = lax.broadcasted_iota(jnp.int32, mine_ref.shape, 1)
    mine = jnp.where(lane >= CHAN * SIDE, mine_ref[...], 0.0)
    mine_ref[...] = mine
    gram_ref[...] = dot_f32(mine, mine, ((1,), (1,)))
    hot = labels_ref[...] == lax.broadcasted_iota(jnp.int32, (n_tgt, ridge_ref.shape[1]), 1)
    hot = jnp.where(hot, 1.0, 0.0)
    hot = jnp.concatenate([hot] * n_sup, axis=0)
    picked_ref[...] = jnp.zeros_like(picked_ref)
    picked_ref[0:n_sup, :] = dot_f32(ridge_ref[...], hot, ((1,), (1,)))
    parts_ref[...] = jnp.zeros_like(parts_ref)

    def keep(k, x):
        for i, part in enumerate(three_parts(x)):
            at = (k * PARTS + i) * n_sup
            parts_ref[at : at + n_sup, :] = part.astype(F32)

    current = 0.0
    for c in range(CHAN):
        s = sup_ref[c]
        keep(c, s)
        current = current + s * s
    current = current * (1.0 / CHAN)
    for depth in range(LAYERS):
        var = BOX_SCALE * flat_box(current) + BIAS_VAR
        inv = lax.rsqrt(1.0 + 2.0 * var)
        keep(CHAN + depth, inv)
        if depth < LAYERS - 1:
            keep(CHAN + LAYERS + depth, (4.0 / math.pi) * inv * inv * lax.rsqrt(1.0 + 4.0 * var))
            current = self_act(var, inv)
    row = lax.broadcasted_iota(jnp.int32, (LANES, LANES), 0)
    lane = lax.broadcasted_iota(jnp.int32, (LANES, LANES), 1)
    same = jnp.where(row == lane, 1.0, 0.0).astype(BF16)
    maps_ref[...] = dot_bf16(parts_ref[...].astype(BF16), same, ((0,), (0,))).astype(BF16)


def fill_spreads(n_sup, n_tgt, tgt_ref, sup_ref):
    row = lax.broadcasted_iota(jnp.int32, (LANES, LANES), 0)
    lane = lax.broadcasted_iota(jnp.int32, (LANES, LANES), 1)
    own = row % n_tgt == lane % n_tgt
    for c in range(CHAN):
        tgt_ref[c] = jnp.where((row // n_tgt == c) & own, 1.0, 0.0).astype(BF16)
    own = row % n_sup == lane // n_tgt
    for k in range(sup_ref.shape[0]):
        sup_ref[k] = jnp.where((row // (PARTS * n_sup) == k) & own, 1.0, 0.0).astype(BF16)


def target_map(pix_ref, tgt_ref, c, b):
    pix = pix_ref[rows_of(b)].reshape(STEP_PIX, LANES)
    return as_map(dot_bf16(pix, tgt_ref[c], ((1,), (0,))))


def support_map(maps_ref, sup_ref, k, b):
    return as_map(dot_bf16(maps_ref[pixels_of(b), :], sup_ref[k], ((1,), (0,))))


QUARTERS = 4
QUARTER_ROWS = SIDE // QUARTERS
PER_QUARTER = QUARTER_ROWS // STEP_ROWS


def lane_block(shape):
    return lax.broadcasted_iota(jnp.int32, shape, len(shape) - 1) // (LANES // QUARTERS)


def put_edges(ref, first, final):
    width = LANES // QUARTERS
    block = lane_block(first.shape)
    ref[0] = jnp.where(block > 0, pltpu.roll(final, width, 2), 0.0)
    ref[QUARTER_ROWS + 1] = jnp.where(block < QUARTERS - 1, pltpu.roll(first, LANES - width, 2), 0.0)


def first_maps(pix_ref, maps_ref, tgt_ref, sup_ref, self_a, self_b, inv_ref, pair_ref):
    def one(b):
        own = pair = 0.0
        for c in range(CHAN):
            t = target_map(pix_ref, tgt_ref, c, b)
            own = own + t * t
            pair = pair + t * support_map(maps_ref, sup_ref, c, b)
        put(pair_ref, b, pair * (2.0 * BOX_SCALE / CHAN))
        at = pl.ds((b % PER_QUARTER) * STEP_ROWS + 1, STEP_ROWS)
        self_a[at] = jnp.where(lane_block(own.shape) == b // PER_QUARTER, own * (BOX_SCALE / CHAN), self_a[at])

    steps(one)
    put_edges(self_a, self_a[1], self_a[QUARTER_ROWS])
    for depth in range(LAYERS):
        now, later = (self_a, self_b) if depth % 2 == 0 else (self_b, self_a)
        for part in range(PER_QUARTER):
            var = box(now, part * STEP_ROWS, STEP_ROWS) + BIAS_VAR
            inv = lax.rsqrt(1.0 + 2.0 * var)
            inv_ref[depth, part] = inv
            if depth < LAYERS - 1:
                value = self_act(var, inv, BOX_SCALE)
                later[part * STEP_ROWS + 1 : (part + 1) * STEP_ROWS + 1] = value
        if depth < LAYERS - 1:
            put_edges(later, later[1], later[QUARTER_ROWS])


def target_inv(inv_ref, depth, b):
    x = inv_ref[depth, b % PER_QUARTER]
    x = jnp.where(lane_block(x.shape) == b // PER_QUARTER, x, 0.0)
    x = x + pltpu.roll(x, LANES // 2, 3)
    return x + pltpu.roll(x, LANES // 4, 3)


def forward_body(
    n_sup, pix_ref, maps_ref, gram_ref, out_ref, tgt_ref, sup_ref, self_a, self_b, inv_ref, pair_a, pair_b, acc_ref
):
    n_tgt = LANES // n_sup
    clear_halo(pair_a, pair_b)
    fill_spreads(n_sup, n_tgt, tgt_ref, sup_ref)
    first_maps(pix_ref, maps_ref, tgt_ref, sup_ref, self_a, self_b, inv_ref, pair_a)
    acc_ref[...] = jnp.zeros_like(acc_ref)
    for depth in range(LAYERS):
        now, later = (pair_a, pair_b) if depth % 2 == 0 else (pair_b, pair_a)

        def one(b, depth=depth, now=now, later=later):
            twice = step_box(now, b) + 2.0 * BIAS_VAR
            both = target_inv(inv_ref, depth, b) * support_map(maps_ref, sup_ref, CHAN + depth, b)
            value = act_of(twice * both, 2.0 * BOX_SCALE if depth < LAYERS - 1 else 1.0)[0]
            if depth < LAYERS - 1:
                put(later, b, value)
            else:
                acc_ref[...] += jnp.sum(value, axis=(0, 1))

        steps(one)
    value = jnp.sum(acc_ref[...], axis=0, keepdims=True) * (1.0 / PIX)
    n_dst = out_ref.shape[0]
    for j in range(n_sup):
        out_ref[:, j, :] = gram_ref[j * n_dst : (j + 1) * n_dst, :]
    for k in range(n_sup, out_ref.shape[1]):
        out_ref[:, k, :] = jnp.broadcast_to(value, (n_dst, LANES))


def backward_body(
    n_sup,
    pix_ref,
    maps_ref,
    high_ref,
    low_ref,
    tgt_ref,
    sup_ref,
    self_a,
    self_b,
    inv_ref,
    pair_a,
    pair_b,
    grad_a,
    grad_b,
    dcov_ref,
    dvar_ref,
):
    n_tgt = LANES // n_sup
    clear_halo(pair_a, pair_b, grad_a, grad_b)
    fill_spreads(n_sup, n_tgt, tgt_ref, sup_ref)
    first_maps(pix_ref, maps_ref, tgt_ref, sup_ref, self_a, self_b, inv_ref, pair_a)
    last = LAYERS - 1
    for depth in range(LAYERS):
        now, later = (pair_a, pair_b) if depth % 2 == 0 else (pair_b, pair_a)

        def one(b, depth=depth, now=now, later=later):
            twice = step_box(now, b) + 2.0 * BIAS_VAR
            s_inv = support_map(maps_ref, sup_ref, CHAN + depth, b)
            both = target_inv(inv_ref, depth, b) * s_inv
            x = twice * both
            if depth < last:
                value, a, left = act_of(x, 2.0 * BOX_SCALE)
                put(later, b, value)
            else:
                a = jnp.abs(x)
                left = lax.rsqrt(1.0 - a)
            slope = (2.0 / math.pi) * left * lax.rsqrt(1.0 + a)
            d_cov = 2.0 * both * slope
            d_var = -(slope * x) * (s_inv * s_inv)
            if depth < last:
                dcov_ref[depth, rows_of(b)] = d_cov
                dvar_ref[depth, rows_of(b)] = d_var
            else:
                put(later, b, d_cov * (1.0 / PIX))
                put(grad_a, b, d_var * (1.0 / PIX))

        steps(one)
    for depth in range(last - 1, -1, -1):
        now, later = (pair_a, pair_b) if depth % 2 == 0 else (pair_b, pair_a)
        own_now, own_later = (grad_a, grad_b) if depth % 2 == 0 else (grad_b, grad_a)

        def one(b, depth=depth, now=now, later=later, own_now=own_now, own_later=own_later):
            g_pair = BOX_SCALE * step_box(now, b)
            g_self = BOX_SCALE * step_box(own_now, b)
            slope = support_map(maps_ref, sup_ref, CHAN + LAYERS + depth, b)
            put(later, b, g_pair * dcov_ref[depth, rows_of(b)])
            put(own_later, b, g_self * slope + g_pair * dvar_ref[depth, rows_of(b)])

        steps(one)

    def finish(b):
        g_pair = (BOX_SCALE / CHAN) * step_box(pair_b, b)
        for c in range(CHAN + 1):
            g = g_pair * target_map(pix_ref, tgt_ref, c, b) if c < CHAN else BOX_SCALE * step_box(grad_b, b)
            g = g.reshape(STEP_PIX, LANES)
            high = g.astype(BF16)
            at = pl.ds(c * PIX + b * STEP_PIX, STEP_PIX)
            high_ref[at, :] = high
            low_ref[at, :] = (g - high.astype(F32)).astype(BF16)

    steps(finish)


def weigh_body(scale, n_tgt, got_ref, high_ref, low_ref, picked_ref, sup_ref, out_ref):
    n_src = got_ref.shape[0]
    n_sup = sup_ref.shape[1]
    rows = got_ref.shape[1]
    gram = jnp.sum(got_ref[...], axis=0)
    values = got_ref[:, n_sup, :]
    lane = lax.broadcasted_iota(jnp.int32, (n_src, LANES), 1)
    big = jnp.concatenate([jnp.where(lane // n_tgt == j, values, 0.0) for j in range(n_sup)], axis=0)
    part = dot_f32(gram, big, ((1,), (0,)))
    part = part + pltpu.roll(part, 64, 1)
    part = part + pltpu.roll(part, 32, 1)
    row = lax.broadcasted_iota(jnp.int32, (rows, LANES), 0)
    lane = lax.broadcasted_iota(jnp.int32, (rows, LANES), 1)
    weight = jnp.where(lane // n_tgt == row, scale * (part - picked_ref[...]), 0.0)
    w_high = weight.astype(BF16)
    w_low = (weight - w_high.astype(F32)).astype(BF16)
    zero = jnp.zeros_like(w_high)
    first = jnp.concatenate([w_high, w_low], axis=0)
    second = jnp.concatenate([w_high, zero], axis=0)
    sums = []
    for c in range(CHAN + 1):
        at = slice(c * PIX, (c + 1) * PIX)
        one = dot_bf16(first, high_ref[at, :], ((1,), (1,)))
        two = dot_bf16(second, low_ref[at, :], ((1,), (1,)))
        sums.append((one[:rows] + one[rows:] + two[:rows])[:n_sup])
    per = PIX // LANES
    for c in range(CHAN):
        grad = sums[c] + (2.0 / CHAN) * sup_ref[c] * sums[CHAN]
        for k in range(per):
            out_ref[pl.ds(c * per + k, n_sup, stride=CHAN * per), :] = grad[:, k * LANES : (k + 1) * LANES]


def residual_body(n_sup, start_ref, got_ref, mine_ref, labels_ref, out_ref):
    n_src = got_ref.shape[0]
    n_tgt, classes = out_ref.shape
    values = got_ref[:, n_sup, :]
    total = jnp.zeros((n_tgt, LANES), F32)
    for j in range(n_sup):
        one = dot_f32(values, mine_ref[j * n_src : (j + 1) * n_src, :], ((0,), (0,)))
        total = total + one[j * n_tgt : (j + 1) * n_tgt, :]
    predicted = total[:, CHAN * SIDE :]
    ids = start_ref[0] + lax.broadcasted_iota(jnp.int32, (n_tgt, classes), 1)
    out_ref[...] = predicted - jnp.where(labels_ref[...] == ids, 1.0, 0.0)


def pair_sum_body(a_ref, b_ref, out_ref):
    total = a_ref[...] + b_ref[...]
    for k in range(out_ref.shape[0]):
        out_ref[k] = total


def last_sum_body(parts_ref, out_ref):
    total = parts_ref[0]
    for k in range(1, parts_ref.shape[0]):
        total = total + parts_ref[k]
    n_sup = out_ref.shape[1]
    per = PIX // LANES
    for j in range(n_sup):
        for c in range(CHAN):
            for k in range(per):
                row = (j * CHAN + c) * per + k
                out_ref[c, j : j + 1, k * LANES : (k + 1) * LANES] = total[row : row + 1, :]


def maps(rows):
    return pltpu.VMEM((rows, TILES, SUB, LANES), F32)


def map_scratch(n_maps):
    return [
        pltpu.VMEM((CHAN, LANES, LANES), BF16),
        pltpu.VMEM((n_maps, LANES, LANES), BF16),
        maps(QUARTER_ROWS + 2),
        maps(QUARTER_ROWS + 2),
        pltpu.VMEM((LAYERS, PER_QUARTER, STEP_ROWS, TILES, SUB, LANES), F32),
        maps(SIDE + 2),
        maps(SIDE + 2),
    ]


def local(image_pool, target_index, labels, support, ridge_coef):
    n_chip, n_core, n_half, n_flat = (lax.axis_size(k) for k in ("chip", "core", "zh", "xy"))
    n_sup_dev = n_half * n_flat
    pool_rows = image_pool.shape[0]
    n_sup = support.shape[0]
    n_tgt = labels.shape[0]
    classes = ridge_coef.shape[1] // n_sup_dev
    chip, core, half = (lax.axis_index(k) for k in ("chip", "core", "zh"))
    first_row = ((chip * n_core + core) * n_half + half) * (n_flat * pool_rows)
    at = jnp.stack([first_row, chip, core]).astype(jnp.int32)
    start = ((half * n_flat + lax.axis_index("xy")) * classes)[None].astype(jnp.int32)
    label_col = labels[:, None]
    index_col = target_index[:, None]

    hbm = pl.BlockSpec(memory_space=pltpu.HBM)
    packed = pl.pallas_call(
        pack_body,
        out_shape=jax.ShapeDtypeStruct((n_flat, n_half, pool_rows, LANES), BF16),
        in_specs=[hbm, hbm],
        out_specs=hbm,
        scratch_shapes=[
            pltpu.VMEM(image_pool.shape, BF16),
            pltpu.VMEM(ridge_coef.shape, F32),
            pltpu.VMEM((pool_rows, PIX), F32),
            pltpu.VMEM((n_flat, n_half, pool_rows, LANES), BF16),
            pltpu.SemaphoreType.DMA((PACK_CUTS, CHAN)),
            pltpu.SemaphoreType.DMA,
            pltpu.SemaphoreType.DMA((PIX // LANES,)),
        ],
        compiler_params=pltpu.CompilerParams(vmem_limit_bytes=56 * 2**20),
        name="pack_pool",
    )(image_pool, ridge_coef)
    rows = lax.all_to_all(packed, "xy", 0, 0, tiled=True)
    pick = call(
        pick_body,
        jax.ShapeDtypeStruct((target_index.shape[0], n_flat * pool_rows), BF16),
        2,
        smem=(0,),
        flops=10**8,
        name="pick_rows",
    )(at, index_col)
    keep, send = call(
        select_body,
        [
            jax.ShapeDtypeStruct((n_chip, n_half, n_half, n_tgt, LANES), BF16),
            jax.ShapeDtypeStruct((n_chip, n_half, n_tgt, LANES), BF16),
        ],
        3,
        smem=(0,),
        name="select_targets",
    )(at, pick, rows)
    swap = [(k, (k + 1) % n_core) for k in range(n_core)]
    other = lax.ppermute(send, "core", swap)
    chosen = call(
        add_body,
        jax.ShapeDtypeStruct((n_chip * n_half, n_half, n_tgt, LANES), BF16),
        2,
        name="add_core_targets",
    )(keep, other)
    got = lax.all_to_all(chosen, ("chip", "zh"), 0, 0, tiled=True)
    by_channel = jnp.swapaxes(support, 0, 1)
    n_maps = CHAN + 2 * LAYERS - 1
    s_maps, mine, gram, picked = call(
        side_body,
        [
            jax.ShapeDtypeStruct((PIX, LANES), BF16),
            jax.ShapeDtypeStruct((n_sup * n_sup_dev, LANES), F32),
            jax.ShapeDtypeStruct((n_sup * n_sup_dev, n_sup * n_sup_dev), F32),
            jax.ShapeDtypeStruct((SUB, LANES), F32),
        ],
        4,
        scratch=[pltpu.VMEM((LANES, PIX), F32)],
        flops=10**8,
        name="support_maps",
    )(by_channel, ridge_coef, label_col, got)
    merged = call(
        merge_body, jax.ShapeDtypeStruct((n_flat, n_half, SIDE, LANES), BF16), 1, name="merge_targets"
    )(got)
    pixels = lax.all_to_all(merged, "xy", 0, 0, tiled=True).reshape(SIDE, SIDE, LANES)
    sent = call(
        functools.partial(forward_body, n_sup),
        jax.ShapeDtypeStruct((n_sup_dev, SUB, LANES), F32),
        3,
        scratch=[*map_scratch(CHAN + LAYERS), pltpu.VMEM((SUB, LANES), F32)],
        flops=10**8,
        name="forward_maps",
        vmem=12,
    )(pixels, s_maps, gram)
    arrived = lax.all_to_all(sent, ("zh", "xy"), 0, 0, tiled=True)
    layer_maps = pltpu.VMEM((LAYERS - 1, SIDE, TILES, SUB, LANES), F32)
    flat = (CHAN + 1) * PIX
    high, low = call(
        functools.partial(backward_body, n_sup),
        [jax.ShapeDtypeStruct((flat, LANES), BF16)] * 2,
        2,
        scratch=[*map_scratch(n_maps), maps(SIDE + 2), maps(SIDE + 2), layer_maps, layer_maps],
        flops=10**10,
        name="backward_maps",
        vmem=20,
    )(pixels, s_maps)
    loss_scale = float(PIX) / n_tgt
    wide = n_sup * CHAN * PIX // LANES
    grad = call(
        functools.partial(weigh_body, loss_scale, n_tgt),
        jax.ShapeDtypeStruct((wide, LANES), F32),
        5,
        name="weigh_gradient",
        vmem=8,
    )(arrived, high, low, picked, by_channel)
    other = lax.ppermute(grad, "core", swap)
    summed = call(pair_sum_body, jax.ShapeDtypeStruct((n_chip, wide, LANES), F32), 2, name="sum_cores")(grad, other)
    shares = lax.all_to_all(summed, "chip", 0, 0, tiled=True)
    residual = call(
        functools.partial(residual_body, n_sup),
        jax.ShapeDtypeStruct((n_tgt, classes), F32),
        4,
        smem=(0,),
        flops=10**7,
        name="residual",
    )(start, arrived, mine, label_col)
    total = call(last_sum_body, jax.ShapeDtypeStruct(by_channel.shape, F32), 1, name="sum_chips")(shares)
    return (residual, jnp.swapaxes(total, 0, 1))


def solution(mesh):
    n_tgt, n_sup = mesh.devices.shape
    parts = Mesh(mesh.devices.reshape(n_tgt // 2, 2, 2, n_sup // 2), ("chip", "core", "zh", "xy"))
    tgt, sup = ("chip", "core"), ("zh", "xy")
    in_specs = (P((*tgt, *sup), None), P(), P(tgt), P(sup, None, None), P(sup, None))
    out_specs = (P(tgt, sup), P(sup, None, None))
    return jax.shard_map(local, mesh=parts, in_specs=in_specs, out_specs=out_specs, check_vma=False)
```

```python
import functools
import math

import jax
import jax.numpy as jnp
from jax import lax
from jax.experimental import pallas as pl
from jax.experimental.pallas import tpu as pltpu
from jax.sharding import Mesh, PartitionSpec as P

SIDE = 32
CHAN = 3
LAYERS = 4
PIX = SIDE * SIDE
SUB = 8
LANES = 128
TILES = SIDE // SUB
STEP_ROWS = 8
STEP_PIX = STEP_ROWS * SIDE
PARTS = 3
PACK_CUTS = 1

WEIGHT_VAR = 2.0
BIAS_VAR = 0.1
BOX_SCALE = WEIGHT_VAR / 9.0

F32 = jnp.float32
BF16 = jnp.bfloat16
VMEM = pl.BlockSpec(memory_space=pltpu.VMEM)
SMEM = pl.BlockSpec(memory_space=pltpu.SMEM)

ASIN_Q = (
    0.9999999439523269,
    -0.13661292782489154,
    0.05655466043182583,
    -0.03131997834776645,
    0.01767426424200143,
    -0.007641460751180656,
    0.0016626264836763138,
)


def call(body, outs, n_in, scratch=(), smem=(), flops=0, name=None, vmem=4):
    specs = [SMEM if k in smem else VMEM for k in range(n_in)]
    many = isinstance(outs, (list, tuple))
    return pl.pallas_call(
        body,
        out_shape=outs,
        in_specs=specs,
        out_specs=[VMEM] * len(outs) if many else VMEM,
        scratch_shapes=list(scratch),
        compiler_params=pltpu.CompilerParams(vmem_limit_bytes=vmem * 2**20),
        cost_estimate=pl.CostEstimate(flops=flops, bytes_accessed=1 << 20, transcendentals=0),
        name=name,
    )


def three_parts(x):
    high = x.astype(BF16)
    rest = x - high.astype(F32)
    mid = rest.astype(BF16)
    low = (rest - mid.astype(F32)).astype(BF16)
    return high, mid, low


def dot_f32(a, b, dims):
    return lax.dot_general(a, b, (dims, ((), ())), preferred_element_type=F32, precision=lax.Precision.HIGHEST)


def dot_bf16(a, b, dims):
    return lax.dot_general(a, b, (dims, ((), ())), preferred_element_type=F32)


def pack_body(pool_ref, ridge_ref, out_ref, pool_here, ridge_here, parts_ref, out_here, pool_sems, ridge_sem, out_sems):
    n_sup = ridge_ref.shape[0]
    halves = out_ref.shape[1]
    width = PIX // PACK_CUTS
    copies = [
        [
            pltpu.make_async_copy(
                pool_ref.at[:, pl.ds(c * PIX + k * width, width)],
                pool_here.at[:, pl.ds(c * PIX + k * width, width)],
                pool_sems.at[k, c],
            )
            for c in range(CHAN)
        ]
        for k in range(PACK_CUTS)
    ]
    ridge_copy = pltpu.make_async_copy(ridge_ref, ridge_here, ridge_sem)
    ridge_copy.start()
    for group in copies:
        for copy in group:
            copy.start()
    parts_ref[...] = jnp.zeros_like(parts_ref)
    ridge_copy.wait()
    for k, part in enumerate(three_parts(ridge_here[...])):
        parts_ref[k * n_sup : (k + 1) * n_sup, :] = part.astype(F32)
    writes = []
    for tile in range(PIX // LANES):
        at = tile * LANES
        if at % width == 0:
            for copy in copies[at // width]:
                copy.wait()
        pieces = [pool_here[:, c * PIX + at : c * PIX + at + LANES] for c in range(CHAN)]
        for r in range(LANES // SIDE):
            cut = [p[:, r * SIDE : (r + 1) * SIDE] for p in pieces]
            image_row = tile * (LANES // SIDE) + r
            owner, half = image_row // halves, image_row % halves
            first = (half * (SIDE // halves) + owner) * SIDE
            cut.append(parts_ref[:, first : first + SIDE].astype(BF16))
            out_here[owner, half] = jnp.concatenate(cut, axis=1)
        owners = LANES // SIDE // halves
        done = pl.ds(tile * owners, owners)
        writes.append(pltpu.make_async_copy(out_here.at[done], out_ref.at[done], out_sems.at[tile]))
        writes[-1].start()
    for write in writes:
        write.wait()


def pick_body(at_ref, index_ref, out_ref):
    wanted = index_ref[...] - at_ref[0]
    ids = lax.broadcasted_iota(jnp.int32, out_ref.shape, 1)
    out_ref[...] = jnp.where(ids == wanted, 1.0, 0.0).astype(BF16)


def select_body(at_ref, pick_ref, rows_ref, keep_ref, send_ref):
    n_src, halves, rows, _ = rows_ref.shape
    n_chip, _, _, n_tgt, _ = keep_ref.shape
    total = n_src * rows
    pick = pick_ref[...]
    lane = lax.broadcasted_iota(jnp.int32, (n_tgt, LANES), 1)
    pixel = lane < CHAN * SIDE
    low_core = at_ref[2] == 0
    share = n_src // n_chip // halves
    ridge = [[None] * halves for _ in range(halves)]
    for half in range(halves):
        for part in range(halves):
            first = (at_ref[1] * halves + part) * share
            block = rows_ref[pl.ds(first, share), half, 0 : n_tgt // share]
            ridge[half][part] = block.reshape(n_tgt, LANES).astype(F32)
    both = jnp.concatenate([rows_ref[:, part].reshape(total, LANES) for part in range(halves)], axis=1)
    both = dot_bf16(pick, both, ((1,), (0,)))
    for part in range(halves):
        got = both[:, part * LANES : (part + 1) * LANES]
        for chip in range(n_chip):
            low = got[2 * chip * n_tgt : (2 * chip + 1) * n_tgt]
            high = got[(2 * chip + 1) * n_tgt : (2 * chip + 2) * n_tgt]
            mine = jnp.where(low_core, low, high)
            send_ref[chip, part] = jnp.where(pixel, jnp.where(low_core, high, low), 0.0).astype(BF16)
            for half in range(halves):
                keep_ref[chip, half, part] = jnp.where(pixel, mine, ridge[half][part]).astype(BF16)


def add_body(keep_ref, other_ref, out_ref):
    n_chip, halves = keep_ref.shape[:2]
    for chip in range(n_chip):
        other = other_ref[chip].astype(F32)
        for half in range(halves):
            out_ref[chip * halves + half] = (keep_ref[chip, half].astype(F32) + other).astype(BF16)


def merge_body(parts_ref, out_ref):
    n_dst, halves, _, _ = out_ref.shape
    for half in range(halves):
        total = parts_ref[0, half].astype(F32)
        for k in range(1, parts_ref.shape[0]):
            total = total + parts_ref[k, half].astype(F32)
        turned = total.T
        n_tgt = turned.shape[1]
        cut = [turned[c * SIDE : (c + 1) * SIDE, :] for c in range(CHAN)]
        cut.append(jnp.zeros((SIDE, LANES - CHAN * n_tgt), F32))
        message = jnp.concatenate(cut, axis=1).astype(BF16)
        for k in range(n_dst):
            out_ref[k, half] = message


def steps(fn):
    for b in range(SIDE // STEP_ROWS):
        fn(b)


def rows_of(b):
    return pl.ds(b * STEP_ROWS, STEP_ROWS)


def pixels_of(b):
    return pl.ds(b * STEP_PIX, STEP_PIX)


def as_map(x):
    return x.reshape(x.shape[0] // SIDE, TILES, SUB, LANES)


def box(ref, row, n):
    x = ref[pl.ds(row, n + 2)]
    x = x[0:n] + x[1 : n + 1] + x[2 : n + 2]
    sub = lax.broadcasted_iota(jnp.int32, x.shape, 2)
    zero = jnp.zeros_like(x[:, 0:1])
    left = pltpu.roll(x, 1, 2)
    right = pltpu.roll(x, SUB - 1, 2)
    left = jnp.where(sub == 0, jnp.concatenate([zero, left[:, : TILES - 1]], axis=1), left)
    right = jnp.where(sub == SUB - 1, jnp.concatenate([right[:, 1:], zero], axis=1), right)
    return x + left + right


def step_box(ref, b):
    return box(ref, b * STEP_ROWS, STEP_ROWS)


def put(ref, b, x):
    ref[pl.ds(b * STEP_ROWS + 1, STEP_ROWS)] = x


def clear_halo(*refs):
    for ref in refs:
        for row in (0, SIDE + 1):
            ref[row] = jnp.zeros((TILES, SUB, LANES), F32)


def q_poly(a, scale=1.0):
    acc = (scale * ASIN_Q[-1]) * a + scale * ASIN_Q[-2]
    for c in ASIN_Q[-3::-1]:
        acc = acc * a + scale * c
    return acc


def act_of(x, scale):
    a = jnp.abs(x)
    left = 1.0 - a
    inv = lax.rsqrt(left)
    value = scale - left * inv * q_poly(a, scale)
    return jnp.where(x < 0.0, -value, value), a, inv


def self_act(var, inv, scale=1.0):
    x = 2.0 * var * inv * inv
    left = 1.0 - x
    return scale - left * lax.rsqrt(left) * q_poly(x, scale)


def flat_box(x):
    at = lax.broadcasted_iota(jnp.int32, x.shape, 1)
    col = at % SIDE
    left = jnp.where(col > 0, pltpu.roll(x, 1, 1), 0.0)
    right = jnp.where(col < SIDE - 1, pltpu.roll(x, PIX - 1, 1), 0.0)
    x = x + left + right
    above = jnp.where(at >= SIDE, pltpu.roll(x, SIDE, 1), 0.0)
    below = jnp.where(at < PIX - SIDE, pltpu.roll(x, PIX - SIDE, 1), 0.0)
    return x + above + below


def side_body(sup_ref, ridge_ref, labels_ref, got_ref, maps_ref, mine_ref, gram_ref, picked_ref, parts_ref):
    n_sup = sup_ref.shape[1]
    n_tgt = labels_ref.shape[0]
    n_parts, halves, n_rows, _ = got_ref.shape
    n_src = mine_ref.shape[0] // n_sup
    share = n_src // n_parts // halves
    for k in range(n_parts):
        for part in range(halves):
            got = got_ref[k, part].astype(F32)
            for i in range(share):
                at = i * (n_rows // share)
                total = got[at : at + n_sup]
                for p in range(1, PARTS):
                    total = total + got[at + p * n_sup : at + (p + 1) * n_sup]
                source = (k % halves) * (n_src // halves) + ((k // halves) * halves + part) * share + i
                mine_ref[pl.ds(source, n_sup, stride=n_src), :] = total
    lane = lax.broadcasted_iota(jnp.int32, mine_ref.shape, 1)
    mine = jnp.where(lane >= CHAN * SIDE, mine_ref[...], 0.0)
    mine_ref[...] = mine
    gram_ref[...] = dot_f32(mine, mine, ((1,), (1,)))
    hot = labels_ref[...] == lax.broadcasted_iota(jnp.int32, (n_tgt, ridge_ref.shape[1]), 1)
    hot = jnp.where(hot, 1.0, 0.0)
    hot = jnp.concatenate([hot] * n_sup, axis=0)
    picked_ref[...] = jnp.zeros_like(picked_ref)
    picked_ref[0:n_sup, :] = dot_f32(ridge_ref[...], hot, ((1,), (1,)))
    parts_ref[...] = jnp.zeros_like(parts_ref)

    def keep(k, x):
        for i, part in enumerate(three_parts(x)):
            at = (k * PARTS + i) * n_sup
            parts_ref[at : at + n_sup, :] = part.astype(F32)

    current = 0.0
    for c in range(CHAN):
        s = sup_ref[c]
        keep(c, s)
        current = current + s * s
    current = current * (1.0 / CHAN)
    for depth in range(LAYERS):
        var = BOX_SCALE * flat_box(current) + BIAS_VAR
        inv = lax.rsqrt(1.0 + 2.0 * var)
        keep(CHAN + depth, inv)
        if depth < LAYERS - 1:
            keep(CHAN + LAYERS + depth, (4.0 / math.pi) * inv * inv * lax.rsqrt(1.0 + 4.0 * var))
            current = self_act(var, inv)
    row = lax.broadcasted_iota(jnp.int32, (LANES, LANES), 0)
    lane = lax.broadcasted_iota(jnp.int32, (LANES, LANES), 1)
    same = jnp.where(row == lane, 1.0, 0.0).astype(BF16)
    maps_ref[...] = dot_bf16(parts_ref[...].astype(BF16), same, ((0,), (0,))).astype(BF16)


def fill_spreads(n_sup, n_tgt, tgt_ref, sup_ref):
    row = lax.broadcasted_iota(jnp.int32, (LANES, LANES), 0)
    lane = lax.broadcasted_iota(jnp.int32, (LANES, LANES), 1)
    own = row % n_tgt == lane % n_tgt
    for c in range(CHAN):
        tgt_ref[c] = jnp.where((row // n_tgt == c) & own, 1.0, 0.0).astype(BF16)
    own = row % n_sup == lane // n_tgt
    for k in range(sup_ref.shape[0]):
        sup_ref[k] = jnp.where((row // (PARTS * n_sup) == k) & own, 1.0, 0.0).astype(BF16)


def target_map(pix_ref, tgt_ref, c, b):
    pix = pix_ref[rows_of(b)].reshape(STEP_PIX, LANES)
    return as_map(dot_bf16(pix, tgt_ref[c], ((1,), (0,))))


def support_map(maps_ref, sup_ref, k, b):
    return as_map(dot_bf16(maps_ref[pixels_of(b), :], sup_ref[k], ((1,), (0,))))


QUARTERS = 4
QUARTER_ROWS = SIDE // QUARTERS
PER_QUARTER = QUARTER_ROWS // STEP_ROWS


def lane_block(shape):
    return lax.broadcasted_iota(jnp.int32, shape, len(shape) - 1) // (LANES // QUARTERS)


def put_edges(ref, first, final):
    width = LANES // QUARTERS
    block = lane_block(first.shape)
    ref[0] = jnp.where(block > 0, pltpu.roll(final, width, 2), 0.0)
    ref[QUARTER_ROWS + 1] = jnp.where(block < QUARTERS - 1, pltpu.roll(first, LANES - width, 2), 0.0)


def first_maps(pix_ref, maps_ref, tgt_ref, sup_ref, self_a, self_b, inv_ref, pair_ref):
    def one(b):
        own = pair = 0.0
        pix = pix_ref[rows_of(b)].reshape(STEP_PIX, LANES)
        spread_t = jnp.concatenate([tgt_ref[c] for c in range(CHAN)], axis=1)
        spread_s = jnp.concatenate([sup_ref[c] for c in range(CHAN)], axis=1)
        all_t = dot_bf16(pix, spread_t, ((1,), (0,)))
        all_s = dot_bf16(maps_ref[pixels_of(b), :], spread_s, ((1,), (0,)))
        for c in range(CHAN):
            t = as_map(all_t[:, c * LANES : (c + 1) * LANES])
            own = own + t * t
            pair = pair + t * as_map(all_s[:, c * LANES : (c + 1) * LANES])
        put(pair_ref, b, pair * (2.0 * BOX_SCALE / CHAN))
        at = pl.ds((b % PER_QUARTER) * STEP_ROWS + 1, STEP_ROWS)
        self_a[at] = jnp.where(lane_block(own.shape) == b // PER_QUARTER, own * (BOX_SCALE / CHAN), self_a[at])

    steps(one)
    put_edges(self_a, self_a[1], self_a[QUARTER_ROWS])
    for depth in range(LAYERS):
        now, later = (self_a, self_b) if depth % 2 == 0 else (self_b, self_a)
        for part in range(PER_QUARTER):
            var = box(now, part * STEP_ROWS, STEP_ROWS) + BIAS_VAR
            inv = lax.rsqrt(1.0 + 2.0 * var)
            inv_ref[depth, part] = inv
            if depth < LAYERS - 1:
                value = self_act(var, inv, BOX_SCALE)
                later[part * STEP_ROWS + 1 : (part + 1) * STEP_ROWS + 1] = value
        if depth < LAYERS - 1:
            put_edges(later, later[1], later[QUARTER_ROWS])


def target_inv(inv_ref, depth, b):
    x = inv_ref[depth, b % PER_QUARTER]
    x = jnp.where(lane_block(x.shape) == b // PER_QUARTER, x, 0.0)
    x = x + pltpu.roll(x, LANES // 2, 3)
    return x + pltpu.roll(x, LANES // 4, 3)


def forward_body(
    n_sup, pix_ref, maps_ref, gram_ref, out_ref, tgt_ref, sup_ref, self_a, self_b, inv_ref, pair_a, pair_b, acc_ref
):
    n_tgt = LANES // n_sup
    clear_halo(pair_a, pair_b)
    fill_spreads(n_sup, n_tgt, tgt_ref, sup_ref)
    first_maps(pix_ref, maps_ref, tgt_ref, sup_ref, self_a, self_b, inv_ref, pair_a)
    acc_ref[...] = jnp.zeros_like(acc_ref)
    for depth in range(LAYERS):
        now, later = (pair_a, pair_b) if depth % 2 == 0 else (pair_b, pair_a)

        def one(b, depth=depth, now=now, later=later):
            twice = step_box(now, b) + 2.0 * BIAS_VAR
            both = target_inv(inv_ref, depth, b) * support_map(maps_ref, sup_ref, CHAN + depth, b)
            value = act_of(twice * both, 2.0 * BOX_SCALE if depth < LAYERS - 1 else 1.0)[0]
            if depth < LAYERS - 1:
                put(later, b, value)
            else:
                acc_ref[...] += jnp.sum(value, axis=(0, 1))

        steps(one)
    value = jnp.sum(acc_ref[...], axis=0, keepdims=True) * (1.0 / PIX)
    n_dst = out_ref.shape[0]
    for j in range(n_sup):
        out_ref[:, j, :] = gram_ref[j * n_dst : (j + 1) * n_dst, :]
    for k in range(n_sup, out_ref.shape[1]):
        out_ref[:, k, :] = jnp.broadcast_to(value, (n_dst, LANES))


def backward_body(
    n_sup,
    pix_ref,
    maps_ref,
    high_ref,
    low_ref,
    tgt_ref,
    sup_ref,
    self_a,
    self_b,
    inv_ref,
    pair_a,
    pair_b,
    grad_a,
    grad_b,
    dcov_ref,
    dvar_ref,
):
    n_tgt = LANES // n_sup
    clear_halo(pair_a, pair_b, grad_a, grad_b)
    fill_spreads(n_sup, n_tgt, tgt_ref, sup_ref)
    first_maps(pix_ref, maps_ref, tgt_ref, sup_ref, self_a, self_b, inv_ref, pair_a)
    last = LAYERS - 1
    for depth in range(LAYERS):
        now, later = (pair_a, pair_b) if depth % 2 == 0 else (pair_b, pair_a)

        def one(b, depth=depth, now=now, later=later):
            twice = step_box(now, b) + 2.0 * BIAS_VAR
            s_inv = support_map(maps_ref, sup_ref, CHAN + depth, b)
            both = target_inv(inv_ref, depth, b) * s_inv
            x = twice * both
            if depth < last:
                value, a, left = act_of(x, 2.0 * BOX_SCALE)
                put(later, b, value)
            else:
                a = jnp.abs(x)
                left = lax.rsqrt(1.0 - a)
            slope = (2.0 / math.pi) * left * lax.rsqrt(1.0 + a)
            d_cov = 2.0 * both * slope
            d_var = -(slope * x) * (s_inv * s_inv)
            if depth < last:
                dcov_ref[depth, rows_of(b)] = d_cov
                dvar_ref[depth, rows_of(b)] = d_var
            else:
                put(later, b, d_cov * (1.0 / PIX))
                put(grad_a, b, d_var * (1.0 / PIX))

        steps(one)
    for depth in range(last - 1, -1, -1):
        now, later = (pair_a, pair_b) if depth % 2 == 0 else (pair_b, pair_a)
        own_now, own_later = (grad_a, grad_b) if depth % 2 == 0 else (grad_b, grad_a)

        def one(b, depth=depth, now=now, later=later, own_now=own_now, own_later=own_later):
            g_pair = BOX_SCALE * step_box(now, b)
            g_self = BOX_SCALE * step_box(own_now, b)
            slope = support_map(maps_ref, sup_ref, CHAN + LAYERS + depth, b)
            put(later, b, g_pair * dcov_ref[depth, rows_of(b)])
            put(own_later, b, g_self * slope + g_pair * dvar_ref[depth, rows_of(b)])

        steps(one)

    def finish(b):
        g_pair = (BOX_SCALE / CHAN) * step_box(pair_b, b)
        for c in range(CHAN + 1):
            g = g_pair * target_map(pix_ref, tgt_ref, c, b) if c < CHAN else BOX_SCALE * step_box(grad_b, b)
            g = g.reshape(STEP_PIX, LANES)
            high = g.astype(BF16)
            at = pl.ds(c * PIX + b * STEP_PIX, STEP_PIX)
            high_ref[at, :] = high
            low_ref[at, :] = (g - high.astype(F32)).astype(BF16)

    steps(finish)


def weigh_body(scale, n_tgt, got_ref, high_ref, low_ref, picked_ref, sup_ref, out_ref):
    n_src = got_ref.shape[0]
    n_sup = sup_ref.shape[1]
    rows = got_ref.shape[1]
    gram = jnp.sum(got_ref[...], axis=0)
    values = got_ref[:, n_sup, :]
    lane = lax.broadcasted_iota(jnp.int32, (n_src, LANES), 1)
    big = jnp.concatenate([jnp.where(lane // n_tgt == j, values, 0.0) for j in range(n_sup)], axis=0)
    part = dot_f32(gram, big, ((1,), (0,)))
    part = part + pltpu.roll(part, 64, 1)
    part = part + pltpu.roll(part, 32, 1)
    row = lax.broadcasted_iota(jnp.int32, (rows, LANES), 0)
    lane = lax.broadcasted_iota(jnp.int32, (rows, LANES), 1)
    weight = jnp.where(lane // n_tgt == row, scale * (part - picked_ref[...]), 0.0)
    w_high = weight.astype(BF16)
    w_low = (weight - w_high.astype(F32)).astype(BF16)
    zero = jnp.zeros_like(w_high)
    first = jnp.concatenate([w_high, w_low], axis=0)
    second = jnp.concatenate([w_high, zero], axis=0)
    sums = []
    for c in range(CHAN + 1):
        at = slice(c * PIX, (c + 1) * PIX)
        one = dot_bf16(first, high_ref[at, :], ((1,), (1,)))
        two = dot_bf16(second, low_ref[at, :], ((1,), (1,)))
        sums.append((one[:rows] + one[rows:] + two[:rows])[:n_sup])
    per = PIX // LANES
    for c in range(CHAN):
        grad = sums[c] + (2.0 / CHAN) * sup_ref[c] * sums[CHAN]
        for k in range(per):
            out_ref[pl.ds(c * per + k, n_sup, stride=CHAN * per), :] = grad[:, k * LANES : (k + 1) * LANES]


def residual_body(n_sup, start_ref, got_ref, mine_ref, labels_ref, out_ref):
    n_src = got_ref.shape[0]
    n_tgt, classes = out_ref.shape
    values = got_ref[:, n_sup, :]
    total = jnp.zeros((n_tgt, LANES), F32)
    for j in range(n_sup):
        one = dot_f32(values, mine_ref[j * n_src : (j + 1) * n_src, :], ((0,), (0,)))
        total = total + one[j * n_tgt : (j + 1) * n_tgt, :]
    predicted = total[:, CHAN * SIDE :]
    ids = start_ref[0] + lax.broadcasted_iota(jnp.int32, (n_tgt, classes), 1)
    out_ref[...] = predicted - jnp.where(labels_ref[...] == ids, 1.0, 0.0)


def pair_sum_body(a_ref, b_ref, out_ref):
    total = a_ref[...] + b_ref[...]
    for k in range(out_ref.shape[0]):
        out_ref[k] = total


def last_sum_body(parts_ref, out_ref):
    total = parts_ref[0]
    for k in range(1, parts_ref.shape[0]):
        total = total + parts_ref[k]
    n_sup = out_ref.shape[1]
    per = PIX // LANES
    for j in range(n_sup):
        for c in range(CHAN):
            for k in range(per):
                row = (j * CHAN + c) * per + k
                out_ref[c, j : j + 1, k * LANES : (k + 1) * LANES] = total[row : row + 1, :]


def maps(rows):
    return pltpu.VMEM((rows, TILES, SUB, LANES), F32)


def map_scratch(n_maps):
    return [
        pltpu.VMEM((CHAN, LANES, LANES), BF16),
        pltpu.VMEM((n_maps, LANES, LANES), BF16),
        maps(QUARTER_ROWS + 2),
        maps(QUARTER_ROWS + 2),
        pltpu.VMEM((LAYERS, PER_QUARTER, STEP_ROWS, TILES, SUB, LANES), F32),
        maps(SIDE + 2),
        maps(SIDE + 2),
    ]


def local(image_pool, target_index, labels, support, ridge_coef):
    n_chip, n_core, n_half, n_flat = (lax.axis_size(k) for k in ("chip", "core", "zh", "xy"))
    n_sup_dev = n_half * n_flat
    pool_rows = image_pool.shape[0]
    n_sup = support.shape[0]
    n_tgt = labels.shape[0]
    classes = ridge_coef.shape[1] // n_sup_dev
    chip, core, half = (lax.axis_index(k) for k in ("chip", "core", "zh"))
    first_row = ((chip * n_core + core) * n_half + half) * (n_flat * pool_rows)
    at = jnp.stack([first_row, chip, core]).astype(jnp.int32)
    start = ((half * n_flat + lax.axis_index("xy")) * classes)[None].astype(jnp.int32)
    label_col = labels[:, None]
    index_col = target_index[:, None]

    hbm = pl.BlockSpec(memory_space=pltpu.HBM)
    packed = pl.pallas_call(
        pack_body,
        out_shape=jax.ShapeDtypeStruct((n_flat, n_half, pool_rows, LANES), BF16),
        in_specs=[hbm, hbm],
        out_specs=hbm,
        scratch_shapes=[
            pltpu.VMEM(image_pool.shape, BF16),
            pltpu.VMEM(ridge_coef.shape, F32),
            pltpu.VMEM((pool_rows, PIX), F32),
            pltpu.VMEM((n_flat, n_half, pool_rows, LANES), BF16),
            pltpu.SemaphoreType.DMA((PACK_CUTS, CHAN)),
            pltpu.SemaphoreType.DMA,
            pltpu.SemaphoreType.DMA((PIX // LANES,)),
        ],
        compiler_params=pltpu.CompilerParams(vmem_limit_bytes=56 * 2**20),
        name="pack_pool",
    )(image_pool, ridge_coef)
    rows = lax.all_to_all(packed, "xy", 0, 0, tiled=True)
    pick = call(
        pick_body,
        jax.ShapeDtypeStruct((target_index.shape[0], n_flat * pool_rows), BF16),
        2,
        smem=(0,),
        flops=10**8,
        name="pick_rows",
    )(at, index_col)
    keep, send = call(
        select_body,
        [
            jax.ShapeDtypeStruct((n_chip, n_half, n_half, n_tgt, LANES), BF16),
            jax.ShapeDtypeStruct((n_chip, n_half, n_tgt, LANES), BF16),
        ],
        3,
        smem=(0,),
        name="select_targets",
    )(at, pick, rows)
    swap = [(k, (k + 1) % n_core) for k in range(n_core)]
    other = lax.ppermute(send, "core", swap)
    chosen = call(
        add_body,
        jax.ShapeDtypeStruct((n_chip * n_half, n_half, n_tgt, LANES), BF16),
        2,
        name="add_core_targets",
    )(keep, other)
    got = lax.all_to_all(chosen, ("chip", "zh"), 0, 0, tiled=True)
    by_channel = jnp.swapaxes(support, 0, 1)
    n_maps = CHAN + 2 * LAYERS - 1
    s_maps, mine, gram, picked = call(
        side_body,
        [
            jax.ShapeDtypeStruct((PIX, LANES), BF16),
            jax.ShapeDtypeStruct((n_sup * n_sup_dev, LANES), F32),
            jax.ShapeDtypeStruct((n_sup * n_sup_dev, n_sup * n_sup_dev), F32),
            jax.ShapeDtypeStruct((SUB, LANES), F32),
        ],
        4,
        scratch=[pltpu.VMEM((LANES, PIX), F32)],
        flops=10**8,
        name="support_maps",
    )(by_channel, ridge_coef, label_col, got)
    merged = call(
        merge_body, jax.ShapeDtypeStruct((n_flat, n_half, SIDE, LANES), BF16), 1, name="merge_targets"
    )(got)
    pixels = lax.all_to_all(merged, "xy", 0, 0, tiled=True).reshape(SIDE, SIDE, LANES)
    sent = call(
        functools.partial(forward_body, n_sup),
        jax.ShapeDtypeStruct((n_sup_dev, SUB, LANES), F32),
        3,
        scratch=[*map_scratch(CHAN + LAYERS), pltpu.VMEM((SUB, LANES), F32)],
        flops=10**8,
        name="forward_maps",
        vmem=12,
    )(pixels, s_maps, gram)
    arrived = lax.all_to_all(sent, ("zh", "xy"), 0, 0, tiled=True)
    layer_maps = pltpu.VMEM((LAYERS - 1, SIDE, TILES, SUB, LANES), F32)
    flat = (CHAN + 1) * PIX
    high, low = call(
        functools.partial(backward_body, n_sup),
        [jax.ShapeDtypeStruct((flat, LANES), BF16)] * 2,
        2,
        scratch=[*map_scratch(n_maps), maps(SIDE + 2), maps(SIDE + 2), layer_maps, layer_maps],
        flops=10**10,
        name="backward_maps",
        vmem=20,
    )(pixels, s_maps)
    loss_scale = float(PIX) / n_tgt
    wide = n_sup * CHAN * PIX // LANES
    grad = call(
        functools.partial(weigh_body, loss_scale, n_tgt),
        jax.ShapeDtypeStruct((wide, LANES), F32),
        5,
        name="weigh_gradient",
        vmem=8,
    )(arrived, high, low, picked, by_channel)
    other = lax.ppermute(grad, "core", swap)
    summed = call(pair_sum_body, jax.ShapeDtypeStruct((n_chip, wide, LANES), F32), 2, name="sum_cores")(grad, other)
    shares = lax.all_to_all(summed, "chip", 0, 0, tiled=True)
    residual = call(
        functools.partial(residual_body, n_sup),
        jax.ShapeDtypeStruct((n_tgt, classes), F32),
        4,
        smem=(0,),
        flops=10**7,
        name="residual",
    )(start, arrived, mine, label_col)
    total = call(last_sum_body, jax.ShapeDtypeStruct(by_channel.shape, F32), 1, name="sum_chips")(shares)
    return (residual, jnp.swapaxes(total, 0, 1))


def solution(mesh):
    n_tgt, n_sup = mesh.devices.shape
    parts = Mesh(mesh.devices.reshape(n_tgt // 2, 2, 2, n_sup // 2), ("chip", "core", "zh", "xy"))
    tgt, sup = ("chip", "core"), ("zh", "xy")
    in_specs = (P((*tgt, *sup), None), P(), P(tgt), P(sup, None, None), P(sup, None))
    out_specs = (P(tgt, sup), P(sup, None, None))
    return jax.shard_map(local, mesh=parts, in_specs=in_specs, out_specs=out_specs, check_vma=False)
```

```python
import functools
import math

import jax
import jax.numpy as jnp
from jax import lax
from jax.experimental import pallas as pl
from jax.experimental.pallas import tpu as pltpu
from jax.sharding import Mesh, PartitionSpec as P

SIDE = 32
CHAN = 3
LAYERS = 4
PIX = SIDE * SIDE
SUB = 8
LANES = 128
TILES = SIDE // SUB
STEP_ROWS = 8
STEP_PIX = STEP_ROWS * SIDE
PARTS = 3
PACK_CUTS = 1

WEIGHT_VAR = 2.0
BIAS_VAR = 0.1
BOX_SCALE = WEIGHT_VAR / 9.0

F32 = jnp.float32
BF16 = jnp.bfloat16
VMEM = pl.BlockSpec(memory_space=pltpu.VMEM)
SMEM = pl.BlockSpec(memory_space=pltpu.SMEM)

ASIN_Q = (
    0.9999999439523269,
    -0.13661292782489154,
    0.05655466043182583,
    -0.03131997834776645,
    0.01767426424200143,
    -0.007641460751180656,
    0.0016626264836763138,
)


def call(body, outs, n_in, scratch=(), smem=(), flops=0, name=None, vmem=4):
    specs = [SMEM if k in smem else VMEM for k in range(n_in)]
    many = isinstance(outs, (list, tuple))
    return pl.pallas_call(
        body,
        out_shape=outs,
        in_specs=specs,
        out_specs=[VMEM] * len(outs) if many else VMEM,
        scratch_shapes=list(scratch),
        compiler_params=pltpu.CompilerParams(vmem_limit_bytes=vmem * 2**20),
        cost_estimate=pl.CostEstimate(flops=flops, bytes_accessed=1 << 20, transcendentals=0),
        name=name,
    )


def three_parts(x):
    high = x.astype(BF16)
    rest = x - high.astype(F32)
    mid = rest.astype(BF16)
    low = (rest - mid.astype(F32)).astype(BF16)
    return high, mid, low


def dot_f32(a, b, dims):
    return lax.dot_general(a, b, (dims, ((), ())), preferred_element_type=F32, precision=lax.Precision.HIGHEST)


def dot_bf16(a, b, dims):
    return lax.dot_general(a, b, (dims, ((), ())), preferred_element_type=F32)


def pack_body(pool_ref, ridge_ref, out_ref, pool_here, ridge_here, parts_ref, out_here, pool_sems, ridge_sem, out_sems):
    n_sup = ridge_ref.shape[0]
    halves = out_ref.shape[1]
    width = PIX // PACK_CUTS
    copies = [
        [
            pltpu.make_async_copy(
                pool_ref.at[:, pl.ds(c * PIX + k * width, width)],
                pool_here.at[:, pl.ds(c * PIX + k * width, width)],
                pool_sems.at[k, c],
            )
            for c in range(CHAN)
        ]
        for k in range(PACK_CUTS)
    ]
    ridge_copy = pltpu.make_async_copy(ridge_ref, ridge_here, ridge_sem)
    ridge_copy.start()
    for group in copies:
        for copy in group:
            copy.start()
    parts_ref[...] = jnp.zeros_like(parts_ref)
    ridge_copy.wait()
    for k, part in enumerate(three_parts(ridge_here[...])):
        parts_ref[k * n_sup : (k + 1) * n_sup, :] = part.astype(F32)
    writes = []
    for tile in range(PIX // LANES):
        at = tile * LANES
        if at % width == 0:
            for copy in copies[at // width]:
                copy.wait()
        pieces = [pool_here[:, c * PIX + at : c * PIX + at + LANES] for c in range(CHAN)]
        for r in range(LANES // SIDE):
            cut = [p[:, r * SIDE : (r + 1) * SIDE] for p in pieces]
            image_row = tile * (LANES // SIDE) + r
            owner, half = image_row // halves, image_row % halves
            first = (half * (SIDE // halves) + owner) * SIDE
            cut.append(parts_ref[:, first : first + SIDE].astype(BF16))
            out_here[owner, half] = jnp.concatenate(cut, axis=1)
        owners = LANES // SIDE // halves
        done = pl.ds(tile * owners, owners)
        writes.append(pltpu.make_async_copy(out_here.at[done], out_ref.at[done], out_sems.at[tile]))
        writes[-1].start()
    for write in writes:
        write.wait()


def pick_body(at_ref, index_ref, out_ref):
    wanted = index_ref[...] - at_ref[0]
    ids = lax.broadcasted_iota(jnp.int32, out_ref.shape, 1)
    out_ref[...] = jnp.where(ids == wanted, 1.0, 0.0).astype(BF16)


def select_body(at_ref, pick_ref, rows_ref, keep_ref, send_ref):
    n_src, halves, rows, _ = rows_ref.shape
    n_chip, _, _, n_tgt, _ = keep_ref.shape
    total = n_src * rows
    pick = pick_ref[...]
    lane = lax.broadcasted_iota(jnp.int32, (n_tgt, LANES), 1)
    pixel = lane < CHAN * SIDE
    low_core = at_ref[2] == 0
    share = n_src // n_chip // halves
    ridge = [[None] * halves for _ in range(halves)]
    for half in range(halves):
        for part in range(halves):
            first = (at_ref[1] * halves + part) * share
            block = rows_ref[pl.ds(first, share), half, 0 : n_tgt // share]
            ridge[half][part] = block.reshape(n_tgt, LANES).astype(F32)
    both = jnp.concatenate([rows_ref[:, part].reshape(total, LANES) for part in range(halves)], axis=1)
    both = dot_bf16(pick, both, ((1,), (0,)))
    for part in range(halves):
        got = both[:, part * LANES : (part + 1) * LANES]
        for chip in range(n_chip):
            low = got[2 * chip * n_tgt : (2 * chip + 1) * n_tgt]
            high = got[(2 * chip + 1) * n_tgt : (2 * chip + 2) * n_tgt]
            mine = jnp.where(low_core, low, high)
            send_ref[chip, part] = jnp.where(pixel, jnp.where(low_core, high, low), 0.0).astype(BF16)
            for half in range(halves):
                keep_ref[chip, half, part] = jnp.where(pixel, mine, ridge[half][part]).astype(BF16)


def add_body(keep_ref, other_ref, out_ref):
    n_chip, halves = keep_ref.shape[:2]
    for chip in range(n_chip):
        other = other_ref[chip].astype(F32)
        for half in range(halves):
            out_ref[chip * halves + half] = (keep_ref[chip, half].astype(F32) + other).astype(BF16)


def merge_body(parts_ref, out_ref):
    n_dst, halves, _, _ = out_ref.shape
    for half in range(halves):
        total = parts_ref[0, half].astype(F32)
        for k in range(1, parts_ref.shape[0]):
            total = total + parts_ref[k, half].astype(F32)
        turned = total.T
        n_tgt = turned.shape[1]
        cut = [turned[c * SIDE : (c + 1) * SIDE, :] for c in range(CHAN)]
        cut.append(jnp.zeros((SIDE, LANES - CHAN * n_tgt), F32))
        message = jnp.concatenate(cut, axis=1).astype(BF16)
        for k in range(n_dst):
            out_ref[k, half] = message


def steps(fn):
    for b in range(SIDE // STEP_ROWS):
        fn(b)


def rows_of(b):
    return pl.ds(b * STEP_ROWS, STEP_ROWS)


def pixels_of(b):
    return pl.ds(b * STEP_PIX, STEP_PIX)


def as_map(x):
    return x.reshape(x.shape[0] // SIDE, TILES, SUB, LANES)


def box(ref, row, n):
    x = ref[pl.ds(row, n + 2)]
    x = x[0:n] + x[1 : n + 1] + x[2 : n + 2]
    sub = lax.broadcasted_iota(jnp.int32, x.shape, 2)
    zero = jnp.zeros_like(x[:, 0:1])
    left = pltpu.roll(x, 1, 2)
    right = pltpu.roll(x, SUB - 1, 2)
    left = jnp.where(sub == 0, jnp.concatenate([zero, left[:, : TILES - 1]], axis=1), left)
    right = jnp.where(sub == SUB - 1, jnp.concatenate([right[:, 1:], zero], axis=1), right)
    return x + left + right


def step_box(ref, b):
    return box(ref, b * STEP_ROWS, STEP_ROWS)


def put(ref, b, x):
    ref[pl.ds(b * STEP_ROWS + 1, STEP_ROWS)] = x


def clear_halo(*refs):
    for ref in refs:
        for row in (0, SIDE + 1):
            ref[row] = jnp.zeros((TILES, SUB, LANES), F32)


def q_poly(a, scale=1.0):
    acc = (scale * ASIN_Q[-1]) * a + scale * ASIN_Q[-2]
    for c in ASIN_Q[-3::-1]:
        acc = acc * a + scale * c
    return acc


def act_of(x, scale):
    a = jnp.abs(x)
    left = 1.0 - a
    inv = lax.rsqrt(left)
    value = scale - left * inv * q_poly(a, scale)
    return jnp.where(x < 0.0, -value, value), a, inv


def self_act(var, inv, scale=1.0):
    x = 2.0 * var * inv * inv
    left = 1.0 - x
    return scale - left * lax.rsqrt(left) * q_poly(x, scale)


def flat_box(x):
    at = lax.broadcasted_iota(jnp.int32, x.shape, 1)
    col = at % SIDE
    left = jnp.where(col > 0, pltpu.roll(x, 1, 1), 0.0)
    right = jnp.where(col < SIDE - 1, pltpu.roll(x, PIX - 1, 1), 0.0)
    x = x + left + right
    above = jnp.where(at >= SIDE, pltpu.roll(x, SIDE, 1), 0.0)
    below = jnp.where(at < PIX - SIDE, pltpu.roll(x, PIX - SIDE, 1), 0.0)
    return x + above + below


def side_body(sup_ref, ridge_ref, labels_ref, got_ref, maps_ref, mine_ref, gram_ref, picked_ref, tgt_ref, spread_ref, parts_ref):
    n_sup = sup_ref.shape[1]
    n_tgt = labels_ref.shape[0]
    n_parts, halves, n_rows, _ = got_ref.shape
    n_src = mine_ref.shape[0] // n_sup
    share = n_src // n_parts // halves
    for k in range(n_parts):
        for part in range(halves):
            got = got_ref[k, part].astype(F32)
            for i in range(share):
                at = i * (n_rows // share)
                total = got[at : at + n_sup]
                for p in range(1, PARTS):
                    total = total + got[at + p * n_sup : at + (p + 1) * n_sup]
                source = (k % halves) * (n_src // halves) + ((k // halves) * halves + part) * share + i
                mine_ref[pl.ds(source, n_sup, stride=n_src), :] = total
    lane = lax.broadcasted_iota(jnp.int32, mine_ref.shape, 1)
    mine = jnp.where(lane >= CHAN * SIDE, mine_ref[...], 0.0)
    mine_ref[...] = mine
    gram_ref[...] = dot_f32(mine, mine, ((1,), (1,)))
    hot = labels_ref[...] == lax.broadcasted_iota(jnp.int32, (n_tgt, ridge_ref.shape[1]), 1)
    hot = jnp.where(hot, 1.0, 0.0)
    hot = jnp.concatenate([hot] * n_sup, axis=0)
    picked_ref[...] = jnp.zeros_like(picked_ref)
    picked_ref[0:n_sup, :] = dot_f32(ridge_ref[...], hot, ((1,), (1,)))
    parts_ref[...] = jnp.zeros_like(parts_ref)

    def keep(k, x):
        for i, part in enumerate(three_parts(x)):
            at = (k * PARTS + i) * n_sup
            parts_ref[at : at + n_sup, :] = part.astype(F32)

    current = 0.0
    for c in range(CHAN):
        s = sup_ref[c]
        keep(c, s)
        current = current + s * s
    current = current * (1.0 / CHAN)
    for depth in range(LAYERS):
        var = BOX_SCALE * flat_box(current) + BIAS_VAR
        inv = lax.rsqrt(1.0 + 2.0 * var)
        keep(CHAN + depth, inv)
        if depth < LAYERS - 1:
            keep(CHAN + LAYERS + depth, (4.0 / math.pi) * inv * inv * lax.rsqrt(1.0 + 4.0 * var))
            current = self_act(var, inv)
    row = lax.broadcasted_iota(jnp.int32, (LANES, LANES), 0)
    lane = lax.broadcasted_iota(jnp.int32, (LANES, LANES), 1)
    same = jnp.where(row == lane, 1.0, 0.0).astype(BF16)
    maps_ref[...] = dot_bf16(parts_ref[...].astype(BF16), same, ((0,), (0,))).astype(BF16)
    fill_spreads(n_sup, n_tgt, tgt_ref, spread_ref)


def fill_spreads(n_sup, n_tgt, tgt_ref, sup_ref):
    row = lax.broadcasted_iota(jnp.int32, (LANES, LANES), 0)
    lane = lax.broadcasted_iota(jnp.int32, (LANES, LANES), 1)
    own = row % n_tgt == lane % n_tgt
    for c in range(CHAN):
        tgt_ref[c] = jnp.where((row // n_tgt == c) & own, 1.0, 0.0).astype(BF16)
    own = row % n_sup == lane // n_tgt
    for k in range(sup_ref.shape[0]):
        sup_ref[k] = jnp.where((row // (PARTS * n_sup) == k) & own, 1.0, 0.0).astype(BF16)


def target_map(pix_ref, tgt_ref, c, b):
    pix = pix_ref[rows_of(b)].reshape(STEP_PIX, LANES)
    return as_map(dot_bf16(pix, tgt_ref[c], ((1,), (0,))))


def support_map(maps_ref, sup_ref, k, b):
    return as_map(dot_bf16(maps_ref[pixels_of(b), :], sup_ref[k], ((1,), (0,))))


QUARTERS = 4
QUARTER_ROWS = SIDE // QUARTERS
PER_QUARTER = QUARTER_ROWS // STEP_ROWS


def lane_block(shape):
    return lax.broadcasted_iota(jnp.int32, shape, len(shape) - 1) // (LANES // QUARTERS)


def put_edges(ref, first, final):
    width = LANES // QUARTERS
    block = lane_block(first.shape)
    ref[0] = jnp.where(block > 0, pltpu.roll(final, width, 2), 0.0)
    ref[QUARTER_ROWS + 1] = jnp.where(block < QUARTERS - 1, pltpu.roll(first, LANES - width, 2), 0.0)


def first_maps(pix_ref, maps_ref, tgt_ref, sup_ref, self_a, self_b, inv_ref, pair_ref):
    def one(b):
        own = pair = 0.0
        pix = pix_ref[rows_of(b)].reshape(STEP_PIX, LANES)
        spread_t = jnp.concatenate([tgt_ref[c] for c in range(CHAN)], axis=1)
        spread_s = jnp.concatenate([sup_ref[c] for c in range(CHAN)], axis=1)
        all_t = dot_bf16(pix, spread_t, ((1,), (0,)))
        all_s = dot_bf16(maps_ref[pixels_of(b), :], spread_s, ((1,), (0,)))
        for c in range(CHAN):
            t = as_map(all_t[:, c * LANES : (c + 1) * LANES])
            own = own + t * t
            pair = pair + t * as_map(all_s[:, c * LANES : (c + 1) * LANES])
        put(pair_ref, b, pair * (2.0 * BOX_SCALE / CHAN))
        at = pl.ds((b % PER_QUARTER) * STEP_ROWS + 1, STEP_ROWS)
        self_a[at] = jnp.where(lane_block(own.shape) == b // PER_QUARTER, own * (BOX_SCALE / CHAN), self_a[at])

    steps(one)
    put_edges(self_a, self_a[1], self_a[QUARTER_ROWS])
    for depth in range(LAYERS):
        now, later = (self_a, self_b) if depth % 2 == 0 else (self_b, self_a)
        for part in range(PER_QUARTER):
            var = box(now, part * STEP_ROWS, STEP_ROWS) + BIAS_VAR
            inv = lax.rsqrt(1.0 + 2.0 * var)
            inv_ref[depth, part] = inv
            if depth < LAYERS - 1:
                value = self_act(var, inv, BOX_SCALE)
                later[part * STEP_ROWS + 1 : (part + 1) * STEP_ROWS + 1] = value
        if depth < LAYERS - 1:
            put_edges(later, later[1], later[QUARTER_ROWS])


def target_inv(inv_ref, depth, b):
    x = inv_ref[depth, b % PER_QUARTER]
    x = jnp.where(lane_block(x.shape) == b // PER_QUARTER, x, 0.0)
    x = x + pltpu.roll(x, LANES // 2, 3)
    return x + pltpu.roll(x, LANES // 4, 3)


def forward_body(
    n_sup, pix_ref, maps_ref, tgt_ref, sup_ref, gram_ref, out_ref, self_a, self_b, inv_ref, pair_a, pair_b, acc_ref
):
    clear_halo(pair_a, pair_b)
    first_maps(pix_ref, maps_ref, tgt_ref, sup_ref, self_a, self_b, inv_ref, pair_a)
    acc_ref[...] = jnp.zeros_like(acc_ref)
    for depth in range(LAYERS):
        now, later = (pair_a, pair_b) if depth % 2 == 0 else (pair_b, pair_a)

        def one(b, depth=depth, now=now, later=later):
            twice = step_box(now, b) + 2.0 * BIAS_VAR
            both = target_inv(inv_ref, depth, b) * support_map(maps_ref, sup_ref, CHAN + depth, b)
            value = act_of(twice * both, 2.0 * BOX_SCALE if depth < LAYERS - 1 else 1.0)[0]
            if depth < LAYERS - 1:
                put(later, b, value)
            else:
                acc_ref[...] += jnp.sum(value, axis=(0, 1))

        steps(one)
    value = jnp.sum(acc_ref[...], axis=0, keepdims=True) * (1.0 / PIX)
    n_dst = out_ref.shape[0]
    for j in range(n_sup):
        out_ref[:, j, :] = gram_ref[j * n_dst : (j + 1) * n_dst, :]
    for k in range(n_sup, out_ref.shape[1]):
        out_ref[:, k, :] = jnp.broadcast_to(value, (n_dst, LANES))


def backward_body(
    pix_ref,
    maps_ref,
    tgt_ref,
    sup_ref,
    high_ref,
    low_ref,
    self_a,
    self_b,
    inv_ref,
    pair_a,
    pair_b,
    grad_a,
    grad_b,
    dcov_ref,
    dvar_ref,
):
    clear_halo(pair_a, pair_b, grad_a, grad_b)
    first_maps(pix_ref, maps_ref, tgt_ref, sup_ref, self_a, self_b, inv_ref, pair_a)
    last = LAYERS - 1
    for depth in range(LAYERS):
        now, later = (pair_a, pair_b) if depth % 2 == 0 else (pair_b, pair_a)

        def one(b, depth=depth, now=now, later=later):
            twice = step_box(now, b) + 2.0 * BIAS_VAR
            s_inv = support_map(maps_ref, sup_ref, CHAN + depth, b)
            both = target_inv(inv_ref, depth, b) * s_inv
            x = twice * both
            if depth < last:
                value, a, left = act_of(x, 2.0 * BOX_SCALE)
                put(later, b, value)
            else:
                a = jnp.abs(x)
                left = lax.rsqrt(1.0 - a)
            slope = (2.0 / math.pi) * left * lax.rsqrt(1.0 + a)
            d_cov = 2.0 * both * slope
            d_var = -(slope * x) * (s_inv * s_inv)
            if depth < last:
                dcov_ref[depth, rows_of(b)] = d_cov
                dvar_ref[depth, rows_of(b)] = d_var
            else:
                put(later, b, d_cov * (1.0 / PIX))
                put(grad_a, b, d_var * (1.0 / PIX))

        steps(one)
    for depth in range(last - 1, -1, -1):
        now, later = (pair_a, pair_b) if depth % 2 == 0 else (pair_b, pair_a)
        own_now, own_later = (grad_a, grad_b) if depth % 2 == 0 else (grad_b, grad_a)

        def one(b, depth=depth, now=now, later=later, own_now=own_now, own_later=own_later):
            g_pair = BOX_SCALE * step_box(now, b)
            g_self = BOX_SCALE * step_box(own_now, b)
            slope = support_map(maps_ref, sup_ref, CHAN + LAYERS + depth, b)
            put(later, b, g_pair * dcov_ref[depth, rows_of(b)])
            put(own_later, b, g_self * slope + g_pair * dvar_ref[depth, rows_of(b)])

        steps(one)

    def finish(b):
        g_pair = (BOX_SCALE / CHAN) * step_box(pair_b, b)
        for c in range(CHAN + 1):
            g = g_pair * target_map(pix_ref, tgt_ref, c, b) if c < CHAN else BOX_SCALE * step_box(grad_b, b)
            g = g.reshape(STEP_PIX, LANES)
            high = g.astype(BF16)
            at = pl.ds(c * PIX + b * STEP_PIX, STEP_PIX)
            high_ref[at, :] = high
            low_ref[at, :] = (g - high.astype(F32)).astype(BF16)

    steps(finish)


def weigh_body(scale, n_tgt, got_ref, high_ref, low_ref, picked_ref, sup_ref, out_ref):
    n_src = got_ref.shape[0]
    n_sup = sup_ref.shape[1]
    rows = got_ref.shape[1]
    gram = jnp.sum(got_ref[...], axis=0)
    values = got_ref[:, n_sup, :]
    lane = lax.broadcasted_iota(jnp.int32, (n_src, LANES), 1)
    big = jnp.concatenate([jnp.where(lane // n_tgt == j, values, 0.0) for j in range(n_sup)], axis=0)
    part = dot_f32(gram, big, ((1,), (0,)))
    part = part + pltpu.roll(part, 64, 1)
    part = part + pltpu.roll(part, 32, 1)
    row = lax.broadcasted_iota(jnp.int32, (rows, LANES), 0)
    lane = lax.broadcasted_iota(jnp.int32, (rows, LANES), 1)
    weight = jnp.where(lane // n_tgt == row, scale * (part - picked_ref[...]), 0.0)
    w_high = weight.astype(BF16)
    w_low = (weight - w_high.astype(F32)).astype(BF16)
    zero = jnp.zeros_like(w_high)
    first = jnp.concatenate([w_high, w_low], axis=0)
    second = jnp.concatenate([w_high, zero], axis=0)
    sums = []
    for c in range(CHAN + 1):
        at = slice(c * PIX, (c + 1) * PIX)
        one = dot_bf16(first, high_ref[at, :], ((1,), (1,)))
        two = dot_bf16(second, low_ref[at, :], ((1,), (1,)))
        sums.append((one[:rows] + one[rows:] + two[:rows])[:n_sup])
    per = PIX // LANES
    for c in range(CHAN):
        grad = sums[c] + (2.0 / CHAN) * sup_ref[c] * sums[CHAN]
        for k in range(per):
            out_ref[pl.ds(c * per + k, n_sup, stride=CHAN * per), :] = grad[:, k * LANES : (k + 1) * LANES]


def residual_body(n_sup, start_ref, got_ref, mine_ref, labels_ref, out_ref):
    n_src = got_ref.shape[0]
    n_tgt, classes = out_ref.shape
    values = got_ref[:, n_sup, :]
    total = jnp.zeros((n_tgt, LANES), F32)
    for j in range(n_sup):
        one = dot_f32(values, mine_ref[j * n_src : (j + 1) * n_src, :], ((0,), (0,)))
        total = total + one[j * n_tgt : (j + 1) * n_tgt, :]
    predicted = total[:, CHAN * SIDE :]
    ids = start_ref[0] + lax.broadcasted_iota(jnp.int32, (n_tgt, classes), 1)
    out_ref[...] = predicted - jnp.where(labels_ref[...] == ids, 1.0, 0.0)


def pair_sum_body(a_ref, b_ref, out_ref):
    total = a_ref[...] + b_ref[...]
    for k in range(out_ref.shape[0]):
        out_ref[k] = total


def last_sum_body(parts_ref, out_ref):
    total = parts_ref[0]
    for k in range(1, parts_ref.shape[0]):
        total = total + parts_ref[k]
    n_sup = out_ref.shape[1]
    per = PIX // LANES
    for j in range(n_sup):
        for c in range(CHAN):
            for k in range(per):
                row = (j * CHAN + c) * per + k
                out_ref[c, j : j + 1, k * LANES : (k + 1) * LANES] = total[row : row + 1, :]


def maps(rows):
    return pltpu.VMEM((rows, TILES, SUB, LANES), F32)


def map_scratch():
    return [
        maps(QUARTER_ROWS + 2),
        maps(QUARTER_ROWS + 2),
        pltpu.VMEM((LAYERS, PER_QUARTER, STEP_ROWS, TILES, SUB, LANES), F32),
        maps(SIDE + 2),
        maps(SIDE + 2),
    ]


def local(image_pool, target_index, labels, support, ridge_coef):
    n_chip, n_core, n_half, n_flat = (lax.axis_size(k) for k in ("chip", "core", "zh", "xy"))
    n_sup_dev = n_half * n_flat
    pool_rows = image_pool.shape[0]
    n_sup = support.shape[0]
    n_tgt = labels.shape[0]
    classes = ridge_coef.shape[1] // n_sup_dev
    chip, core, half = (lax.axis_index(k) for k in ("chip", "core", "zh"))
    first_row = ((chip * n_core + core) * n_half + half) * (n_flat * pool_rows)
    at = jnp.stack([first_row, chip, core]).astype(jnp.int32)
    start = ((half * n_flat + lax.axis_index("xy")) * classes)[None].astype(jnp.int32)
    label_col = labels[:, None]
    index_col = target_index[:, None]

    hbm = pl.BlockSpec(memory_space=pltpu.HBM)
    packed = pl.pallas_call(
        pack_body,
        out_shape=jax.ShapeDtypeStruct((n_flat, n_half, pool_rows, LANES), BF16),
        in_specs=[hbm, hbm],
        out_specs=hbm,
        scratch_shapes=[
            pltpu.VMEM(image_pool.shape, BF16),
            pltpu.VMEM(ridge_coef.shape, F32),
            pltpu.VMEM((pool_rows, PIX), F32),
            pltpu.VMEM((n_flat, n_half, pool_rows, LANES), BF16),
            pltpu.SemaphoreType.DMA((PACK_CUTS, CHAN)),
            pltpu.SemaphoreType.DMA,
            pltpu.SemaphoreType.DMA((PIX // LANES,)),
        ],
        compiler_params=pltpu.CompilerParams(vmem_limit_bytes=56 * 2**20),
        name="pack_pool",
    )(image_pool, ridge_coef)
    rows = lax.all_to_all(packed, "xy", 0, 0, tiled=True)
    pick = call(
        pick_body,
        jax.ShapeDtypeStruct((target_index.shape[0], n_flat * pool_rows), BF16),
        2,
        smem=(0,),
        flops=10**8,
        name="pick_rows",
    )(at, index_col)
    keep, send = call(
        select_body,
        [
            jax.ShapeDtypeStruct((n_chip, n_half, n_half, n_tgt, LANES), BF16),
            jax.ShapeDtypeStruct((n_chip, n_half, n_tgt, LANES), BF16),
        ],
        3,
        smem=(0,),
        name="select_targets",
    )(at, pick, rows)
    swap = [(k, (k + 1) % n_core) for k in range(n_core)]
    other = lax.ppermute(send, "core", swap)
    chosen = call(
        add_body,
        jax.ShapeDtypeStruct((n_chip * n_half, n_half, n_tgt, LANES), BF16),
        2,
        name="add_core_targets",
    )(keep, other)
    got = lax.all_to_all(chosen, ("chip", "zh"), 0, 0, tiled=True)
    by_channel = jnp.swapaxes(support, 0, 1)
    n_maps = CHAN + 2 * LAYERS - 1
    s_maps, mine, gram, picked, spread_t, spread_s = call(
        side_body,
        [
            jax.ShapeDtypeStruct((PIX, LANES), BF16),
            jax.ShapeDtypeStruct((n_sup * n_sup_dev, LANES), F32),
            jax.ShapeDtypeStruct((n_sup * n_sup_dev, n_sup * n_sup_dev), F32),
            jax.ShapeDtypeStruct((SUB, LANES), F32),
            jax.ShapeDtypeStruct((CHAN, LANES, LANES), BF16),
            jax.ShapeDtypeStruct((n_maps, LANES, LANES), BF16),
        ],
        4,
        scratch=[pltpu.VMEM((LANES, PIX), F32)],
        flops=10**8,
        name="support_maps",
    )(by_channel, ridge_coef, label_col, got)
    merged = call(
        merge_body, jax.ShapeDtypeStruct((n_flat, n_half, SIDE, LANES), BF16), 1, name="merge_targets"
    )(got)
    pixels = lax.all_to_all(merged, "xy", 0, 0, tiled=True).reshape(SIDE, SIDE, LANES)
    sent = call(
        functools.partial(forward_body, n_sup),
        jax.ShapeDtypeStruct((n_sup_dev, SUB, LANES), F32),
        5,
        scratch=[*map_scratch(), pltpu.VMEM((SUB, LANES), F32)],
        flops=10**8,
        name="forward_maps",
        vmem=12,
    )(pixels, s_maps, spread_t, spread_s, gram)
    arrived = lax.all_to_all(sent, ("zh", "xy"), 0, 0, tiled=True)
    layer_maps = pltpu.VMEM((LAYERS - 1, SIDE, TILES, SUB, LANES), F32)
    flat = (CHAN + 1) * PIX
    high, low = call(
        backward_body,
        [jax.ShapeDtypeStruct((flat, LANES), BF16)] * 2,
        4,
        scratch=[*map_scratch(), maps(SIDE + 2), maps(SIDE + 2), layer_maps, layer_maps],
        flops=10**10,
        name="backward_maps",
        vmem=20,
    )(pixels, s_maps, spread_t, spread_s)
    loss_scale = float(PIX) / n_tgt
    wide = n_sup * CHAN * PIX // LANES
    grad = call(
        functools.partial(weigh_body, loss_scale, n_tgt),
        jax.ShapeDtypeStruct((wide, LANES), F32),
        5,
        name="weigh_gradient",
        vmem=8,
    )(arrived, high, low, picked, by_channel)
    other = lax.ppermute(grad, "core", swap)
    summed = call(pair_sum_body, jax.ShapeDtypeStruct((n_chip, wide, LANES), F32), 2, name="sum_cores")(grad, other)
    shares = lax.all_to_all(summed, "chip", 0, 0, tiled=True)
    residual = call(
        functools.partial(residual_body, n_sup),
        jax.ShapeDtypeStruct((n_tgt, classes), F32),
        4,
        smem=(0,),
        flops=10**7,
        name="residual",
    )(start, arrived, mine, label_col)
    total = call(last_sum_body, jax.ShapeDtypeStruct(by_channel.shape, F32), 1, name="sum_chips")(shares)
    return (residual, jnp.swapaxes(total, 0, 1))


def solution(mesh):
    n_tgt, n_sup = mesh.devices.shape
    parts = Mesh(mesh.devices.reshape(n_tgt // 2, 2, 2, n_sup // 2), ("chip", "core", "zh", "xy"))
    tgt, sup = ("chip", "core"), ("zh", "xy")
    in_specs = (P((*tgt, *sup), None), P(), P(tgt), P(sup, None, None), P(sup, None))
    out_specs = (P(tgt, sup), P(sup, None, None))
    return jax.shard_map(local, mesh=parts, in_specs=in_specs, out_specs=out_specs, check_vma=False)
```
